128 devices in a mesh: section: 2 (over y_lo), blk: 16 (over z, x), wshard: 4 (over y_hi, core).
Axes of the slice: x: 4, y: 4 (y_hi: 2, y_lo: 2; y = y_hi * 2 + y_lo), z: 4, core: 2. Of those that a mesh axis runs over, the one named last changes fastest.
Arguments:
- tokens: bfloat16 [2, 4, 2048, 960], P(None, 'wshard', 'blk'), may hold values from -6 to 6
- cotangent: bfloat16 [2, 4, 2048, 960], P(None, 'wshard', 'blk'), may hold values from -6 to 6
- span_order: int32 [16], replicated, may hold values from 0 to 15, each once
- norm_one: bfloat16 [2, 960], P('section', 'wshard'), may hold values from 0.5 to 1.5
- w_query: bfloat16 [2, 960, 960], P('section', 'wshard'), may hold values from -0.1875 to 0.1875
- w_key: bfloat16 [2, 960, 320], P('section', 'wshard'), may hold values from -0.1875 to 0.1875
- w_value: bfloat16 [2, 960, 320], P('section', 'wshard'), may hold values from -0.1875 to 0.1875
- w_out: bfloat16 [2, 960, 960], P('section', 'wshard'), may hold values from -1.5 to 1.5
- norm_two: bfloat16 [2, 960], P('section', 'wshard'), may hold values from 0.5 to 1.5
- w_gate: bfloat16 [2, 960, 2560], P('section', 'wshard'), may hold values from -0.1875 to 0.1875
- w_up: bfloat16 [2, 960, 2560], P('section', 'wshard'), may hold values from -0.1875 to 0.1875
- w_down: bfloat16 [2, 2560, 960], P('section', 'wshard'), may hold values from -0.125 to 0.125
Outputs:
- layer_outputs: bfloat16 [2, 2, 4, 2048, 960], P('section', None, 'wshard', 'blk')
- input_grads: float32 [2, 2, 4, 2048, 960], P('section', None, 'wshard', 'blk')
- grad_norm_one: float32 [2, 960], P('section', 'wshard')
- grad_query: float32 [2, 960, 960], P('section', 'wshard')
- grad_key: float32 [2, 960, 320], P('section', 'wshard')
- grad_value: float32 [2, 960, 320], P('section', 'wshard')
- grad_out: float32 [2, 960, 960], P('section', 'wshard')
- grad_norm_two: float32 [2, 960], P('section', 'wshard')
- grad_gate: float32 [2, 960, 2560], P('section', 'wshard')
- grad_up: float32 [2, 960, 2560], P('section', 'wshard')
- grad_down: float32 [2, 2560, 960], P('section', 'wshard')
The draws below stay inside these ranges and needn't reach their ends.
Inputs may be any that keep to these rules, and one draw needn't show every extreme that they name: `span_order`: a permutation: each index of blk holds a different position block.
All inputs are finite; a program needn't handle non-finite values.
Results may differ from the reference program's by a relative error of at most 0.03.
Values may be sent and summed in bfloat16 or wider, within the bound.
No kernel may reach another device: no remote copies, remote signals or barrier semaphores. Data moves between devices by JAX's collectives and lax.ppermute only.
A program may use at most 256 MiB of HBM per device.

```python
import jax
import jax.numpy as jnp
from jax import lax

D = 960
H = 15
KV = 5
HD = 64
FF = 2560
LEN = 2048
MB = 2
SEQS = 4
N_SECTION = 2
N_BLK = 16


def shard_levels(key, dims, split, least, top_value):
    factor_of, own = 1.0, jax.random.fold_in(key, 6)
    for position, parts in split:
        steps = jnp.exp(jax.random.uniform(jax.random.fold_in(own, position), (parts,), jnp.float32, least / len(split), top_value / len(split)))
        factor_of = factor_of * jnp.repeat(steps, dims[position] // parts).reshape([-1 if axis == position else 1 for axis in range(len(dims))])
    return factor_of


def gaussian(own_key, extent, width, reach, cuts=(), held_as=jnp.bfloat16):
    values = jax.random.normal(own_key, extent, jnp.float32) * width
    if len(cuts) > 0:
        values = shard_levels(own_key, extent, cuts, -0.22, 0.18) * values
    return jnp.clip(values, min=-reach, max=reach).astype(held_as)


def setup_inputs(seed: int = 0) -> dict:
    key_list = jax.random.split(jax.random.key(seed), 13)
    tokens = gaussian(key_list[0], (MB, SEQS, LEN, D), 1.0, 6.0, ((1, 4), (2, 16)))
    cotangent = gaussian(key_list[1], (MB, SEQS, LEN, D), 1.0, 6.0, ((1, 4), (2, 16)))
    span_order = jax.random.permutation(key_list[2], N_BLK).astype(jnp.int32)
    norm_one = jnp.clip(1.0 + 0.1 * jax.random.normal(key_list[3], (N_SECTION, D), jnp.float32), 0.5, 1.5).astype(jnp.bfloat16)
    w_query = gaussian(key_list[4], (N_SECTION, D, H * HD), D ** -0.5, 0.1875, ((0, 2), (1, 4)))
    w_key = gaussian(key_list[5], (N_SECTION, D, KV * HD), D ** -0.5, 0.1875, ((0, 2), (1, 4)))
    w_value = gaussian(key_list[6], (N_SECTION, D, KV * HD), D ** -0.5, 0.1875, ((0, 2), (1, 4)))
    w_out = gaussian(key_list[7], (N_SECTION, H * HD, D), (H * HD * 32 // LEN) ** -0.5, 1.5, ((0, 2), (1, 4)))
    norm_two = jnp.clip(1.0 + 0.1 * jax.random.normal(key_list[8], (N_SECTION, D), jnp.float32), 0.5, 1.5).astype(jnp.bfloat16)
    w_gate = gaussian(key_list[9], (N_SECTION, D, FF), D ** -0.5, 0.1875, ((0, 2), (1, 4)))
    w_up = gaussian(key_list[10], (N_SECTION, D, FF), D ** -0.5, 0.1875, ((0, 2), (1, 4)))
    w_down = gaussian(key_list[11], (N_SECTION, FF, D), FF ** -0.5, 0.125, ((0, 2), (1, 4)))
    return {"tokens": tokens, "cotangent": cotangent, "span_order": span_order, "norm_one": norm_one, "w_query": w_query, "w_key": w_key, "w_value": w_value, "w_out": w_out, "norm_two": norm_two, "w_gate": w_gate, "w_up": w_up, "w_down": w_down}


@jax.custom_vjp
def low(v):
    return lax.optimization_barrier(v.astype(jnp.bfloat16)).astype(jnp.float32)

@jax.custom_vjp
def low_back(v):
    return v

def low_keep(v):
    return (low(v), None)

def low_pass(kept, grad):
    return (grad,)

def back_keep(v):
    return (v, None)

def back_low(kept, grad):
    return (low(grad),)
low.defvjp(low_keep, low_pass)
low_back.defvjp(back_keep, back_low)
eps_norm = 1e-05
rope_base = 10000.0

def rms_scale(values, gain):
    return values * lax.rsqrt(lax.optimization_barrier(jnp.mean(values * values, axis=-1, keepdims=True)) + eps_norm) * gain

def rotate(values, cosine, sine):
    halfway = values.shape[-1] // 2
    turned = jnp.concatenate([-values[..., halfway:], values[..., :halfway]], axis=-1)
    return values * cosine + turned * sine

def rope_tables(positions, head_size):
    exponent = jnp.arange(head_size // 2, dtype=jnp.float32) * (2.0 / head_size)
    frequency = rope_base ** (-exponent)
    angles = positions.astype(jnp.float32)[:, None] * frequency[None, :]
    angles = jnp.concatenate([angles, angles], axis=-1)
    return (jnp.cos(angles), jnp.sin(angles))

def layer_apply(inputs, params, cosine, sine, allowed):
    gain_one, query_w, key_w, value_w, out_w, gain_two, gate_w, up_w, down_w = params
    highest = lax.Precision.HIGHEST
    length = inputs.shape[0]
    normed = low(rms_scale(inputs, gain_one))
    query_lin = low_back(jnp.dot(normed, query_w, precision=highest))
    key_lin = low_back(jnp.dot(normed, key_w, precision=highest))
    value_all = low(low_back(jnp.dot(normed, value_w, precision=highest))).reshape(length, KV, HD)
    queries = low(rotate(query_lin.reshape(length, H, HD), cosine[:, None, :], sine[:, None, :]))
    keys_rot = low(rotate(key_lin.reshape(length, KV, HD), cosine[:, None, :], sine[:, None, :]))
    grouped = queries.reshape(length, KV, H // KV, HD)
    raw_scores = jnp.einsum('qkgd,skd->kgqs', grouped, keys_rot, precision=highest)
    scores = low_back(raw_scores * HD ** (-0.5))
    scores = jnp.where(allowed[None, None], scores, -jnp.inf)
    attend = low(jax.nn.softmax(scores, axis=-1))
    mixed = jnp.einsum('kgqs,skd->qkgd', attend, value_all, precision=highest).reshape(length, H * HD)
    mixed = low(low_back(mixed))
    residual = inputs + low_back(jnp.dot(mixed, out_w, precision=highest))
    normed_two = low(rms_scale(residual, gain_two))
    gate_value = low_back(jnp.dot(normed_two, gate_w, precision=highest))
    up_value = low_back(jnp.dot(normed_two, up_w, precision=highest))
    hidden = low(jax.nn.silu(gate_value) * up_value)
    return residual + low_back(jnp.dot(hidden, down_w, precision=highest))

def reference(tokens, cotangent, span_order, norm_one, w_query, w_key, w_value, w_out, norm_two, w_gate, w_up, w_down):
    span_rows = LEN // N_BLK
    row_ids = jnp.arange(LEN, dtype=jnp.int32)
    positions = span_order[row_ids // span_rows].astype(jnp.int32) * span_rows + row_ids % span_rows
    cosine, sine = rope_tables(positions, HD)
    allowed = positions[None, :] <= positions[:, None]
    weights = tuple((item.astype(jnp.float32) for item in (norm_one, w_query, w_key, w_value, w_out, norm_two, w_gate, w_up, w_down)))
    inputs = tokens.astype(jnp.float32).reshape(MB * SEQS, LEN, D)
    extras = jnp.zeros_like(inputs)

    def whole_model(inputs, extras, weights):
        first_params = tuple((item[0] for item in weights))
        second_params = tuple((item[1] for item in weights))

        def per_sequence(pair):
            first_out = layer_apply(pair[0], first_params, cosine, sine, allowed)
            handed = low(low_back(first_out)) + pair[1]
            second_out = layer_apply(handed, second_params, cosine, sine, allowed)
            return (first_out, second_out)
        return lax.map(jax.checkpoint(per_sequence), (inputs, extras))
    (first_out, second_out), pullback = jax.vjp(whole_model, inputs, extras, weights)
    cot_rows = cotangent.astype(jnp.float32).reshape(MB * SEQS, LEN, D)
    input_grad, extra_grad, weight_grads = pullback((jnp.zeros_like(first_out), cot_rows))
    layer_outputs = jnp.stack([first_out, second_out]).astype(jnp.bfloat16).reshape(N_SECTION, MB, SEQS, LEN, D)
    input_grads = jnp.stack([input_grad, extra_grad]).reshape(N_SECTION, MB, SEQS, LEN, D)
    return (layer_outputs, input_grads, weight_grads[0], weight_grads[1], weight_grads[2], weight_grads[3], weight_grads[4], weight_grads[5], weight_grads[6], weight_grads[7], weight_grads[8])
```

```python
import functools

import jax
import jax.numpy as jnp
from jax import lax
from jax.experimental import pallas as pl
from jax.experimental.pallas import tpu as pltpu
from jax.sharding import PartitionSpec as P

D = 960
H = 15
KV = 5
HD = 64
FF = 2560
ROWS = 128
NB = 16
LEN = ROWS * NB
QKV = H * HD + 2 * KV * HD
UNITS = FF // 8
SHARE = D // 4
PIECE = 16
QKV_PART = QKV // 8
OUT_PART = D // 8
OUT_AT = 256
ATT_WIDTH = 384
DOWN_ROWS = 30
FF_ROWS = 96
TILE = 256

EIGHT = ("section", "wshard")
eps_norm = 1e-05
rope_base = 10000.0
BF = jnp.bfloat16
F32 = jnp.float32
VMEM_BYTES = 56 * 1024 * 1024


def place_of(y, core):
    return (y % 2) * 4 + (y // 2) * 2 + core


def ring_pairs(step, flip):
    return [
        (place_of(y, c), place_of((y + step) % 4, c ^ flip)) for y in range(4) for c in range(2)
    ]


def hop(array, step, flip=0):
    return lax.ppermute(array, EIGHT, ring_pairs(step, flip))


def swap_section(array):
    return lax.ppermute(array, "section", [(0, 1), (1, 0)])


def gather_eight(block):
    half = block.shape[0] // 2
    beside = hop(block, 0, 1)
    before = hop(block, 1)
    after = hop(block, -1)
    far = jnp.concatenate([hop(before[:half], 1), hop(after[half:], -1)], axis=0)
    return [
        [block, beside],
        [after, hop(after, 0, 1)],
        [far, hop(far, 0, 1)],
        [before, hop(before, 0, 1)],
    ]


def scatter_eight(parts):
    half = parts[0][0].shape[0] // 2
    total = [None] * 4
    for step in (2, 1, 3, 0):
        arrived = hop(parts[step][1].astype(BF), 0, 1)
        total[step] = parts[step][0].astype(F32) + arrived.astype(F32)
    far = total[2].astype(BF)
    low = hop(far[:half], 1).astype(F32)
    high = hop(far[half:], -1).astype(F32)
    forth = jnp.concatenate([total[1][:half] + low, total[1][half:]], axis=0).astype(BF)
    back = jnp.concatenate([total[3][:half], total[3][half:] + high], axis=0).astype(BF)
    return total[0] + hop(forth, 1).astype(F32) + hop(back, -1).astype(F32)


def norm_factor(values):
    return lax.rsqrt(jnp.mean(values * values, axis=-1, keepdims=True) + eps_norm)


def norm_backward(values, gain, grad):
    factor = norm_factor(values)
    scaled = grad * gain
    inner = jnp.mean(values * scaled, axis=-1, keepdims=True)
    grad_values = factor * scaled - values * (factor * factor * factor * inner)
    grad_gain = jnp.sum(grad * values * factor, axis=0, keepdims=True)
    return grad_values, grad_gain


def dot(left, right):
    return jnp.dot(left, right, preferred_element_type=F32)


def against(left, right):
    return lax.dot_general(left, right, (((1,), (1,)), ((), ())), preferred_element_type=F32)


def across(left, right):
    return lax.dot_general(left, right, (((0,), (0,)), ((), ())), preferred_element_type=F32)


def rotate(values, cosine, sine):
    half = HD // 2
    turned = jnp.concatenate([-values[:, half:], values[:, :half]], axis=1)
    return values * cosine + turned * sine


def rotate_back(grad, cosine, sine):
    half = HD // 2
    part = grad * sine
    return grad * cosine + jnp.concatenate([part[:, half:], -part[:, :half]], axis=1)


def fold(rows):
    half = rows.shape[0] // 2
    return jnp.concatenate([rows[:half], rows[half:]], axis=1)


def unfold(block):
    return jnp.concatenate([block[:, :HD], block[:, HD:]], axis=0)


def load_blocks(table_ref, layer, blocks, weight_ref, gain_ref, sems):
    def copies(number):
        place = table_ref[2 * number + 1]
        block = blocks[number]
        return (
            pltpu.make_async_copy(
                block.at[pl.ds(0, SHARE)],
                weight_ref.at[pl.ds(pl.multiple_of(place * SHARE, 16), SHARE)],
                sems.at[0, number],
            ),
            pltpu.make_async_copy(
                block.at[pl.ds(SHARE, 16), pl.ds(0, 256)], gain_ref.at[place], sems.at[1, number]
            ),
        )

    for number in range(8):

        @pl.when(table_ref[2 * number] == layer)
        def _():
            for copy in copies(number):
                copy.start()

    for number in range(8):

        @pl.when(table_ref[2 * number] == layer)
        def _():
            for copy in copies(number):
                copy.wait()

    return jnp.concatenate([gain_ref[w, 0:1, :SHARE] for w in range(4)], axis=1).astype(F32)


def project_kernel(layer, table_ref, x_ref, cos_ref, sin_ref, *refs):
    blocks, (h_ref, out_ref, w_ref, gain_ref, sems) = refs[:8], refs[8:]
    gain = load_blocks(table_ref, layer, blocks, w_ref, gain_ref, sems)
    x = x_ref[...]
    h = (x * norm_factor(x) * gain).astype(BF)
    h_ref[...] = h
    cosine, sine = cos_ref[...], sin_ref[...]
    lin = dot(h, w_ref[...])

    def head(at):
        return lin[:, at * HD : (at + 1) * HD]

    for group in range(KV):
        key = rotate(head(H + group), cosine, sine).astype(BF)
        pair = jnp.concatenate([key, head(H + KV + group).astype(BF)], axis=1)
        for member in range(H // KV):
            index = group * (H // KV) + member
            out_ref[index, 0:ROWS, :] = pair
            query = rotate(head(index), cosine, sine).astype(BF)
            out_ref[index, ROWS:, :] = fold(query)
    out_ref[NB - 1] = jnp.zeros((ROWS + ROWS // 2, 2 * HD), BF)


def diagonal_mask(size, keys_first):
    rows = lax.broadcasted_iota(jnp.int32, (size, size), 0)
    columns = lax.broadcasted_iota(jnp.int32, (size, size), 1)
    return rows <= columns if keys_first else columns <= rows


def attend_kernel(place_ref, in_ref, out_ref, lse_ref, q_ref, k_ref, v_ref):
    for p in range(NB):
        block = in_ref[place_ref[p]]
        at = slice(p * ROWS, (p + 1) * ROWS)
        k_ref[at, :] = block[:ROWS, :HD]
        v_ref[at, :] = block[:ROWS, HD:]
        q_ref[at, :] = unfold(block[ROWS:])
    mask = diagonal_mask(TILE, False)
    for tile in range(LEN // TILE):
        at = slice(tile * TILE, (tile + 1) * TILE)
        seen = (tile + 1) * TILE
        scores = against(q_ref[at, :], k_ref[:seen, :]) * HD ** (-0.5)
        last = jnp.where(mask, scores[:, seen - TILE :], -jnp.inf)
        if tile:
            scores = jnp.concatenate([scores[:, : seen - TILE], last], axis=1)
        else:
            scores = last
        peak = jnp.max(scores, axis=-1, keepdims=True)
        terms = jnp.exp(scores - peak)
        total = jnp.sum(terms, axis=-1, keepdims=True)
        attend = (terms * (1.0 / total)).astype(BF)
        mixed = dot(attend, v_ref[:seen, :]).astype(BF)
        lse = peak + jnp.log(total)
        lse_ref[:, at] = jnp.transpose(jnp.broadcast_to(lse, (TILE, 128)))[:8, :]
        for part in range(TILE // ROWS):
            index = place_ref[tile * (TILE // ROWS) + part]
            out_ref[index] = fold(mixed[part * ROWS : (part + 1) * ROWS])


def attend_back_kernel(
    place_ref, in_ref, do_ref, lse_ref, out_ref, q_ref, k_ref, v_ref, g_ref, kt_ref, dq_ref, dk_ref, dv_ref
):
    for p in range(NB):
        block = in_ref[place_ref[p]]
        at = slice(p * ROWS, (p + 1) * ROWS)
        k_ref[at, :] = block[:ROWS, :HD]
        v_ref[at, :] = block[:ROWS, HD:]
        q_ref[at, :] = unfold(block[ROWS:])
        g_ref[at, :] = unfold(do_ref[place_ref[p]])
    kt_ref[...] = jnp.transpose(k_ref[...].astype(F32)).astype(BF)
    dk_ref[...] = jnp.zeros((LEN, HD), F32)
    dv_ref[...] = jnp.zeros((LEN, HD), F32)
    mask = diagonal_mask(TILE, True)
    for tile in range(LEN // TILE):
        at = slice(tile * TILE, (tile + 1) * TILE)
        seen = (tile + 1) * TILE
        query = q_ref[at, :]
        grad = g_ref[at, :]
        scores = against(k_ref[:seen, :], query) * HD ** (-0.5)
        last = jnp.where(mask, scores[seen - TILE :], -jnp.inf)
        if tile:
            scores = jnp.concatenate([scores[: seen - TILE], last], axis=0)
        else:
            scores = last
        full = jnp.exp(scores - lse_ref[0:1, at])
        attend_grad = against(v_ref[:seen, :], grad)
        inner = jnp.sum(full * attend_grad, axis=0, keepdims=True)
        score_grad = (full * (attend_grad - inner)).astype(BF)
        dv_ref[:seen, :] += dot(full.astype(BF), grad)
        dk_ref[:seen, :] += dot(score_grad, query)
        dq_ref[at, :] = jnp.transpose(dot(kt_ref[:, :seen], score_grad))
    for p in range(NB):
        index = place_ref[p]
        at = slice(p * ROWS, (p + 1) * ROWS)
        key_grad = (dk_ref[at, :] * HD ** (-0.5)).astype(BF)
        query_grad = (dq_ref[at, :] * HD ** (-0.5)).astype(BF)
        out_ref[index, 0:ROWS, :] = jnp.concatenate([key_grad, dv_ref[at, :].astype(BF)], axis=1)
        out_ref[index, ROWS:, :] = fold(query_grad)


def mix_kernel(layer, table_ref, in_ref, x_ref, *refs):
    blocks, (o_ref, x2_ref, h_ref, w_ref, gain_ref, sems) = refs[:8], refs[8:]
    gain = load_blocks(table_ref, layer, blocks, w_ref, gain_ref, sems)
    mixed = jnp.concatenate([unfold(in_ref[index]) for index in range(H)], axis=1)
    o_ref[...] = mixed
    x2 = x_ref[...] + dot(mixed, w_ref[...])
    x2_ref[...] = x2
    h_ref[...] = (x2 * norm_factor(x2) * gain).astype(BF)


def mix_back_kernel(layer, table_ref, dy_ref, dh_ref, x2_ref, *refs):
    blocks, (dx2_ref, out_ref, e_ref, gg_ref, w_ref, gain_ref, sems) = refs[:8], refs[8:]
    gain = load_blocks(table_ref, layer, blocks, w_ref, gain_ref, sems)
    part, grad_gain = norm_backward(x2_ref[...], gain, dh_ref[...])
    dx2 = dy_ref[...] + part
    dx2_ref[...] = dx2
    gg_ref[...] = grad_gain
    low = dx2.astype(BF)
    for index in range(8):
        e_ref[index, :, 0:OUT_PART] = low[:, index * OUT_PART : (index + 1) * OUT_PART]
        e_ref[index, :, OUT_PART:] = jnp.zeros((ROWS, 128 - OUT_PART), BF)
    mixed_grad = against(low, w_ref[...]).astype(BF)
    for index in range(H):
        out_ref[index] = fold(mixed_grad[:, index * HD : (index + 1) * HD])
    out_ref[NB - 1] = jnp.zeros((ROWS // 2, 2 * HD), BF)


def project_back_kernel(layer, table_ref, in_ref, dx2_ref, x_ref, cos_ref, sin_ref, gg_ref, *refs):
    blocks, (dx_ref, lin_ref, w_ref, gain_ref, sems) = refs[:8], refs[8:]
    gain = load_blocks(table_ref, layer, blocks, w_ref, gain_ref, sems)
    cosine, sine = cos_ref[...], sin_ref[...]
    queries, keys, values = [], [], []
    for group in range(KV):
        pair = None
        for member in range(H // KV):
            index = group * (H // KV) + member
            own = in_ref[index, 0:ROWS, :].astype(F32)
            pair = own if pair is None else pair + own
            query = unfold(in_ref[index, ROWS:, :].astype(F32))
            queries.append(rotate_back(query, cosine, sine).astype(BF))
        keys.append(rotate_back(pair[:, :HD], cosine, sine).astype(BF))
        values.append(pair[:, HD:].astype(BF))
    lin_grad = jnp.concatenate(queries + keys + values, axis=1)
    part, grad_gain = norm_backward(x_ref[...], gain, against(lin_grad, w_ref[...]))
    dx_ref[...] = dx2_ref[...] + part
    gains = jnp.concatenate([grad_gain, gg_ref[...], jnp.zeros((14, D), F32)], axis=0).astype(BF)
    for index in range(8):
        lin_ref[index, 0:ROWS, 0:QKV_PART] = lin_grad[:, index * QKV_PART : (index + 1) * QKV_PART]
        lin_ref[index, 0:ROWS, QKV_PART:] = jnp.zeros((ROWS, 256 - QKV_PART), BF)
        lin_ref[index, ROWS:, 0:OUT_PART] = gains[:, index * OUT_PART : (index + 1) * OUT_PART]
        lin_ref[index, ROWS:, OUT_PART:] = jnp.zeros((16, 256 - OUT_PART), BF)


def feed_kernel(count, *refs):
    normed = jnp.concatenate([ref[...] for ref in refs[:count]], axis=0)
    wgu_ref, wd_ref, lin_ref, hidden_ref = refs[count : count + 4]
    lin = dot(normed, wgu_ref[...])
    lin_ref[...] = lin
    gate, up = lin[:, :UNITS], lin[:, UNITS:]
    hidden = (gate * jax.nn.sigmoid(gate) * up).astype(BF)
    hidden_ref[...] = hidden
    part = dot(hidden, wd_ref[...]).astype(BF)
    for index, ref in enumerate(refs[count + 4 :]):
        ref[...] = part[index * ROWS : (index + 1) * ROWS]


def feed_back_kernel(count, *refs):
    branch = jnp.concatenate([ref[...] for ref in refs[:count]], axis=0)
    lin_ref, wgu_ref, wd_ref, grad_ref = refs[count : count + 4]
    hidden_grad = against(branch, wd_ref[...])
    gate, up = lin_ref[:, :UNITS], lin_ref[:, UNITS:]
    sig = jax.nn.sigmoid(gate)
    up_grad = hidden_grad * (gate * sig)
    gate_grad = hidden_grad * up * (sig + gate * sig * (1.0 - sig))
    lin_grad = jnp.concatenate([gate_grad, up_grad], axis=1).astype(BF)
    grad_ref[...] = lin_grad
    part = against(lin_grad, wgu_ref[...]).astype(BF)
    for index, ref in enumerate(refs[count + 4 :]):
        ref[...] = part[index * ROWS : (index + 1) * ROWS]


def feed_grads_kernel(*refs):
    normed = jnp.concatenate([ref[...] for ref in refs[:8]], axis=0)
    branch = jnp.concatenate([ref[...] for ref in refs[8:16]], axis=0)
    lin_grad = jnp.concatenate([ref[...] for ref in refs[16:19]], axis=0)
    hidden = jnp.concatenate([ref[...] for ref in refs[19:22]], axis=0)
    out_ref = refs[22]
    gate_up = across(normed, lin_grad).astype(BF)
    for piece in range(NB - 1):
        for w in range(4):
            at = w * SHARE + piece * PIECE
            out_ref[piece, w * PIECE : (w + 1) * PIECE, :] = gate_up[at : at + PIECE]
    out_ref[NB - 1, 0 : 4 * PIECE, :] = jnp.zeros((4 * PIECE, 2 * UNITS), BF)
    down = across(hidden, branch)
    each = UNITS // NB
    for piece in range(NB):
        rows = down[piece * each : (piece + 1) * each]
        tail = rows[:, 2 * UNITS :]
        tail = jnp.concatenate([tail[: each // 2], tail[each // 2 :]], axis=1)
        rest = jnp.zeros((FF_ROWS - 4 * PIECE - DOWN_ROWS, 2 * UNITS), F32)
        out_ref[piece, 4 * PIECE :, :] = jnp.concatenate(
            [rows[:, : 2 * UNITS], tail, rest], axis=0
        ).astype(BF)


def attend_grads_kernel(index_ref, rows_ref, lin_ref, e_ref, out_ref):
    normed = jnp.concatenate([rows_ref[t, 0:ROWS, :] for t in range(8)], axis=0)
    mixed = jnp.concatenate([rows_ref[t, ROWS:, :] for t in range(8)], axis=0)
    lin_grad = jnp.concatenate([lin_ref[t, 0:ROWS, :] for t in range(8)], axis=0)
    branch = jnp.concatenate([e_ref[t] for t in range(8)], axis=0)
    weight = across(normed, lin_grad).astype(BF)
    out_weight = across(mixed, branch).astype(BF)
    for piece in range(NB - 1):
        for w in range(4):
            at = w * SHARE + piece * PIECE
            to = slice(w * PIECE, (w + 1) * PIECE)
            out_ref[piece, to, 0:OUT_AT] = weight[at : at + PIECE]
            out_ref[piece, to, OUT_AT:] = out_weight[at : at + PIECE]
    gains = lin_ref[0, ROWS:, :].astype(F32)
    for t in range(1, 8):
        gains = gains + lin_ref[t, ROWS:, :].astype(F32)
    out_ref[NB - 1] = jnp.zeros((4 * PIECE, ATT_WIDTH), BF)
    at = pl.multiple_of(index_ref[0] * PIECE, PIECE)
    out_ref[NB - 1, pl.ds(at, PIECE), 0:OUT_AT] = gains.astype(BF)


def finish_feed_kernel(in_ref, gate_ref, up_ref, down_ref):
    for piece in range(NB - 1):
        at = slice(piece * PIECE, (piece + 1) * PIECE)
        parts = []
        for w in range(4):
            for s in range(2):
                source = 4 * s + w
                parts.append(in_ref[piece, source * PIECE : (source + 1) * PIECE, :].astype(F32))
        gate_ref[at, :] = jnp.concatenate([part[:, :UNITS] for part in parts], axis=1)
        up_ref[at, :] = jnp.concatenate([part[:, UNITS:] for part in parts], axis=1)
    each = UNITS // NB
    for piece in range(NB):
        for s in range(2):
            at = 8 * PIECE + s * (FF_ROWS - 4 * PIECE)
            rows = in_ref[piece, at : at + FF_ROWS - 4 * PIECE, :].astype(F32)
            tail = rows[each:DOWN_ROWS]
            tail = jnp.concatenate([tail[:, :UNITS], tail[:, UNITS:]], axis=0)
            to = s * UNITS + piece * each
            down_ref[to : to + each, :] = jnp.concatenate([rows[:each], tail], axis=1)


def finish_attend_kernel(in_ref, q_ref, k_ref, v_ref, o_ref, gain_ref):
    for piece in range(NB - 1):
        at = slice(piece * PIECE, (piece + 1) * PIECE)
        parts = [in_ref[piece, t * PIECE : (t + 1) * PIECE, :].astype(F32) for t in range(8)]
        lin = jnp.concatenate([part[:, :QKV_PART] for part in parts], axis=1)
        q_ref[at, :] = lin[:, : H * HD]
        k_ref[at, :] = lin[:, H * HD : (H + KV) * HD]
        v_ref[at, :] = lin[:, (H + KV) * HD :]
        o_ref[at, :] = jnp.concatenate(
            [part[:, OUT_AT : OUT_AT + OUT_PART] for part in parts], axis=1
        )
    sides = []
    for side in range(2):
        total = None
        for w in range(4):
            t = 2 * w + side
            own = in_ref[NB - 1, t * PIECE : (t + 1) * PIECE, 0:OUT_PART].astype(F32)[:8]
            total = own if total is None else total + own
        sides.append(total)
    gain_ref[...] = jnp.concatenate(sides, axis=1)


def whole(shape):
    return pl.BlockSpec(shape, lambda i: (0,) * len(shape))


def layer_of(layer, shape):
    return pl.BlockSpec((None,) + shape, lambda i: (layer,) + (0,) * len(shape))


def call(kernel, in_specs, outs, args, scratch=(), flops=0, moved=8_000_000, exps=0):
    return pl.pallas_call(
        kernel,
        grid=(1,),
        in_specs=in_specs,
        out_specs=[whole(shape) for shape, _ in outs],
        out_shape=[jax.ShapeDtypeStruct(shape, dtype) for shape, dtype in outs],
        scratch_shapes=list(scratch),
        compiler_params=pltpu.CompilerParams(vmem_limit_bytes=VMEM_BYTES),
        cost_estimate=pl.CostEstimate(flops=flops, bytes_accessed=moved, transcendentals=exps),
    )(*args)


SMEM = pl.BlockSpec(memory_space=pltpu.SMEM)
HBM = pl.BlockSpec(memory_space=pl.ANY)
PACK = (NB, ROWS + ROWS // 2, 2 * HD)
HEADS = (NB, ROWS // 2, 2 * HD)
GROUPS = ((0,), (1, 3), (2,))


def exchange(array):
    return lax.all_to_all(array, "blk", 0, 0, tiled=True)


def exchange_eight(array):
    return lax.all_to_all(array, EIGHT, 0, 0, tiled=True)


def sum_over_blocks(pieces):
    return jnp.sum(exchange(pieces).astype(F32), axis=0).astype(BF)


def weight_scratch(width):
    return [
        pltpu.VMEM((D, width), BF),
        pltpu.VMEM((4, 16, 256), BF),
        pltpu.SemaphoreType.DMA((2, 8)),
    ]


def body(
    tokens,
    cotangent,
    span_order,
    norm_one,
    w_query,
    w_key,
    w_value,
    w_out,
    norm_two,
    w_gate,
    w_up,
    w_down,
):
    section = lax.axis_index("section")
    shard = lax.axis_index("wshard")
    core = shard % 2
    y = 2 * (shard // 2) + section

    owners = []
    for step in range(4):
        there = (y + step) % 4
        for flip in range(2):
            owners += [there % 2, 2 * (there // 2) + (core ^ flip)]
    table = jnp.stack(owners).astype(jnp.int32)

    def with_gain(weight, gain):
        row = jnp.pad(gain[None], ((0, 15), (0, weight.shape[1] - SHARE)))
        return jnp.concatenate([weight, row], axis=0)

    first = jnp.concatenate([w_query[0], w_key[0], w_value[0]], axis=1)
    wqkv = sum(gather_eight(with_gain(first, norm_one[0])), [])
    out_block, gate_block, up_block, down_block = lax.optimization_barrier(
        (w_out[0], w_gate[0], w_up[0], w_down[0], wqkv[4])
    )[:4]
    wout = sum(gather_eight(with_gain(out_block, norm_two[0])), [])

    pieces = jnp.concatenate(
        [gate_block.reshape(SHARE, 4, 2, UNITS), up_block.reshape(SHARE, 4, 2, UNITS)], axis=3
    ).transpose(2, 1, 0, 3)
    wgu = exchange_eight(pieces.reshape(8, SHARE, 2 * UNITS)).reshape(2, D, 2 * UNITS)
    halves = down_block.reshape(2, UNITS, D)
    kept = lax.dynamic_index_in_dim(halves, section, 0, keepdims=False)
    sent = lax.dynamic_index_in_dim(halves, 1 - section, 0, keepdims=False)
    other = swap_section(sent)
    wdown = jnp.where(section == 0, jnp.stack([kept, other]), jnp.stack([other, kept]))

    block_index = lax.axis_index("blk")
    own_block = lax.dynamic_index_in_dim(span_order, block_index, 0, keepdims=False)
    positions = own_block * ROWS + jnp.arange(ROWS, dtype=jnp.int32)
    exponent = jnp.arange(HD // 2, dtype=F32) * (2.0 / HD)
    angles = positions.astype(F32)[:, None] * (rope_base ** (-exponent))[None, :]
    angles = jnp.concatenate([angles, angles], axis=-1)
    cosine, sine = jnp.cos(angles), jnp.sin(angles)
    slots = jnp.arange(NB, dtype=jnp.int32)
    place = jnp.sum(
        jnp.where(span_order[None, :] == slots[:, None], slots[None, :], 0), axis=1
    ).astype(jnp.int32)

    angle = whole((ROWS, HD))
    rows = whole((ROWS, D))
    row_scratch = pltpu.VMEM((LEN, HD), BF)
    weights = [HBM] * 8
    feed_weights = [(D, 2 * UNITS), (UNITS, D)]

    def forward(layer, x):
        h1, packed = call(
            functools.partial(project_kernel, layer),
            [SMEM, rows, angle, angle] + weights,
            [((ROWS, D), BF), (PACK, BF)],
            (table, x, cosine, sine, *wqkv),
            weight_scratch(QKV),
        )
        packed = exchange(packed)
        heads, lse = call(
            attend_kernel,
            [SMEM, whole(PACK)],
            [(HEADS, BF), ((8, LEN), F32)],
            (place, packed),
            [row_scratch] * 3,
            flops=1_000_000_000,
        )
        heads = exchange(heads)
        mixed, x2, h2 = call(
            functools.partial(mix_kernel, layer),
            [SMEM, whole(HEADS), rows] + weights,
            [((ROWS, D), BF), ((ROWS, D), F32), ((ROWS, D), BF)],
            (table, heads, x, *wout),
            weight_scratch(D),
        )
        found = gather_eight(h2)
        kept_ff, parts = [], [None] * 4
        for group in GROUPS:
            blocks = sum([found[step] for step in group], [])
            count = len(blocks)
            lin, hidden, *part = call(
                functools.partial(feed_kernel, count),
                [rows] * count + [layer_of(layer, shape) for shape in feed_weights],
                [((count * ROWS, 2 * UNITS), F32), ((count * ROWS, UNITS), BF)]
                + [((ROWS, D), BF)] * count,
                (*blocks, wgu, wdown),
                flops=500_000_000,
            )
            kept_ff.append((blocks, lin, hidden))
            for number, step in enumerate(group):
                parts[step] = part[2 * number : 2 * number + 2]
        y_out = x2 + scatter_eight(parts)
        both = lax.all_gather(jnp.concatenate([h1, mixed], axis=0), EIGHT, axis=0)
        return y_out, (x, both, packed, lse, x2, kept_ff)

    def backward(layer, dy, kept_state):
        x, both, packed, lse, x2, kept_ff = kept_state
        found = gather_eight(dy.astype(BF))
        parts, branches, lin_grads = [None] * 4, [], []
        for group, (_, lin, _) in zip(GROUPS, kept_ff):
            blocks = sum([found[step] for step in group], [])
            count = len(blocks)
            lin_grad, *part = call(
                functools.partial(feed_back_kernel, count),
                [rows] * count
                + [whole((count * ROWS, 2 * UNITS))]
                + [layer_of(layer, shape) for shape in feed_weights],
                [((count * ROWS, 2 * UNITS), BF)] + [((ROWS, D), BF)] * count,
                (*blocks, lin, wgu, wdown),
                flops=500_000_000,
            )
            branches += blocks
            lin_grads.append(lin_grad)
            for number, step in enumerate(group):
                parts[step] = part[2 * number : 2 * number + 2]
        dh2 = scatter_eight(parts)
        normed = sum([item[0] for item in kept_ff], [])
        sizes = [len(item[0]) * ROWS for item in kept_ff]
        grad_ff = call(
            feed_grads_kernel,
            [rows] * 16
            + [whole((size, 2 * UNITS)) for size in sizes]
            + [whole((size, UNITS)) for size in sizes],
            [((NB, FF_ROWS, 2 * UNITS), BF)],
            (*normed, *branches, *lin_grads, *[item[2] for item in kept_ff]),
            flops=2_000_000_000,
        )[0]
        dx2, heads_grad, e_parts, grad_gain_two = call(
            functools.partial(mix_back_kernel, layer),
            [SMEM, rows, rows, rows] + weights,
            [((ROWS, D), F32), (HEADS, BF), ((8, ROWS, 128), BF), ((1, D), F32)],
            (table, dy, dh2, x2, *wout),
            weight_scratch(D),
        )
        heads_grad = exchange(heads_grad)
        e_all = exchange_eight(e_parts)
        packed_grad = call(
            attend_back_kernel,
            [SMEM, whole(PACK), whole(HEADS), whole((8, LEN))],
            [(PACK, BF)],
            (place, packed, heads_grad, lse),
            [row_scratch] * 4
            + [pltpu.VMEM((HD, LEN), BF)]
            + [pltpu.VMEM((LEN, HD), F32)] * 3,
            flops=3_000_000_000,
        )[0]
        packed_grad = exchange(packed_grad)
        dx, lin_parts = call(
            functools.partial(project_back_kernel, layer),
            [SMEM, whole(PACK), rows, rows, angle, angle, whole((1, D))] + weights,
            [((ROWS, D), F32), ((8, ROWS + 16, 256), BF)],
            (table, packed_grad, dx2, x, cosine, sine, grad_gain_two, *wqkv),
            weight_scratch(QKV),
        )
        lin_all = exchange_eight(lin_parts)
        grad_att = call(
            attend_grads_kernel,
            [
                SMEM,
                whole((8, 2 * ROWS, D)),
                whole((8, ROWS + 16, 256)),
                whole((8, ROWS, 128)),
            ],
            [((NB, 4 * PIECE, ATT_WIDTH), BF)],
            (gain_owner, both, lin_all, e_all),
            flops=1_000_000_000,
        )[0]
        return dx, sum_over_blocks(grad_ff), sum_over_blocks(grad_att)

    gain_owner = ((4 * section + shard) // 2).astype(jnp.int32).reshape(1)
    x0 = lax.dynamic_index_in_dim(tokens[:, 0], section, 0, keepdims=False).astype(F32)
    cot = lax.dynamic_index_in_dim(cotangent[:, 0], section, 0, keepdims=False).astype(F32)
    y0, kept0 = forward(0, x0)
    y0 = y0.astype(BF)
    y1, kept1 = forward(1, y0.astype(F32))
    y1 = y1.astype(BF)
    dx1, ff1, att1 = backward(1, cot, kept1)
    dx0, ff0, att0 = backward(0, dx1.astype(BF).astype(F32), kept0)

    def by_section(of_first, of_second):
        own = jnp.where(section == 0, of_first, of_second)
        other = swap_section(jnp.where(section == 0, of_second, of_first))
        return jnp.where(section == 0, jnp.stack([own, other]), jnp.stack([other, own]))

    layer_outputs = by_section(y0, y1)
    input_grads = by_section(dx0, dx1)

    upper = 4 * PIECE
    spread = jnp.stack([ff0[:upper], ff1[:upper]]).reshape(8, PIECE, 2 * UNITS)
    spread = exchange_eight(spread).reshape(8 * PIECE, 2 * UNITS)
    lower = by_section(ff0[upper:], ff1[upper:]).reshape(-1, 2 * UNITS)
    found = lax.all_gather(jnp.concatenate([spread, lower], axis=0), "blk", axis=0)
    grad_gate, grad_up, grad_down = call(
        finish_feed_kernel,
        [whole(found.shape)],
        [((SHARE, FF), F32), ((SHARE, FF), F32), ((FF // 4, D), F32)],
        (found,),
    )
    spread = jnp.stack([att0, att1]).reshape(8, PIECE, ATT_WIDTH)
    spread = exchange_eight(spread).reshape(1, 8 * PIECE, ATT_WIDTH)
    found = exchange(jnp.broadcast_to(spread, (NB, 8 * PIECE, ATT_WIDTH)))
    grad_query, grad_key, grad_value, grad_out, gain_grads = call(
        finish_attend_kernel,
        [whole(found.shape)],
        [
            ((SHARE, H * HD), F32),
            ((SHARE, KV * HD), F32),
            ((SHARE, KV * HD), F32),
            ((SHARE, D), F32),
            ((8, SHARE), F32),
        ],
        (found,),
    )
    return (
        layer_outputs[None, :, None],
        input_grads[None, :, None],
        gain_grads[0][None],
        grad_query[None],
        grad_key[None],
        grad_value[None],
        grad_out[None],
        gain_grads[1][None],
        grad_gate[None],
        grad_up[None],
        grad_down[None],
    )


def solution(mesh):
    return jax.shard_map(
        body,
        mesh=mesh,
        in_specs=(
            P(None, "wshard", "blk", None),
            P(None, "wshard", "blk", None),
            P(),
            P("section", "wshard"),
            P("section", "wshard", None),
            P("section", "wshard", None),
            P("section", "wshard", None),
            P("section", "wshard", None),
            P("section", "wshard"),
            P("section", "wshard", None),
            P("section", "wshard", None),
            P("section", "wshard", None),
        ),
        out_specs=(
            P("section", None, "wshard", "blk", None),
            P("section", None, "wshard", "blk", None),
            P("section", "wshard"),
            P("section", "wshard", None),
            P("section", "wshard", None),
            P("section", "wshard", None),
            P("section", "wshard", None),
            P("section", "wshard"),
            P("section", "wshard", None),
            P("section", "wshard", None),
            P("section", "wshard", None),
        ),
        check_vma=False,
    )
```

```python
import functools

import jax
import jax.numpy as jnp
from jax import lax
from jax.experimental import pallas as pl
from jax.experimental.pallas import tpu as pltpu
from jax.sharding import PartitionSpec as P

D = 960
H = 15
KV = 5
HD = 64
FF = 2560
ROWS = 128
NB = 16
LEN = ROWS * NB
QKV = H * HD + 2 * KV * HD
UNITS = FF // 8
WIDE = 1664
SHARE = D // 4
PIECE = 16
QKV_PART = QKV // 8
OUT_PART = D // 8
OUT_AT = 256
ATT_WIDTH = 384
FF_WIDTH = D
TILE = 256

EIGHT = ("section", "wshard")
eps_norm = 1e-05
rope_base = 10000.0
BF = jnp.bfloat16
F32 = jnp.float32
VMEM_BYTES = 56 * 1024 * 1024


def place_of(y, core):
    return (y % 2) * 4 + (y // 2) * 2 + core


def ring_pairs(step, flip):
    return [
        (place_of(y, c), place_of((y + step) % 4, c ^ flip)) for y in range(4) for c in range(2)
    ]


def hop(array, step, flip=0):
    return lax.ppermute(array, EIGHT, ring_pairs(step, flip))


def swap_section(array):
    return lax.ppermute(array, "section", [(0, 1), (1, 0)])


def gather_eight(block):
    half = block.shape[0] // 2
    beside = hop(block, 0, 1)
    before = hop(block, 1)
    after = hop(block, -1)
    far = jnp.concatenate([hop(before[:half], 1), hop(after[half:], -1)], axis=0)
    return [
        [block, beside],
        [after, hop(after, 0, 1)],
        [far, hop(far, 0, 1)],
        [before, hop(before, 0, 1)],
    ]


def scatter_eight(parts):
    half = parts[0][0].shape[0] // 2
    total = [None] * 4
    for step in (2, 1, 3, 0):
        arrived = hop(parts[step][1].astype(BF), 0, 1)
        total[step] = parts[step][0].astype(F32) + arrived.astype(F32)
    far = total[2].astype(BF)
    low = hop(far[:half], 1).astype(F32)
    high = hop(far[half:], -1).astype(F32)
    forth = jnp.concatenate([total[1][:half] + low, total[1][half:]], axis=0).astype(BF)
    back = jnp.concatenate([total[3][:half], total[3][half:] + high], axis=0).astype(BF)
    return total[0] + hop(forth, 1).astype(F32) + hop(back, -1).astype(F32)


def norm_factor(values):
    return lax.rsqrt(jnp.mean(values * values, axis=-1, keepdims=True) + eps_norm)


def norm_backward(values, gain, grad):
    factor = norm_factor(values)
    scaled = grad * gain
    inner = jnp.mean(values * scaled, axis=-1, keepdims=True)
    grad_values = factor * scaled - values * (factor * factor * factor * inner)
    grad_gain = jnp.sum(grad * values * factor, axis=0, keepdims=True)
    return grad_values, grad_gain


def dot(left, right):
    return jnp.dot(left, right, preferred_element_type=F32)


def against(left, right):
    return lax.dot_general(left, right, (((1,), (1,)), ((), ())), preferred_element_type=F32)


def across(left, right):
    return lax.dot_general(left, right, (((0,), (0,)), ((), ())), preferred_element_type=F32)


def rotate(values, cosine, sine):
    half = HD // 2
    turned = jnp.concatenate([-values[:, half:], values[:, :half]], axis=1)
    return values * cosine + turned * sine


def rotate_back(grad, cosine, sine):
    half = HD // 2
    part = grad * sine
    return grad * cosine + jnp.concatenate([part[:, half:], -part[:, :half]], axis=1)


def fold(rows):
    half = rows.shape[0] // 2
    return jnp.concatenate([rows[:half], rows[half:]], axis=1)


def unfold(block):
    return jnp.concatenate([block[:, :HD], block[:, HD:]], axis=0)


def pack_attend_kernel(q_ref, k_ref, v_ref, o_ref, one_ref, two_ref, first_ref, second_ref):
    gap = jnp.zeros((SHARE, WIDE - QKV), BF)
    keys, values = jnp.transpose(k_ref[...]), jnp.transpose(v_ref[...])
    first_ref[0:SHARE, :] = jnp.concatenate([q_ref[...], keys, values, gap], axis=1)
    second_ref[0:SHARE, :] = o_ref[...]
    for ref, gain in ((first_ref, one_ref), (second_ref, two_ref)):
        row = jnp.concatenate([gain[...], jnp.zeros((15, SHARE), BF)], axis=0)
        width = ref.shape[1]
        ref[SHARE:, :] = jnp.concatenate([row, jnp.zeros((16, width - SHARE), BF)], axis=1)


def pack_feed_kernel(table_ref, gate_ref, up_ref, down_ref, pieces_ref, kept_ref, sent_ref):
    for s in range(2):
        for w in range(4):
            at = 2 * w + s
            at = slice(at * UNITS, (at + 1) * UNITS)
            pieces_ref[4 * s + w] = jnp.concatenate([gate_ref[:, at], up_ref[:, at]], axis=1)
    first, second = down_ref[:, :UNITS], down_ref[:, UNITS:]

    @pl.when(table_ref[0] == 0)
    def _():
        kept_ref[...] = first
        sent_ref[...] = second

    @pl.when(table_ref[0] == 1)
    def _():
        kept_ref[...] = second
        sent_ref[...] = first


def load_blocks(table_ref, layer, blocks, weight_ref, gain_ref, sems):
    def copies(number):
        place = table_ref[2 * number + 1]
        block = blocks[number]
        return (
            pltpu.make_async_copy(
                block.at[pl.ds(0, SHARE)],
                weight_ref.at[pl.ds(pl.multiple_of(place * SHARE, 16), SHARE)],
                sems.at[0, number],
            ),
            pltpu.make_async_copy(
                block.at[pl.ds(SHARE, 16), pl.ds(0, 256)], gain_ref.at[place], sems.at[1, number]
            ),
        )

    for number in range(8):

        @pl.when(table_ref[2 * number] == layer)
        def _():
            for copy in copies(number):
                copy.start()

    for number in range(8):

        @pl.when(table_ref[2 * number] == layer)
        def _():
            for copy in copies(number):
                copy.wait()

    return jnp.concatenate([gain_ref[w, 0:1, :SHARE] for w in range(4)], axis=1).astype(F32)


def project_kernel(layer, table_ref, x_ref, cos_ref, sin_ref, *refs):
    blocks, (h_ref, out_ref, w_ref, gain_ref, sems) = refs[:8], refs[8:]
    gain = load_blocks(table_ref, layer, blocks, w_ref, gain_ref, sems)
    x = x_ref[...]
    h = (x * norm_factor(x) * gain).astype(BF)
    h_ref[...] = h
    cosine, sine = cos_ref[...], sin_ref[...]
    lin = dot(h, w_ref[:, :QKV])

    def head(at):
        return lin[:, at * HD : (at + 1) * HD]

    for group in range(KV):
        key = rotate(head(H + group), cosine, sine).astype(BF)
        pair = jnp.concatenate([key, head(H + KV + group).astype(BF)], axis=1)
        for member in range(H // KV):
            index = group * (H // KV) + member
            out_ref[index, 0:ROWS, :] = pair
            query = rotate(head(index), cosine, sine).astype(BF)
            out_ref[index, ROWS:, :] = fold(query)
    out_ref[NB - 1] = jnp.zeros((ROWS + ROWS // 2, 2 * HD), BF)


def diagonal_mask(size, keys_first):
    rows = lax.broadcasted_iota(jnp.int32, (size, size), 0)
    columns = lax.broadcasted_iota(jnp.int32, (size, size), 1)
    return rows <= columns if keys_first else columns <= rows


def attend_kernel(place_ref, in_ref, out_ref, lse_ref, q_ref, k_ref, v_ref):
    for p in range(NB):
        block = in_ref[place_ref[p]]
        at = slice(p * ROWS, (p + 1) * ROWS)
        k_ref[at, :] = block[:ROWS, :HD]
        v_ref[at, :] = block[:ROWS, HD:]
        q_ref[at, :] = unfold(block[ROWS:])
    mask = diagonal_mask(TILE, False)
    for tile in range(LEN // TILE):
        at = slice(tile * TILE, (tile + 1) * TILE)
        seen = (tile + 1) * TILE
        scores = against(q_ref[at, :], k_ref[:seen, :]) * HD ** (-0.5)
        last = jnp.where(mask, scores[:, seen - TILE :], -jnp.inf)
        if tile:
            scores = jnp.concatenate([scores[:, : seen - TILE], last], axis=1)
        else:
            scores = last
        peak = jnp.max(scores, axis=-1, keepdims=True)
        terms = jnp.exp(scores - peak)
        total = jnp.sum(terms, axis=-1, keepdims=True)
        attend = (terms * (1.0 / total)).astype(BF)
        mixed = dot(attend, v_ref[:seen, :]).astype(BF)
        lse = peak + jnp.log(total)
        lse_ref[:, at] = jnp.transpose(jnp.broadcast_to(lse, (TILE, 128)))[:8, :]
        for part in range(TILE // ROWS):
            index = place_ref[tile * (TILE // ROWS) + part]
            out_ref[index] = fold(mixed[part * ROWS : (part + 1) * ROWS])


def attend_back_kernel(
    place_ref, in_ref, do_ref, lse_ref, out_ref, q_ref, k_ref, v_ref, g_ref, kt_ref, dq_ref, dk_ref, dv_ref
):
    for p in range(NB):
        block = in_ref[place_ref[p]]
        at = slice(p * ROWS, (p + 1) * ROWS)
        k_ref[at, :] = block[:ROWS, :HD]
        v_ref[at, :] = block[:ROWS, HD:]
        q_ref[at, :] = unfold(block[ROWS:])
        g_ref[at, :] = unfold(do_ref[place_ref[p]])
    kt_ref[...] = jnp.transpose(k_ref[...].astype(F32)).astype(BF)
    dk_ref[...] = jnp.zeros((LEN, HD), F32)
    dv_ref[...] = jnp.zeros((LEN, HD), F32)
    mask = diagonal_mask(TILE, True)
    for tile in range(LEN // TILE):
        at = slice(tile * TILE, (tile + 1) * TILE)
        seen = (tile + 1) * TILE
        query = q_ref[at, :]
        grad = g_ref[at, :]
        scores = against(k_ref[:seen, :], query) * HD ** (-0.5)
        last = jnp.where(mask, scores[seen - TILE :], -jnp.inf)
        if tile:
            scores = jnp.concatenate([scores[: seen - TILE], last], axis=0)
        else:
            scores = last
        full = jnp.exp(scores - lse_ref[0:1, at])
        attend_grad = against(v_ref[:seen, :], grad)
        inner = jnp.sum(full * attend_grad, axis=0, keepdims=True)
        score_grad = (full * (attend_grad - inner)).astype(BF)
        dv_ref[:seen, :] += dot(full.astype(BF), grad)
        dk_ref[:seen, :] += dot(score_grad, query)
        dq_ref[at, :] = jnp.transpose(dot(kt_ref[:, :seen], score_grad))
    for p in range(NB):
        index = place_ref[p]
        at = slice(p * ROWS, (p + 1) * ROWS)
        key_grad = (dk_ref[at, :] * HD ** (-0.5)).astype(BF)
        query_grad = (dq_ref[at, :] * HD ** (-0.5)).astype(BF)
        out_ref[index, 0:ROWS, :] = jnp.concatenate([key_grad, dv_ref[at, :].astype(BF)], axis=1)
        out_ref[index, ROWS:, :] = fold(query_grad)


def mix_kernel(layer, table_ref, in_ref, x_ref, *refs):
    blocks, (o_ref, x2_ref, h_ref, w_ref, gain_ref, sems) = refs[:8], refs[8:]
    gain = load_blocks(table_ref, layer, blocks, w_ref, gain_ref, sems)
    mixed = jnp.concatenate([unfold(in_ref[index]) for index in range(H)], axis=1)
    o_ref[...] = mixed
    x2 = x_ref[...] + dot(mixed, w_ref[...])
    x2_ref[...] = x2
    h_ref[...] = (x2 * norm_factor(x2) * gain).astype(BF)


def mix_back_kernel(layer, table_ref, dy_ref, dh_ref, x2_ref, *refs):
    blocks, (dx2_ref, out_ref, e_ref, gg_ref, w_ref, gain_ref, sems) = refs[:8], refs[8:]
    gain = load_blocks(table_ref, layer, blocks, w_ref, gain_ref, sems)
    part, grad_gain = norm_backward(x2_ref[...], gain, dh_ref[...])
    dx2 = dy_ref[...] + part
    dx2_ref[...] = dx2
    gg_ref[...] = grad_gain
    low = dx2.astype(BF)
    for index in range(8):
        e_ref[index, :, 0:OUT_PART] = low[:, index * OUT_PART : (index + 1) * OUT_PART]
        e_ref[index, :, OUT_PART:] = jnp.zeros((ROWS, 128 - OUT_PART), BF)
    mixed_grad = against(low, w_ref[...]).astype(BF)
    for index in range(H):
        out_ref[index] = fold(mixed_grad[:, index * HD : (index + 1) * HD])
    out_ref[NB - 1] = jnp.zeros((ROWS // 2, 2 * HD), BF)


def project_back_kernel(layer, table_ref, in_ref, dx2_ref, x_ref, cos_ref, sin_ref, gg_ref, *refs):
    blocks, (dx_ref, lin_ref, w_ref, gain_ref, sems) = refs[:8], refs[8:]
    gain = load_blocks(table_ref, layer, blocks, w_ref, gain_ref, sems)
    cosine, sine = cos_ref[...], sin_ref[...]
    queries, keys, values = [], [], []
    for group in range(KV):
        pair = None
        for member in range(H // KV):
            index = group * (H // KV) + member
            own = in_ref[index, 0:ROWS, :].astype(F32)
            pair = own if pair is None else pair + own
            query = unfold(in_ref[index, ROWS:, :].astype(F32))
            queries.append(rotate_back(query, cosine, sine).astype(BF))
        keys.append(rotate_back(pair[:, :HD], cosine, sine).astype(BF))
        values.append(pair[:, HD:].astype(BF))
    lin_grad = jnp.concatenate(queries + keys + values, axis=1)
    part, grad_gain = norm_backward(x_ref[...], gain, against(lin_grad, w_ref[:, :QKV]))
    dx_ref[...] = dx2_ref[...] + part
    gains = jnp.concatenate([grad_gain, gg_ref[...], jnp.zeros((14, D), F32)], axis=0).astype(BF)
    for index in range(8):
        lin_ref[index, 0:ROWS, 0:QKV_PART] = lin_grad[:, index * QKV_PART : (index + 1) * QKV_PART]
        lin_ref[index, 0:ROWS, QKV_PART:] = jnp.zeros((ROWS, 256 - QKV_PART), BF)
        lin_ref[index, ROWS:, 0:OUT_PART] = gains[:, index * OUT_PART : (index + 1) * OUT_PART]
        lin_ref[index, ROWS:, OUT_PART:] = jnp.zeros((16, 256 - OUT_PART), BF)


def feed_kernel(count, layer, table_ref, *refs):
    normed = jnp.concatenate([ref[...] for ref in refs[:count]], axis=0)
    wgu_ref, kept_ref, other_ref, lin_ref, hidden_ref = refs[count : count + 5]
    lin = dot(normed, wgu_ref[...])
    lin_ref[...] = lin
    gate, up = lin[:, :UNITS], lin[:, UNITS:]
    hidden = (gate * jax.nn.sigmoid(gate) * up).astype(BF)
    hidden_ref[...] = hidden
    down = jnp.where(table_ref[0] == layer, kept_ref[...], other_ref[...])
    part = against(hidden, down).astype(BF)
    for index, ref in enumerate(refs[count + 5 :]):
        ref[...] = part[index * ROWS : (index + 1) * ROWS]


def feed_back_kernel(count, layer, table_ref, *refs):
    branch = jnp.concatenate([ref[...] for ref in refs[:count]], axis=0)
    lin_ref, wgu_ref, kept_ref, other_ref, grad_ref = refs[count : count + 5]
    down = jnp.where(table_ref[0] == layer, kept_ref[...], other_ref[...])
    hidden_grad = dot(branch, down)
    gate, up = lin_ref[:, :UNITS], lin_ref[:, UNITS:]
    sig = jax.nn.sigmoid(gate)
    up_grad = hidden_grad * (gate * sig)
    gate_grad = hidden_grad * up * (sig + gate * sig * (1.0 - sig))
    lin_grad = jnp.concatenate([gate_grad, up_grad], axis=1).astype(BF)
    grad_ref[...] = lin_grad
    part = against(lin_grad, wgu_ref[...]).astype(BF)
    for index, ref in enumerate(refs[count + 5 :]):
        ref[...] = part[index * ROWS : (index + 1) * ROWS]


def feed_grads_kernel(*refs):
    normed = jnp.concatenate([ref[...] for ref in refs[:8]], axis=0)
    branch = jnp.concatenate([ref[...] for ref in refs[8:16]], axis=0)
    lin_grad = jnp.concatenate([ref[...] for ref in refs[16:19]], axis=0)
    hidden = jnp.concatenate([ref[...] for ref in refs[19:22]], axis=0)
    out_ref = refs[22]
    gate_up = across(normed, lin_grad).astype(BF)
    down = across(branch, hidden).astype(BF)
    for piece in range(NB - 1):
        rows = [
            gate_up[w * SHARE + piece * PIECE : w * SHARE + (piece + 1) * PIECE] for w in range(4)
        ]
        lower = down[4 * piece * PIECE : 4 * (piece + 1) * PIECE]
        out_ref[piece] = jnp.concatenate([jnp.concatenate(rows, axis=0), lower], axis=1)
    out_ref[NB - 1] = jnp.zeros((4 * PIECE, FF_WIDTH), BF)


def attend_grads_kernel(index_ref, table_ref, *refs):
    blocks, (lin_ref, e_ref, out_ref) = refs[:8], refs[8:]
    sources = [4 * table_ref[2 * k] + table_ref[2 * k + 1] for k in range(8)]
    normed = jnp.concatenate([ref[0:ROWS, :] for ref in blocks], axis=0)
    mixed = jnp.concatenate([ref[ROWS:, :] for ref in blocks], axis=0)
    lin_grad = jnp.concatenate([lin_ref[t, 0:ROWS, :] for t in sources], axis=0)
    branch = jnp.concatenate([e_ref[t] for t in sources], axis=0)
    weight = across(normed, lin_grad).astype(BF)
    out_weight = across(mixed, branch).astype(BF)
    for piece in range(NB - 1):
        for w in range(4):
            at = w * SHARE + piece * PIECE
            to = slice(w * PIECE, (w + 1) * PIECE)
            out_ref[piece, to, 0:OUT_AT] = weight[at : at + PIECE]
            out_ref[piece, to, OUT_AT:] = out_weight[at : at + PIECE]
    gains = lin_ref[0, ROWS:, :].astype(F32)
    for t in range(1, 8):
        gains = gains + lin_ref[t, ROWS:, :].astype(F32)
    out_ref[NB - 1] = jnp.zeros((4 * PIECE, ATT_WIDTH), BF)
    at = pl.multiple_of(index_ref[0] * PIECE, PIECE)
    out_ref[NB - 1, pl.ds(at, PIECE), 0:OUT_AT] = gains.astype(BF)


def finish_feed_kernel(in_ref, gate_ref, up_ref, down_ref):
    for piece in range(NB - 1):
        at = slice(piece * PIECE, (piece + 1) * PIECE)
        parts = []
        for w in range(4):
            for s in range(2):
                at_row = (4 * s + w) * PIECE
                parts.append(in_ref[piece, at_row : at_row + PIECE, :].astype(F32))
        gate_ref[at, :] = jnp.concatenate([part[:, :UNITS] for part in parts], axis=1)
        up_ref[at, :] = jnp.concatenate([part[:, UNITS:] for part in parts], axis=1)
        rows = in_ref[piece, 8 * PIECE :, :].astype(F32)
        to = slice(4 * piece * PIECE, 4 * (piece + 1) * PIECE)
        down_ref[to, :] = rows


def finish_attend_kernel(in_ref, q_ref, k_ref, v_ref, o_ref, gain_ref):
    keys, values = [], []
    for piece in range(NB - 1):
        at = slice(piece * PIECE, (piece + 1) * PIECE)
        parts = [in_ref[piece, t * PIECE : (t + 1) * PIECE, :].astype(F32) for t in range(8)]
        lin = jnp.concatenate([part[:, :QKV_PART] for part in parts], axis=1)
        q_ref[at, :] = lin[:, : H * HD]
        keys.append(lin[:, H * HD : (H + KV) * HD])
        values.append(lin[:, (H + KV) * HD :])
        o_ref[at, :] = jnp.concatenate(
            [part[:, OUT_AT : OUT_AT + OUT_PART] for part in parts], axis=1
        )
    k_ref[...] = jnp.transpose(jnp.concatenate(keys, axis=0))
    v_ref[...] = jnp.transpose(jnp.concatenate(values, axis=0))
    sides = []
    for side in range(2):
        total = None
        for w in range(4):
            t = 2 * w + side
            own = in_ref[NB - 1, t * PIECE : (t + 1) * PIECE, 0:OUT_PART].astype(F32)[:8]
            total = own if total is None else total + own
        sides.append(total)
    gain_ref[...] = jnp.concatenate(sides, axis=1)


def whole(shape):
    return pl.BlockSpec(shape, lambda i: (0,) * len(shape))


def layer_of(layer, shape):
    return pl.BlockSpec((None,) + shape, lambda i: (layer,) + (0,) * len(shape))


def call(kernel, in_specs, outs, args, scratch=()):
    return pl.pallas_call(
        kernel,
        grid=(1,),
        in_specs=in_specs,
        out_specs=[whole(shape) for shape, _ in outs],
        out_shape=[jax.ShapeDtypeStruct(shape, dtype) for shape, dtype in outs],
        scratch_shapes=list(scratch),
        compiler_params=pltpu.CompilerParams(vmem_limit_bytes=VMEM_BYTES),
        cost_estimate=pl.CostEstimate(flops=1, bytes_accessed=1, transcendentals=0),
    )(*args)


SMEM = pl.BlockSpec(memory_space=pltpu.SMEM)
HBM = pl.BlockSpec(memory_space=pl.ANY)
PACK = (NB, ROWS + ROWS // 2, 2 * HD)
HEADS = (NB, ROWS // 2, 2 * HD)
GROUPS = ((0,), (1, 3), (2,))


def exchange(array):
    return lax.all_to_all(array, "blk", 0, 0, tiled=True)


def exchange_eight(array):
    return lax.all_to_all(array, EIGHT, 0, 0, tiled=True)


def sum_over_blocks(pieces):
    return jnp.sum(exchange(pieces).astype(F32), axis=0).astype(BF)


def weight_scratch(width):
    return [
        pltpu.VMEM((D, width), BF),
        pltpu.VMEM((4, 16, 256), BF),
        pltpu.SemaphoreType.DMA((2, 8)),
    ]


def body(
    tokens,
    cotangent,
    span_order,
    norm_one,
    w_query,
    w_key,
    w_value,
    w_out,
    norm_two,
    w_gate,
    w_up,
    w_down,
):
    section = lax.axis_index("section")
    shard = lax.axis_index("wshard")
    core = shard % 2
    y = 2 * (shard // 2) + section

    owners = []
    for step in range(4):
        there = (y + step) % 4
        for flip in range(2):
            owners += [there % 2, 2 * (there // 2) + (core ^ flip)]
    table = jnp.stack(owners).astype(jnp.int32)

    x0 = lax.dynamic_index_in_dim(tokens[:, 0], section, 0, keepdims=False).astype(F32)
    cot = lax.dynamic_index_in_dim(cotangent[:, 0], section, 0, keepdims=False).astype(F32)
    first, second = call(
        pack_attend_kernel,
        [
            whole((SHARE, D)),
            whole((KV * HD, SHARE)),
            whole((KV * HD, SHARE)),
            whole((SHARE, D)),
            whole((1, SHARE)),
            whole((1, SHARE)),
        ],
        [((SHARE + 16, WIDE), BF), ((SHARE + 16, D), BF)],
        (w_query[0], w_key[0].T, w_value[0].T, w_out[0], norm_one, norm_two),
    )
    pieces, kept, sent = call(
        pack_feed_kernel,
        [SMEM, whole((SHARE, FF)), whole((SHARE, FF)), whole((D, FF // 4))],
        [((8, SHARE, 2 * UNITS), BF), ((D, UNITS), BF), ((D, UNITS), BF)],
        (table, w_gate[0], w_up[0], w_down[0].T),
    )
    wqkv = sum(gather_eight(first), [])
    wqkv[4], second, pieces, sent = lax.optimization_barrier((wqkv[4], second, pieces, sent))
    wout = sum(gather_eight(second), [])
    wgu = exchange_eight(pieces).reshape(2, D, 2 * UNITS)
    other = swap_section(sent)

    block_index = lax.axis_index("blk")
    own_block = lax.dynamic_index_in_dim(span_order, block_index, 0, keepdims=False)
    positions = own_block * ROWS + jnp.arange(ROWS, dtype=jnp.int32)
    exponent = jnp.arange(HD // 2, dtype=F32) * (2.0 / HD)
    angles = positions.astype(F32)[:, None] * (rope_base ** (-exponent))[None, :]
    angles = jnp.concatenate([angles, angles], axis=-1)
    cosine, sine = jnp.cos(angles), jnp.sin(angles)
    slots = jnp.arange(NB, dtype=jnp.int32)
    place = jnp.sum(
        jnp.where(span_order[None, :] == slots[:, None], slots[None, :], 0), axis=1
    ).astype(jnp.int32)

    angle = whole((ROWS, HD))
    rows = whole((ROWS, D))
    row_scratch = pltpu.VMEM((LEN, HD), BF)
    weights = [HBM] * 8
    half_down = whole((D, UNITS))

    def forward(layer, x, meanwhile):
        h1, packed = call(
            functools.partial(project_kernel, layer),
            [SMEM, rows, angle, angle] + weights,
            [((ROWS, D), BF), (PACK, BF)],
            (table, x, cosine, sine, *wqkv),
            weight_scratch(WIDE),
        )
        beside = meanwhile(packed)
        packed = exchange(packed)
        heads, lse = call(
            attend_kernel,
            [SMEM, whole(PACK)],
            [(HEADS, BF), ((8, LEN), F32)],
            (place, packed),
            [row_scratch] * 3,
        )
        heads = exchange(heads)
        heads, beside = lax.optimization_barrier((heads, beside))
        mixed, x2, h2 = call(
            functools.partial(mix_kernel, layer),
            [SMEM, whole(HEADS), rows] + weights,
            [((ROWS, D), BF), ((ROWS, D), F32), ((ROWS, D), BF)],
            (table, heads, x, *wout),
            weight_scratch(D),
        )
        found = gather_eight(h2)
        kept_ff, parts = [], [None] * 4
        for group in GROUPS:
            blocks = sum([found[step] for step in group], [])
            count = len(blocks)
            lin, hidden, *part = call(
                functools.partial(feed_kernel, count, layer),
                [SMEM] + [rows] * count + [layer_of(layer, (D, 2 * UNITS)), half_down, half_down],
                [((count * ROWS, 2 * UNITS), F32), ((count * ROWS, UNITS), BF)]
                + [((ROWS, D), BF)] * count,
                (table, *blocks, wgu, kept, other),
            )
            kept_ff.append((blocks, lin, hidden))
            for number, step in enumerate(group):
                parts[step] = part[2 * number : 2 * number + 2]
        both = jnp.concatenate([h1, mixed], axis=0)
        return parts, beside, (x, both, packed, lse, x2, kept_ff)

    def backward(layer, dy, found, kept_state, beside_feed, beside_attend):
        x, _, packed, lse, x2, kept_ff = kept_state
        parts, branches, lin_grads = [None] * 4, [], []
        for group, (_, lin, _) in zip(GROUPS, kept_ff):
            blocks = sum([found[step] for step in group], [])
            count = len(blocks)
            lin_grad, *part = call(
                functools.partial(feed_back_kernel, count, layer),
                [SMEM]
                + [rows] * count
                + [whole((count * ROWS, 2 * UNITS))]
                + [layer_of(layer, (D, 2 * UNITS)), half_down, half_down],
                [((count * ROWS, 2 * UNITS), BF)] + [((ROWS, D), BF)] * count,
                (table, *blocks, lin, wgu, kept, other),
            )
            branches += blocks
            lin_grads.append(lin_grad)
            for number, step in enumerate(group):
                parts[step] = part[2 * number : 2 * number + 2]
        dh2 = scatter_eight(parts)
        normed = sum([item[0] for item in kept_ff], [])
        sizes = [len(item[0]) * ROWS for item in kept_ff]
        grad_ff = call(
            feed_grads_kernel,
            [rows] * 16
            + [whole((size, 2 * UNITS)) for size in sizes]
            + [whole((size, UNITS)) for size in sizes],
            [((NB, 4 * PIECE, FF_WIDTH), BF)],
            (*normed, *branches, *lin_grads, *[item[2] for item in kept_ff]),
        )[0]
        dh2, fed = lax.optimization_barrier((dh2, beside_feed))
        dx2, heads_grad, e_parts, grad_gain_two = call(
            functools.partial(mix_back_kernel, layer),
            [SMEM, rows, rows, rows] + weights,
            [((ROWS, D), F32), (HEADS, BF), ((8, ROWS, 128), BF), ((1, D), F32)],
            (table, dy, dh2, x2, *wout),
            weight_scratch(D),
        )
        attended = beside_attend(dx2, grad_ff)
        e_all = exchange_eight(e_parts)
        heads_grad = exchange(heads_grad)
        packed_grad = call(
            attend_back_kernel,
            [SMEM, whole(PACK), whole(HEADS), whole((8, LEN))],
            [(PACK, BF)],
            (place, packed, heads_grad, lse),
            [row_scratch] * 4
            + [pltpu.VMEM((HD, LEN), BF)]
            + [pltpu.VMEM((LEN, HD), F32)] * 3,
        )[0]
        packed_grad = exchange(packed_grad)
        packed_grad, e_all, attended = lax.optimization_barrier((packed_grad, e_all, attended))
        dx, lin_parts = call(
            functools.partial(project_back_kernel, layer),
            [SMEM, whole(PACK), rows, rows, angle, angle, whole((1, D))] + weights,
            [((ROWS, D), F32), ((8, ROWS + 16, 256), BF)],
            (table, packed_grad, dx2, x, cosine, sine, grad_gain_two, *wqkv),
            weight_scratch(WIDE),
        )
        return dx, lin_parts, e_all, grad_ff, fed, attended

    def attend_grads(blocks, lin_all, e_all):
        return call(
            attend_grads_kernel,
            [SMEM, SMEM]
            + [whole((2 * ROWS, D))] * 8
            + [whole((8, ROWS + 16, 256)), whole((8, ROWS, 128))],
            [((NB, 4 * PIECE, ATT_WIDTH), BF)],
            (gain_owner, table, *blocks, lin_all, e_all),
        )[0]

    def after(value, *others):
        return lax.optimization_barrier((value, *others))[0]

    def by_section(of_first, of_second):
        own = jnp.where(section == 0, of_first, of_second)
        other = swap_section(jnp.where(section == 0, of_second, of_first))
        return jnp.where(section == 0, jnp.stack([own, other]), jnp.stack([other, own]))

    gain_owner = ((4 * section + shard) // 2).astype(jnp.int32).reshape(1)
    parts, (wgu, other), kept0 = forward(0, x0, lambda packed: (wgu, other))
    y0 = (kept0[4] + scatter_eight(parts)).astype(BF)
    parts1, (found, both0), kept1 = forward(
        1,
        y0.astype(F32),
        lambda packed: (gather_eight(after(cot.astype(BF), packed)), gather_eight(after(kept0[1], packed))),
    )
    dx1, lin1, e1, grad_ff1, _, both1 = backward(
        1, cot, found, kept1, (), lambda dx2, grad_ff: gather_eight(after(kept1[1], dx2))
    )
    dy0 = dx1.astype(BF)
    ff1 = sum_over_blocks(after(grad_ff1, dx1))

    def beside_last(dx2, grad_ff):
        parts = after(parts1, dx2)
        y1 = (kept1[4] + scatter_eight(parts)).astype(BF)
        outputs = by_section(y0, y1)
        return exchange_eight(after(lin1, dx2)), outputs

    dx0, lin0, e0, grad_ff0, ff1, (lin1, layer_outputs) = backward(
        0, dy0.astype(F32), gather_eight(dy0), kept0, ff1, beside_last
    )
    ff0 = sum_over_blocks(grad_ff0)
    upper = 2 * UNITS
    spread = jnp.stack([ff0[:, :upper], ff1[:, :upper]]).reshape(8, PIECE, upper)
    spread = exchange_eight(spread).reshape(8 * PIECE, upper)
    lower = by_section(ff0[:, upper:], ff1[:, upper:])
    lower = jnp.concatenate([lower[0], lower[1]], axis=1)
    found = lax.all_gather(jnp.concatenate([spread, lower], axis=0), "blk", axis=0)
    att1 = sum_over_blocks(attend_grads(sum(both1, []), lin1, e1))
    att0 = attend_grads(sum(both0, []), exchange_eight(lin0), e0)
    input_grads = by_section(dx0, dx1)
    att0 = sum_over_blocks(att0)
    grad_gate, grad_up, grad_down = call(
        finish_feed_kernel,
        [whole(found.shape)],
        [((SHARE, FF), F32), ((SHARE, FF), F32), ((D, FF // 4), F32)],
        (found,),
    )
    spread = jnp.stack([att0, att1]).reshape(8, PIECE, ATT_WIDTH)
    spread = exchange_eight(spread).reshape(1, 8 * PIECE, ATT_WIDTH)
    found = exchange(jnp.broadcast_to(spread, (NB, 8 * PIECE, ATT_WIDTH)))
    grad_query, grad_key, grad_value, grad_out, gain_grads = call(
        finish_attend_kernel,
        [whole(found.shape)],
        [
            ((SHARE, H * HD), F32),
            ((KV * HD, SHARE), F32),
            ((KV * HD, SHARE), F32),
            ((SHARE, D), F32),
            ((8, SHARE), F32),
        ],
        (found,),
    )
    return (
        layer_outputs[None, :, None],
        input_grads[None, :, None],
        gain_grads[0][None],
        grad_query[None],
        grad_key.T[None],
        grad_value.T[None],
        grad_out[None],
        gain_grads[1][None],
        grad_gate[None],
        grad_up[None],
        grad_down.T[None],
    )


def solution(mesh):
    return jax.shard_map(
        body,
        mesh=mesh,
        in_specs=(
            P(None, "wshard", "blk", None),
            P(None, "wshard", "blk", None),
            P(),
            P("section", "wshard"),
            P("section", "wshard", None),
            P("section", "wshard", None),
            P("section", "wshard", None),
            P("section", "wshard", None),
            P("section", "wshard"),
            P("section", "wshard", None),
            P("section", "wshard", None),
            P("section", "wshard", None),
        ),
        out_specs=(
            P("section", None, "wshard", "blk", None),
            P("section", None, "wshard", "blk", None),
            P("section", "wshard"),
            P("section", "wshard", None),
            P("section", "wshard", None),
            P("section", "wshard", None),
            P("section", "wshard", None),
            P("section", "wshard"),
            P("section", "wshard", None),
            P("section", "wshard", None),
            P("section", "wshard", None),
        ),
        check_vma=False,
    )
```

```python
import functools

import jax
import jax.numpy as jnp
from jax import lax
from jax.experimental import pallas as pl
from jax.experimental.pallas import tpu as pltpu
from jax.sharding import PartitionSpec as P

D = 960
H = 15
KV = 5
HD = 64
FF = 2560
ROWS = 128
NB = 16
LEN = ROWS * NB
QKV = H * HD + 2 * KV * HD
UNITS = FF // 8
WIDE = 1664
SHARE = D // 4
PIECE = 16
QKV_PART = QKV // 8
OUT_PART = D // 8
OUT_AT = 256
ATT_WIDTH = 384
FF_WIDTH = D
TILE = 256

EIGHT = ("section", "wshard")
eps_norm = 1e-05
rope_base = 10000.0
BF = jnp.bfloat16
F32 = jnp.float32
VMEM_BYTES = 56 * 1024 * 1024


def place_of(y, core):
    return (y % 2) * 4 + (y // 2) * 2 + core


def ring_pairs(step, flip):
    return [
        (place_of(y, c), place_of((y + step) % 4, c ^ flip)) for y in range(4) for c in range(2)
    ]


def hop(array, step, flip=0):
    return lax.ppermute(array, EIGHT, ring_pairs(step, flip))


def swap_section(array):
    return lax.ppermute(array, "section", [(0, 1), (1, 0)])


def after(values, *others):
    return lax.optimization_barrier((values, others))[0]


def gather_near(block):
    before = hop(block, 1)
    after_it = hop(block, -1)
    return block, hop(block, 0, 1), after_it, before


def gather_far(near):
    half = near[0].shape[0] // 2
    low, high = hop(near[3][:half], 1), hop(near[2][half:], -1)
    beside = [hop(near[2], 0, 1), hop(near[3], 0, 1)]
    return low, high, hop(low, 0, 1), hop(high, 0, 1), *beside


def arranged(near, far):
    return [[near[0], near[1]], [near[2], far[4]], list(far[:4]), [near[3], far[5]]]


def gather_eight(block):
    near = gather_near(block)
    return arranged(near, gather_far(near))


def exchange_eight(parts):
    found = [parts[0]] + [None] * 7
    for step, flip in ((0, 1), (1, 0), (3, 0), (1, 1), (3, 1), (2, 0), (2, 1)):
        found[2 * ((4 - step) % 4) + flip] = hop(parts[2 * step + flip], step, flip)
    return found


def scatter_eight(parts):
    half = parts[0][0].shape[0] // 2
    total = [None] * 4
    for step in (2, 1, 3, 0):
        total[step] = parts[step][0].astype(F32) + hop(parts[step][1], 0, 1).astype(F32)
    far = total[2].astype(BF)
    low = hop(far[:half], 1).astype(F32)
    high = hop(far[half:], -1).astype(F32)
    forth = jnp.concatenate([total[1][:half] + low, total[1][half:]], axis=0).astype(BF)
    back = jnp.concatenate([total[3][:half], total[3][half:] + high], axis=0).astype(BF)
    return total[0] + hop(forth, 1).astype(F32) + hop(back, -1).astype(F32)


def norm_factor(values):
    return lax.rsqrt(jnp.mean(values * values, axis=-1, keepdims=True) + eps_norm)


def norm_backward(values, gain, grad):
    factor = norm_factor(values)
    scaled = grad * gain
    inner = jnp.mean(values * scaled, axis=-1, keepdims=True)
    grad_values = factor * scaled - values * (factor * factor * factor * inner)
    grad_gain = jnp.sum(grad * values * factor, axis=0, keepdims=True)
    return grad_values, grad_gain


def dot(left, right):
    return jnp.dot(left, right, preferred_element_type=F32)


def against(left, right):
    return lax.dot_general(left, right, (((1,), (1,)), ((), ())), preferred_element_type=F32)


def across(left, right):
    return lax.dot_general(left, right, (((0,), (0,)), ((), ())), preferred_element_type=F32)


def rotate(values, cosine, sine):
    half = HD // 2
    turned = jnp.concatenate([-values[:, half:], values[:, :half]], axis=1)
    return values * cosine + turned * sine


def rotate_back(grad, cosine, sine):
    half = HD // 2
    part = grad * sine
    return grad * cosine + jnp.concatenate([part[:, half:], -part[:, :half]], axis=1)


def fold(rows):
    half = rows.shape[0] // 2
    return jnp.concatenate([rows[:half], rows[half:]], axis=1)


def unfold(block):
    return jnp.concatenate([block[:, :HD], block[:, HD:]], axis=0)


def pack_attend_kernel(q_ref, k_ref, v_ref, o_ref, one_ref, two_ref, first_ref, second_ref):
    gap = jnp.zeros((SHARE, WIDE - QKV), BF)
    keys, values = jnp.transpose(k_ref[...]), jnp.transpose(v_ref[...])
    first_ref[0:SHARE, :] = jnp.concatenate([q_ref[...], keys, values, gap], axis=1)
    second_ref[0:SHARE, :] = o_ref[...]
    for ref, gain in ((first_ref, one_ref), (second_ref, two_ref)):
        row = jnp.concatenate([gain[...], jnp.zeros((15, SHARE), BF)], axis=0)
        width = ref.shape[1]
        ref[SHARE:, :] = jnp.concatenate([row, jnp.zeros((16, width - SHARE), BF)], axis=1)


def pack_feed_kernel(table_ref, gate_ref, up_ref, down_ref, *refs):
    pieces, (kept_ref, sent_ref, held_ref) = refs[:8], refs[8:]
    for s in range(2):
        for w in range(4):
            at = 2 * w + s
            at = slice(at * UNITS, (at + 1) * UNITS)
            held_ref[4 * s + w] = jnp.concatenate([gate_ref[:, at], up_ref[:, at]], axis=1)
    for number in range(8):
        pieces[number][...] = held_ref[4 * table_ref[2 * number] + table_ref[2 * number + 1]]
    first, second = down_ref[:, :UNITS], down_ref[:, UNITS:]

    @pl.when(table_ref[0] == 0)
    def _():
        kept_ref[...] = first
        sent_ref[...] = second

    @pl.when(table_ref[0] == 1)
    def _():
        kept_ref[...] = second
        sent_ref[...] = first


def load_blocks(table_ref, layer, blocks, weight_ref, sems, gain_ref=None):
    def copies(number):
        place = table_ref[2 * number + 1]
        done = 0
        for part, block in enumerate(blocks[number]):
            rows = min(block.shape[0], SHARE - done)
            yield pltpu.make_async_copy(
                block.at[pl.ds(0, rows)],
                weight_ref.at[pl.ds(pl.multiple_of(place * SHARE + done, 16), rows)],
                sems.at[part, number],
            )
            done += rows
        if gain_ref is not None:
            last = block.shape[0] - 16
            yield pltpu.make_async_copy(
                block.at[pl.ds(last, 16), pl.ds(0, 256)], gain_ref.at[place], sems.at[2, number]
            )

    for number in range(8):

        @pl.when(table_ref[2 * number] == layer)
        def _():
            for copy in copies(number):
                copy.start()

    for number in range(8):

        @pl.when(table_ref[2 * number] == layer)
        def _():
            for copy in copies(number):
                copy.wait()

    if gain_ref is not None:
        return jnp.concatenate([gain_ref[w, 0:1, :SHARE] for w in range(4)], axis=1).astype(F32)


def by_block(refs):
    return [refs[0:1], refs[1:2], refs[2:3], refs[3:4], refs[4:6], refs[6:8], refs[8:9], refs[9:10]]


def project_kernel(layer, table_ref, x_ref, cos_ref, sin_ref, *refs):
    blocks, (h_ref, out_ref, w_ref, gain_ref, sems) = by_block(refs), refs[10:]
    gain = load_blocks(table_ref, layer, blocks, w_ref, sems, gain_ref)
    x = x_ref[...]
    h = (x * norm_factor(x) * gain).astype(BF)
    h_ref[...] = h
    cosine, sine = cos_ref[...], sin_ref[...]
    lin = dot(h, w_ref[:, :QKV])

    def head(at):
        return lin[:, at * HD : (at + 1) * HD]

    for group in range(KV):
        key = rotate(head(H + group), cosine, sine).astype(BF)
        pair = jnp.concatenate([key, head(H + KV + group).astype(BF)], axis=1)
        for member in range(H // KV):
            index = group * (H // KV) + member
            out_ref[index, 0:ROWS, :] = pair
            query = rotate(head(index), cosine, sine).astype(BF)
            out_ref[index, ROWS:, :] = fold(query)
    out_ref[NB - 1] = jnp.zeros((ROWS + ROWS // 2, 2 * HD), BF)


def diagonal_mask(size, keys_first):
    rows = lax.broadcasted_iota(jnp.int32, (size, size), 0)
    columns = lax.broadcasted_iota(jnp.int32, (size, size), 1)
    return rows <= columns if keys_first else columns <= rows


def attend_kernel(place_ref, in_ref, out_ref, lse_ref, q_ref, k_ref, v_ref):
    for p in range(NB):
        block = in_ref[place_ref[p]]
        at = slice(p * ROWS, (p + 1) * ROWS)
        k_ref[at, :] = block[:ROWS, :HD]
        v_ref[at, :] = block[:ROWS, HD:]
        q_ref[at, :] = unfold(block[ROWS:])
    mask = diagonal_mask(TILE, False)
    for tile in range(LEN // TILE):
        at = slice(tile * TILE, (tile + 1) * TILE)
        seen = (tile + 1) * TILE
        scores = against(q_ref[at, :], k_ref[:seen, :]) * HD ** (-0.5)
        last = jnp.where(mask, scores[:, seen - TILE :], -jnp.inf)
        if tile:
            scores = jnp.concatenate([scores[:, : seen - TILE], last], axis=1)
        else:
            scores = last
        peak = jnp.max(scores, axis=-1, keepdims=True)
        terms = jnp.exp(scores - peak)
        total = jnp.sum(terms, axis=-1, keepdims=True)
        attend = (terms * (1.0 / total)).astype(BF)
        mixed = dot(attend, v_ref[:seen, :]).astype(BF)
        lse = peak + jnp.log(total)
        lse_ref[:, at] = jnp.transpose(jnp.broadcast_to(lse, (TILE, 128)))[:8, :]
        for part in range(TILE // ROWS):
            index = place_ref[tile * (TILE // ROWS) + part]
            out_ref[index] = fold(mixed[part * ROWS : (part + 1) * ROWS])


def attend_back_kernel(
    place_ref, in_ref, do_ref, lse_ref, out_ref, q_ref, k_ref, v_ref, g_ref, kt_ref, dq_ref, dk_ref, dv_ref
):
    for p in range(NB):
        block = in_ref[place_ref[p]]
        at = slice(p * ROWS, (p + 1) * ROWS)
        k_ref[at, :] = block[:ROWS, :HD]
        v_ref[at, :] = block[:ROWS, HD:]
        q_ref[at, :] = unfold(block[ROWS:])
        g_ref[at, :] = unfold(do_ref[place_ref[p]])
    kt_ref[...] = jnp.transpose(k_ref[...].astype(F32)).astype(BF)
    dk_ref[...] = jnp.zeros((LEN, HD), F32)
    dv_ref[...] = jnp.zeros((LEN, HD), F32)
    mask = diagonal_mask(TILE, True)
    for tile in range(LEN // TILE):
        at = slice(tile * TILE, (tile + 1) * TILE)
        seen = (tile + 1) * TILE
        query = q_ref[at, :]
        grad = g_ref[at, :]
        scores = against(k_ref[:seen, :], query) * HD ** (-0.5)
        last = jnp.where(mask, scores[seen - TILE :], -jnp.inf)
        if tile:
            scores = jnp.concatenate([scores[: seen - TILE], last], axis=0)
        else:
            scores = last
        full = jnp.exp(scores - lse_ref[0:1, at])
        attend_grad = against(v_ref[:seen, :], grad)
        inner = jnp.sum(full * attend_grad, axis=0, keepdims=True)
        score_grad = (full * (attend_grad - inner)).astype(BF)
        dv_ref[:seen, :] += dot(full.astype(BF), grad)
        dk_ref[:seen, :] += dot(score_grad, query)
        dq_ref[at, :] = jnp.transpose(dot(kt_ref[:, :seen], score_grad))
    for p in range(NB):
        index = place_ref[p]
        at = slice(p * ROWS, (p + 1) * ROWS)
        key_grad = (dk_ref[at, :] * HD ** (-0.5)).astype(BF)
        query_grad = (dq_ref[at, :] * HD ** (-0.5)).astype(BF)
        out_ref[index, 0:ROWS, :] = jnp.concatenate([key_grad, dv_ref[at, :].astype(BF)], axis=1)
        out_ref[index, ROWS:, :] = fold(query_grad)


def mix_kernel(layer, table_ref, in_ref, x_ref, *refs):
    blocks, (o_ref, x2_ref, h_ref, w_ref, gain_ref, sems) = by_block(refs), refs[10:]
    gain = load_blocks(table_ref, layer, blocks, w_ref, sems, gain_ref)
    mixed = jnp.concatenate([unfold(in_ref[index]) for index in range(H)], axis=1)
    o_ref[...] = mixed
    x2 = x_ref[...] + dot(mixed, w_ref[...])
    x2_ref[...] = x2
    h_ref[...] = (x2 * norm_factor(x2) * gain).astype(BF)


def mix_back_kernel(layer, table_ref, dy_ref, dh_ref, x2_ref, *refs):
    blocks, (dx2_ref, out_ref, gg_ref, w_ref, gain_ref, sems) = by_block(refs), refs[10:]
    gain = load_blocks(table_ref, layer, blocks, w_ref, sems, gain_ref)
    part, grad_gain = norm_backward(x2_ref[...], gain, dh_ref[...])
    dx2 = dy_ref[...] + part
    dx2_ref[...] = dx2
    gg_ref[...] = grad_gain
    low = dx2.astype(BF)
    mixed_grad = against(low, w_ref[...]).astype(BF)
    for index in range(H):
        out_ref[index] = fold(mixed_grad[:, index * HD : (index + 1) * HD])
    out_ref[NB - 1] = jnp.zeros((ROWS // 2, 2 * HD), BF)


def project_back_kernel(layer, table_ref, in_ref, dx2_ref, x_ref, cos_ref, sin_ref, gg_ref, *refs):
    blocks, parts, refs = by_block(refs), refs[11:19], refs[10:11] + refs[19:]
    dx_ref, held_ref, w_ref, gain_ref, sems = refs
    gain = load_blocks(table_ref, layer, blocks, w_ref, sems, gain_ref)
    cosine, sine = cos_ref[...], sin_ref[...]
    queries, keys, values = [], [], []
    for group in range(KV):
        pair = None
        for member in range(H // KV):
            index = group * (H // KV) + member
            own = in_ref[index, 0:ROWS, :].astype(F32)
            pair = own if pair is None else pair + own
            query = unfold(in_ref[index, ROWS:, :].astype(F32))
            queries.append(rotate_back(query, cosine, sine).astype(BF))
        keys.append(rotate_back(pair[:, :HD], cosine, sine).astype(BF))
        values.append(pair[:, HD:].astype(BF))
    lin_grad = jnp.concatenate(queries + keys + values, axis=1)
    part, grad_gain = norm_backward(x_ref[...], gain, against(lin_grad, w_ref[:, :QKV]))
    dx_ref[...] = dx2_ref[...] + part
    gains = jnp.concatenate([grad_gain, gg_ref[...], jnp.zeros((14, D), F32)], axis=0).astype(BF)
    low = dx2_ref[...].astype(BF)
    for index in range(8):
        at = slice(index * OUT_PART, (index + 1) * OUT_PART)
        lin = lin_grad[:, index * QKV_PART : (index + 1) * QKV_PART]
        held_ref[index, 0:ROWS, :] = jnp.concatenate(
            [
                lin,
                jnp.zeros((ROWS, OUT_AT - QKV_PART), BF),
                low[:, at],
                jnp.zeros((ROWS, ATT_WIDTH - OUT_AT - OUT_PART), BF),
            ],
            axis=1,
        )
        held_ref[index, ROWS:, 0:OUT_PART] = gains[:, at]
        held_ref[index, ROWS:, OUT_PART:] = jnp.zeros((16, ATT_WIDTH - OUT_PART), BF)
    for number in range(8):
        parts[number][...] = held_ref[4 * table_ref[2 * number] + table_ref[2 * number + 1]]


def feed_kernel(count, layer, table_ref, *refs):
    normed = jnp.concatenate([ref[...] for ref in refs[:count]], axis=0)
    refs = refs[count:]
    kept_ref, other_ref, lin_ref, hidden_ref = refs[8:12]
    wgu_ref, sems = refs[-2:]
    load_blocks(table_ref, layer, [refs[k : k + 1] for k in range(8)], wgu_ref, sems)
    lin = dot(normed, wgu_ref[...])
    lin_ref[...] = lin
    gate, up = lin[:, :UNITS], lin[:, UNITS:]
    hidden = (gate * jax.nn.sigmoid(gate) * up).astype(BF)
    hidden_ref[...] = hidden
    down = jnp.where(table_ref[0] == layer, kept_ref[...], other_ref[...])
    part = against(hidden, down).astype(BF)
    for index, ref in enumerate(refs[12:-2]):
        ref[...] = part[index * ROWS : (index + 1) * ROWS]


def feed_back_kernel(count, layer, table_ref, *refs):
    branch = jnp.concatenate([ref[...] for ref in refs[:count]], axis=0)
    refs = refs[count:]
    kept_ref, other_ref, lin_ref, grad_ref = refs[8:12]
    wgu_ref, sems = refs[-2:]
    load_blocks(table_ref, layer, [refs[k : k + 1] for k in range(8)], wgu_ref, sems)
    down = jnp.where(table_ref[0] == layer, kept_ref[...], other_ref[...])
    hidden_grad = dot(branch, down)
    gate, up = lin_ref[:, :UNITS], lin_ref[:, UNITS:]
    sig = jax.nn.sigmoid(gate)
    up_grad = hidden_grad * (gate * sig)
    gate_grad = hidden_grad * up * (sig + gate * sig * (1.0 - sig))
    lin_grad = jnp.concatenate([gate_grad, up_grad], axis=1).astype(BF)
    grad_ref[...] = lin_grad
    part = against(lin_grad, wgu_ref[...]).astype(BF)
    for index, ref in enumerate(refs[12:-2]):
        ref[...] = part[index * ROWS : (index + 1) * ROWS]


def feed_grads_kernel(*refs):
    normed = jnp.concatenate([ref[...] for ref in refs[:10]], axis=0)
    branch = jnp.concatenate([ref[...] for ref in refs[10:20]], axis=0)
    lin_grad = jnp.concatenate([ref[...] for ref in refs[20:23]], axis=0)
    hidden = jnp.concatenate([ref[...] for ref in refs[23:26]], axis=0)
    out_ref = refs[26]
    gate_up = across(normed, lin_grad).astype(BF)
    down = across(branch, hidden).astype(BF)
    for piece in range(NB - 1):
        rows = [
            gate_up[w * SHARE + piece * PIECE : w * SHARE + (piece + 1) * PIECE] for w in range(4)
        ]
        lower = down[4 * piece * PIECE : 4 * (piece + 1) * PIECE]
        out_ref[piece] = jnp.concatenate([jnp.concatenate(rows, axis=0), lower], axis=1)
    out_ref[NB - 1] = jnp.zeros((4 * PIECE, FF_WIDTH), BF)


def attend_grads_kernel(index_ref, *refs):
    found, parts, out_ref = by_block(refs), refs[10:18], refs[18]
    normed, mixed = [], []
    for block in found:
        if len(block) == 2:
            normed.append(block[0][...])
            mixed.append(block[1][...])
        else:
            normed.append(block[0][0:ROWS, :])
            mixed.append(block[0][ROWS:, :])
    normed, mixed = jnp.concatenate(normed, axis=0), jnp.concatenate(mixed, axis=0)
    lin_grad = jnp.concatenate([ref[0:ROWS, 0:OUT_AT] for ref in parts], axis=0)
    branch = jnp.concatenate([ref[0:ROWS, OUT_AT:] for ref in parts], axis=0)
    weight = across(normed, lin_grad).astype(BF)
    out_weight = across(mixed, branch).astype(BF)
    for piece in range(NB - 1):
        for w in range(4):
            at = w * SHARE + piece * PIECE
            to = slice(w * PIECE, (w + 1) * PIECE)
            out_ref[piece, to, 0:OUT_AT] = weight[at : at + PIECE]
            out_ref[piece, to, OUT_AT:] = out_weight[at : at + PIECE]
    gains = parts[0][ROWS:, 0:OUT_AT].astype(F32)
    for ref in parts[1:]:
        gains = gains + ref[ROWS:, 0:OUT_AT].astype(F32)
    out_ref[NB - 1] = jnp.zeros((4 * PIECE, ATT_WIDTH), BF)
    at = pl.multiple_of(index_ref[0] * PIECE, PIECE)
    out_ref[NB - 1, pl.ds(at, PIECE), 0:OUT_AT] = gains.astype(BF)


def finish_feed_kernel(in_ref, gate_ref, up_ref, down_ref):
    for piece in range(NB - 1):
        at = slice(piece * PIECE, (piece + 1) * PIECE)
        parts = []
        for w in range(4):
            for s in range(2):
                at_row = (4 * s + w) * PIECE
                parts.append(in_ref[piece, at_row : at_row + PIECE, :].astype(F32))
        gate_ref[at, :] = jnp.concatenate([part[:, :UNITS] for part in parts], axis=1)
        up_ref[at, :] = jnp.concatenate([part[:, UNITS:] for part in parts], axis=1)
        rows = in_ref[piece, 8 * PIECE :, :].astype(F32)
        to = slice(4 * piece * PIECE, 4 * (piece + 1) * PIECE)
        down_ref[to, :] = rows


def finish_attend_kernel(in_ref, q_ref, k_ref, v_ref, o_ref, gain_ref):
    keys, values = [], []
    for piece in range(NB - 1):
        at = slice(piece * PIECE, (piece + 1) * PIECE)
        parts = [in_ref[piece, t * PIECE : (t + 1) * PIECE, :].astype(F32) for t in range(8)]
        lin = jnp.concatenate([part[:, :QKV_PART] for part in parts], axis=1)
        q_ref[at, :] = lin[:, : H * HD]
        keys.append(lin[:, H * HD : (H + KV) * HD])
        values.append(lin[:, (H + KV) * HD :])
        o_ref[at, :] = jnp.concatenate(
            [part[:, OUT_AT : OUT_AT + OUT_PART] for part in parts], axis=1
        )
    k_ref[...] = jnp.transpose(jnp.concatenate(keys, axis=0))
    v_ref[...] = jnp.transpose(jnp.concatenate(values, axis=0))
    sides = []
    for side in range(2):
        total = None
        for w in range(4):
            t = 2 * w + side
            own = in_ref[NB - 1, t * PIECE : (t + 1) * PIECE, 0:OUT_PART].astype(F32)[:8]
            total = own if total is None else total + own
        sides.append(total)
    gain_ref[...] = jnp.concatenate(sides, axis=1)


def whole(shape):
    return pl.BlockSpec(shape, lambda i: (0,) * len(shape))


def layer_of(layer, shape):
    return pl.BlockSpec((None,) + shape, lambda i: (layer,) + (0,) * len(shape))


def call(kernel, in_specs, outs, args, scratch=()):
    return pl.pallas_call(
        kernel,
        grid=(1,),
        in_specs=in_specs,
        out_specs=[whole(shape) for shape, _ in outs],
        out_shape=[jax.ShapeDtypeStruct(shape, dtype) for shape, dtype in outs],
        scratch_shapes=list(scratch),
        compiler_params=pltpu.CompilerParams(vmem_limit_bytes=VMEM_BYTES),
        cost_estimate=pl.CostEstimate(flops=1, bytes_accessed=1, transcendentals=0),
    )(*args)


SMEM = pl.BlockSpec(memory_space=pltpu.SMEM)
HBM = pl.BlockSpec(memory_space=pl.ANY)
PACK = (NB, ROWS + ROWS // 2, 2 * HD)
HEADS = (NB, ROWS // 2, 2 * HD)
GROUPS = ((0,), (1, 3), (2,))


def exchange(array):
    return lax.all_to_all(array, "blk", 0, 0, tiled=True)


def sum_over_blocks(pieces):
    return jnp.sum(exchange(pieces).astype(F32), axis=0).astype(BF)


def weight_scratch(width):
    return [
        pltpu.VMEM((D, width), BF),
        pltpu.VMEM((4, 16, 256), BF),
        pltpu.SemaphoreType.DMA((3, 8)),
    ]


def body(
    tokens,
    cotangent,
    span_order,
    norm_one,
    w_query,
    w_key,
    w_value,
    w_out,
    norm_two,
    w_gate,
    w_up,
    w_down,
):
    section = lax.axis_index("section")
    shard = lax.axis_index("wshard")
    core = shard % 2
    y = 2 * (shard // 2) + section

    owners = []
    for step in range(4):
        there = (y + step) % 4
        for flip in range(2):
            owners += [there % 2, 2 * (there // 2) + (core ^ flip)]
    table = jnp.stack(owners).astype(jnp.int32)

    x0 = lax.dynamic_index_in_dim(tokens[:, 0], section, 0, keepdims=False).astype(F32)
    cot = lax.dynamic_index_in_dim(cotangent[:, 0], section, 0, keepdims=False).astype(F32)
    first, second = call(
        pack_attend_kernel,
        [
            whole((SHARE, D)),
            whole((KV * HD, SHARE)),
            whole((KV * HD, SHARE)),
            whole((SHARE, D)),
            whole((1, SHARE)),
            whole((1, SHARE)),
        ],
        [((SHARE + 16, WIDE), BF), ((SHARE + 16, D), BF)],
        (w_query[0], w_key[0].T, w_value[0].T, w_out[0], norm_one, norm_two),
    )
    *pieces, kept, sent = call(
        pack_feed_kernel,
        [SMEM, whole((SHARE, FF)), whole((SHARE, FF)), whole((D, FF // 4))],
        [((SHARE, 2 * UNITS), BF)] * 8 + [((D, UNITS), BF)] * 2,
        (table, w_gate[0], w_up[0], w_down[0].T),
        [pltpu.VMEM((8, SHARE, 2 * UNITS), BF)],
    )
    wqkv = sum(gather_eight(first), [])
    second, pieces, sent = after((second, pieces, sent), wqkv[4:6])
    wout_near = gather_near(second)
    wgu = exchange_eight(pieces)
    other = swap_section(sent)
    wout = sum(arranged(wout_near, gather_far(wout_near)), [])

    block_index = lax.axis_index("blk")
    own_block = lax.dynamic_index_in_dim(span_order, block_index, 0, keepdims=False)
    positions = own_block * ROWS + jnp.arange(ROWS, dtype=jnp.int32)
    exponent = jnp.arange(HD // 2, dtype=F32) * (2.0 / HD)
    angles = positions.astype(F32)[:, None] * (rope_base ** (-exponent))[None, :]
    angles = jnp.concatenate([angles, angles], axis=-1)
    cosine, sine = jnp.cos(angles), jnp.sin(angles)
    slots = jnp.arange(NB, dtype=jnp.int32)
    place = jnp.sum(
        jnp.where(span_order[None, :] == slots[:, None], slots[None, :], 0), axis=1
    ).astype(jnp.int32)

    angle = whole((ROWS, HD))
    rows = whole((ROWS, D))
    row_scratch = pltpu.VMEM((LEN, HD), BF)
    weights = [HBM] * 10
    half_down = whole((D, UNITS))
    feed_scratch = [pltpu.VMEM((D, 2 * UNITS), BF), pltpu.SemaphoreType.DMA((3, 8))]

    def row_specs(blocks):
        return [whole(block.shape) for block in blocks]

    def forward(layer, x, early, late):
        h1, packed = call(
            functools.partial(project_kernel, layer),
            [SMEM, rows, angle, angle] + weights,
            [((ROWS, D), BF), (PACK, BF)],
            (table, x, cosine, sine, *wqkv),
            weight_scratch(WIDE),
        )
        first = early(packed)
        packed, first = lax.optimization_barrier((exchange(packed), first))
        heads, lse = call(
            attend_kernel,
            [SMEM, whole(PACK)],
            [(HEADS, BF), ((8, LEN), F32)],
            (place, packed),
            [row_scratch] * 3,
        )
        heads = exchange(heads)
        heads, beside = lax.optimization_barrier((heads, late(first)))
        mixed, x2, h2 = call(
            functools.partial(mix_kernel, layer),
            [SMEM, whole(HEADS), rows] + weights,
            [((ROWS, D), BF), ((ROWS, D), F32), ((ROWS, D), BF)],
            (table, heads, x, *wout),
            weight_scratch(D),
        )
        found = gather_eight(h2)
        kept_ff, parts = [], [None] * 4
        for group in GROUPS:
            blocks = sum([found[step] for step in group], [])
            count = len(blocks)
            size = 2 * len(group)
            if kept_ff:
                blocks = after(blocks, kept_ff[-1][1])
            lin, hidden, *part = call(
                functools.partial(feed_kernel, count, layer),
                [SMEM] + row_specs(blocks) + [HBM] * 8 + [half_down, half_down],
                [((size * ROWS, 2 * UNITS), F32), ((size * ROWS, UNITS), BF)]
                + [((ROWS, D), BF)] * size,
                (table, *blocks, *wgu, kept, other),
                feed_scratch,
            )
            kept_ff.append((blocks, lin, hidden))
            for number, step in enumerate(group):
                parts[step] = part[2 * number : 2 * number + 2]
        both = jnp.concatenate([h1, mixed], axis=0)
        return parts, beside, (x, both, packed, lse, x2, kept_ff)

    def backward(layer, dy, found, kept_state, early, late):
        x, _, packed, lse, x2, kept_ff = kept_state
        parts, branches, lin_grads = [None] * 4, [], []
        for group, (_, lin, _) in zip(GROUPS, kept_ff):
            blocks = sum([found[step] for step in group], [])
            count = len(blocks)
            size = 2 * len(group)
            if lin_grads:
                blocks = after(blocks, lin_grads[-1])
            lin_grad, *part = call(
                functools.partial(feed_back_kernel, count, layer),
                [SMEM]
                + row_specs(blocks)
                + [HBM] * 8
                + [half_down, half_down]
                + [whole((size * ROWS, 2 * UNITS))],
                [((size * ROWS, 2 * UNITS), BF)] + [((ROWS, D), BF)] * size,
                (table, *blocks, *wgu, kept, other, lin),
                feed_scratch,
            )
            branches += blocks
            lin_grads.append(lin_grad)
            for number, step in enumerate(group):
                parts[step] = part[2 * number : 2 * number + 2]
        dh2 = scatter_eight(parts)
        normed = sum([item[0] for item in kept_ff], [])
        sizes = [len(group) * 2 * ROWS for group in GROUPS]
        lin_grads[0] = after(lin_grads[0], parts[2])
        grad_ff = call(
            feed_grads_kernel,
            row_specs(normed + branches)
            + [whole((size, 2 * UNITS)) for size in sizes]
            + [whole((size, UNITS)) for size in sizes],
            [((NB, 4 * PIECE, FF_WIDTH), BF)],
            (*normed, *branches, *lin_grads, *[item[2] for item in kept_ff]),
        )[0]
        dx2, heads_grad, grad_gain_two = call(
            functools.partial(mix_back_kernel, layer),
            [SMEM, rows, rows, rows] + weights,
            [((ROWS, D), F32), (HEADS, BF), ((1, D), F32)],
            (table, dy, dh2, x2, *wout),
            weight_scratch(D),
        )
        first = early(dx2)
        heads_grad, first = lax.optimization_barrier((exchange(heads_grad), first))
        packed_grad = call(
            attend_back_kernel,
            [SMEM, whole(PACK), whole(HEADS), whole((8, LEN))],
            [(PACK, BF)],
            (place, packed, heads_grad, lse),
            [row_scratch] * 4
            + [pltpu.VMEM((HD, LEN), BF)]
            + [pltpu.VMEM((LEN, HD), F32)] * 3,
        )[0]
        packed_grad, second = lax.optimization_barrier((exchange(packed_grad), late(first)))
        dx, *lin_parts = call(
            functools.partial(project_back_kernel, layer),
            [SMEM, whole(PACK), rows, rows, angle, angle, whole((1, D))] + weights,
            [((ROWS, D), F32)] + [((ROWS + 16, ATT_WIDTH), BF)] * 8,
            (table, packed_grad, dx2, x, cosine, sine, grad_gain_two, *wqkv),
            [pltpu.VMEM((8, ROWS + 16, ATT_WIDTH), BF)] + weight_scratch(WIDE),
        )
        return dx, lin_parts, grad_ff, second

    def attend_grads(blocks, lin_all):
        return call(
            attend_grads_kernel,
            [SMEM] + row_specs(blocks) + [whole((ROWS + 16, ATT_WIDTH))] * 8,
            [((NB, 4 * PIECE, ATT_WIDTH), BF)],
            (gain_owner, *blocks, *lin_all),
        )[0]

    def sum_feed(pieces):
        flat = pieces.reshape(NB * 4 * PIECE, FF_WIDTH)
        return lax.psum_scatter(flat, "blk", scatter_dimension=0, tiled=True)

    def by_section(of_first, of_second):
        own = jnp.where(section == 0, of_first, of_second)
        other = swap_section(jnp.where(section == 0, of_second, of_first))
        return jnp.where(section == 0, jnp.stack([own, other]), jnp.stack([other, own]))

    gain_owner = ((4 * section + shard) // 2).astype(jnp.int32).reshape(1)
    parts, (wout, wgu, other), kept0 = forward(
        0, x0, lambda packed: (wout_near, wgu[1:3], wgu[6]), lambda first: (wout, wgu, other)
    )
    y0 = (kept0[4] + scatter_eight(parts)).astype(BF)
    cot_low = cot.astype(BF)
    parts1, (found_cot, both0), kept1 = forward(
        1,
        y0.astype(F32),
        lambda packed: (gather_near(after(cot_low, packed)), gather_near(after(kept0[1], packed))),
        lambda near: tuple(arranged(item, gather_far(item)) for item in near),
    )
    dx1, lin1, grad_ff1, (both1, y1) = backward(
        1,
        cot,
        found_cot,
        kept1,
        lambda dx2: (gather_near(after(kept1[1], dx2)), dx2),
        lambda first: (
            arranged(first[0], gather_far(first[0])),
            kept1[4] + scatter_eight(after(parts1, first[1])),
        ),
    )
    y1 = y1.astype(BF)
    dy0 = dx1.astype(BF)
    ff1 = sum_feed(after(grad_ff1, dx1))
    dx0, lin0, grad_ff0, (lin1, layer_outputs) = backward(
        0,
        dy0.astype(F32),
        gather_eight(dy0),
        kept0,
        lambda dx2: exchange_eight(after(lin1, dx2)),
        lambda first: (first, by_section(y0, after(y1, first[1]))),
    )
    ff0 = sum_feed(grad_ff0)
    upper = 2 * UNITS
    spread = jnp.stack([ff0[:, :upper], ff1[:, :upper]]).reshape(8, PIECE, upper)
    spread = lax.all_to_all(spread, EIGHT, 0, 0, tiled=True).reshape(8 * PIECE, upper)
    lower = by_section(ff0[:, upper:], ff1[:, upper:])
    lower = jnp.concatenate([lower[0], lower[1]], axis=1)
    found = lax.all_gather(jnp.concatenate([spread, lower], axis=0), "blk", axis=0)
    att1 = sum_over_blocks(attend_grads(sum(both1, []), lin1))
    att0 = attend_grads(sum(both0, []), exchange_eight(lin0))
    input_grads = by_section(dx0, dx1)
    att0 = sum_over_blocks(att0)
    grad_gate, grad_up, grad_down = call(
        finish_feed_kernel,
        [whole(found.shape)],
        [((SHARE, FF), F32), ((SHARE, FF), F32), ((D, FF // 4), F32)],
        (found,),
    )
    spread = jnp.stack([att0, att1]).reshape(8, PIECE, ATT_WIDTH)
    spread = lax.all_to_all(spread, EIGHT, 0, 0, tiled=True).reshape(1, 8 * PIECE, ATT_WIDTH)
    found = exchange(jnp.broadcast_to(spread, (NB, 8 * PIECE, ATT_WIDTH)))
    grad_query, grad_key, grad_value, grad_out, gain_grads = call(
        finish_attend_kernel,
        [whole(found.shape)],
        [
            ((SHARE, H * HD), F32),
            ((KV * HD, SHARE), F32),
            ((KV * HD, SHARE), F32),
            ((SHARE, D), F32),
            ((8, SHARE), F32),
        ],
        (found,),
    )
    return (
        layer_outputs[None, :, None],
        input_grads[None, :, None],
        gain_grads[0][None],
        grad_query[None],
        grad_key.T[None],
        grad_value.T[None],
        grad_out[None],
        gain_grads[1][None],
        grad_gate[None],
        grad_up[None],
        grad_down.T[None],
    )


def solution(mesh):
    return jax.shard_map(
        body,
        mesh=mesh,
        in_specs=(
            P(None, "wshard", "blk", None),
            P(None, "wshard", "blk", None),
            P(),
            P("section", "wshard"),
            P("section", "wshard", None),
            P("section", "wshard", None),
            P("section", "wshard", None),
            P("section", "wshard", None),
            P("section", "wshard"),
            P("section", "wshard", None),
            P("section", "wshard", None),
            P("section", "wshard", None),
        ),
        out_specs=(
            P("section", None, "wshard", "blk", None),
            P("section", None, "wshard", "blk", None),
            P("section", "wshard"),
            P("section", "wshard", None),
            P("section", "wshard", None),
            P("section", "wshard", None),
            P("section", "wshard", None),
            P("section", "wshard"),
            P("section", "wshard", None),
            P("section", "wshard", None),
            P("section", "wshard", None),
        ),
        check_vma=False,
    )
```

```python
import functools

import jax
import jax.numpy as jnp
from jax import lax
from jax.experimental import pallas as pl
from jax.experimental.pallas import tpu as pltpu
from jax.sharding import PartitionSpec as P

D = 960
H = 15
KV = 5
HD = 64
FF = 2560
ROWS = 128
NB = 16
LEN = ROWS * NB
QKV = H * HD + 2 * KV * HD
UNITS = FF // 8
WIDE = 1664
SHARE = D // 4
PIECE = 16
QKV_PART = QKV // 8
OUT_PART = D // 8
OUT_AT = 256
ATT_WIDTH = 384
FF_WIDTH = D
TILE = 256

EIGHT = ("section", "wshard")
eps_norm = 1e-05
rope_base = 10000.0
BF = jnp.bfloat16
F32 = jnp.float32
VMEM_BYTES = 56 * 1024 * 1024


def place_of(y, core):
    return (y % 2) * 4 + (y // 2) * 2 + core


def ring_pairs(step, flip):
    return [
        (place_of(y, c), place_of((y + step) % 4, c ^ flip)) for y in range(4) for c in range(2)
    ]


def hop(array, step, flip=0):
    return lax.ppermute(array, EIGHT, ring_pairs(step, flip))


def swap_section(array):
    return lax.ppermute(array, "section", [(0, 1), (1, 0)])


def after(values, *others):
    return lax.optimization_barrier((values, others))[0]


def gather_near(block):
    before = hop(block, 1)
    after_it = hop(block, -1)
    return block, hop(block, 0, 1), after_it, before


def gather_far(near):
    half = near[0].shape[0] // 2
    low, high = hop(near[3][:half], 1), hop(near[2][half:], -1)
    beside = [hop(near[2], 0, 1), hop(near[3], 0, 1)]
    return low, high, hop(low, 0, 1), hop(high, 0, 1), *beside


def arranged(near, far):
    return [[near[0], near[1]], [near[2], far[4]], list(far[:4]), [near[3], far[5]]]


def gather_eight(block):
    near = gather_near(block)
    return arranged(near, gather_far(near))


def exchange_eight(parts):
    found = [parts[0]] + [None] * 7
    for step, flip in ((0, 1), (1, 0), (3, 0), (1, 1), (3, 1)):
        found[2 * ((4 - step) % 4) + flip] = hop(parts[2 * step + flip], step, flip)
    found[4] = hop(hop(parts[4], 1), 1)
    found[5] = hop(hop(parts[5], -1), -1, 1)
    return found


def scatter_eight(parts):
    half = parts[0][0].shape[0] // 2
    total = [None] * 4
    for step in (2, 1, 3, 0):
        total[step] = parts[step][0].astype(F32) + hop(parts[step][1], 0, 1).astype(F32)
    far = total[2].astype(BF)
    low = hop(far[:half], 1).astype(F32)
    high = hop(far[half:], -1).astype(F32)
    forth = jnp.concatenate([total[1][:half] + low, total[1][half:]], axis=0).astype(BF)
    back = jnp.concatenate([total[3][:half], total[3][half:] + high], axis=0).astype(BF)
    return total[0] + hop(forth, 1).astype(F32) + hop(back, -1).astype(F32)


def norm_factor(values):
    return lax.rsqrt(jnp.mean(values * values, axis=-1, keepdims=True) + eps_norm)


def norm_backward(values, gain, grad):
    factor = norm_factor(values)
    scaled = grad * gain
    inner = jnp.mean(values * scaled, axis=-1, keepdims=True)
    grad_values = factor * scaled - values * (factor * factor * factor * inner)
    grad_gain = jnp.sum(grad * values * factor, axis=0, keepdims=True)
    return grad_values, grad_gain


def dot(left, right):
    return jnp.dot(left, right, preferred_element_type=F32)


def against(left, right):
    return lax.dot_general(left, right, (((1,), (1,)), ((), ())), preferred_element_type=F32)


def across(left, right):
    return lax.dot_general(left, right, (((0,), (0,)), ((), ())), preferred_element_type=F32)


def rotate(values, cosine, sine):
    half = HD // 2
    turned = jnp.concatenate([-values[:, half:], values[:, :half]], axis=1)
    return values * cosine + turned * sine


def rotate_back(grad, cosine, sine):
    half = HD // 2
    part = grad * sine
    return grad * cosine + jnp.concatenate([part[:, half:], -part[:, :half]], axis=1)


def fold(rows):
    half = rows.shape[0] // 2
    return jnp.concatenate([rows[:half], rows[half:]], axis=1)


def unfold(block):
    return jnp.concatenate([block[:, :HD], block[:, HD:]], axis=0)


def pack_attend_kernel(q_ref, k_ref, v_ref, o_ref, one_ref, two_ref, first_ref, second_ref):
    gap = jnp.zeros((SHARE, WIDE - QKV), BF)
    keys, values = jnp.transpose(k_ref[...]), jnp.transpose(v_ref[...])
    first_ref[0:SHARE, :] = jnp.concatenate([q_ref[...], keys, values, gap], axis=1)
    second_ref[0:SHARE, :] = o_ref[...]
    for ref, gain in ((first_ref, one_ref), (second_ref, two_ref)):
        row = jnp.concatenate([gain[...], jnp.zeros((15, SHARE), BF)], axis=0)
        width = ref.shape[1]
        ref[SHARE:, :] = jnp.concatenate([row, jnp.zeros((16, width - SHARE), BF)], axis=1)


def pack_feed_kernel(table_ref, gate_ref, up_ref, down_ref, *refs):
    pieces, (kept_ref, sent_ref, held_ref) = refs[:8], refs[8:]
    for s in range(2):
        for w in range(4):
            at = 2 * w + s
            at = slice(at * UNITS, (at + 1) * UNITS)
            held_ref[4 * s + w] = jnp.concatenate([gate_ref[:, at], up_ref[:, at]], axis=1)
    for number in range(8):
        pieces[number][...] = held_ref[4 * table_ref[2 * number] + table_ref[2 * number + 1]]
    first, second = down_ref[:, :UNITS], down_ref[:, UNITS:]
    gap = jnp.zeros((D, 384 - UNITS), BF)

    @pl.when(table_ref[0] == 0)
    def _():
        kept_ref[...] = jnp.concatenate([first, gap], axis=1)
        sent_ref[...] = jnp.concatenate([second, gap], axis=1)

    @pl.when(table_ref[0] == 1)
    def _():
        kept_ref[...] = jnp.concatenate([second, gap], axis=1)
        sent_ref[...] = jnp.concatenate([first, gap], axis=1)


def load_blocks(table_ref, layer, blocks, weight_ref, sems, gain_ref=None):
    def copies(number):
        place = table_ref[2 * number + 1]
        done = 0
        for part, block in enumerate(blocks[number]):
            rows = min(block.shape[0], SHARE - done)
            yield pltpu.make_async_copy(
                block.at[pl.ds(0, rows)],
                weight_ref.at[pl.ds(pl.multiple_of(place * SHARE + done, 16), rows)],
                sems.at[part, number],
            )
            done += rows
        if gain_ref is not None:
            last = block.shape[0] - 16
            yield pltpu.make_async_copy(
                block.at[pl.ds(last, 16), pl.ds(0, 256)], gain_ref.at[place], sems.at[2, number]
            )

    for number in range(8):

        @pl.when(table_ref[2 * number] == layer)
        def _():
            for copy in copies(number):
                copy.start()

    for number in range(8):

        @pl.when(table_ref[2 * number] == layer)
        def _():
            for copy in copies(number):
                copy.wait()

    if gain_ref is not None:
        return jnp.concatenate([gain_ref[w, 0:1, :SHARE] for w in range(4)], axis=1).astype(F32)


def by_block(refs):
    return [refs[0:1], refs[1:2], refs[2:3], refs[3:4], refs[4:6], refs[6:8], refs[8:9], refs[9:10]]


def project_kernel(layer, table_ref, x_ref, cos_ref, sin_ref, *refs):
    blocks, (h_ref, out_ref, w_ref, gain_ref, sems) = by_block(refs), refs[10:]
    gain = load_blocks(table_ref, layer, blocks, w_ref, sems, gain_ref)
    x = x_ref[...]
    h = (x * norm_factor(x) * gain).astype(BF)
    h_ref[...] = h
    cosine, sine = cos_ref[...], sin_ref[...]
    lin = dot(h, w_ref[:, :QKV])

    def head(at):
        return lin[:, at * HD : (at + 1) * HD]

    for group in range(KV):
        key = rotate(head(H + group), cosine, sine).astype(BF)
        pair = jnp.concatenate([key, head(H + KV + group).astype(BF)], axis=1)
        for member in range(H // KV):
            index = group * (H // KV) + member
            out_ref[index, 0:ROWS, :] = pair
            query = rotate(head(index), cosine, sine).astype(BF)
            out_ref[index, ROWS:, :] = fold(query)
    out_ref[NB - 1] = jnp.zeros((ROWS + ROWS // 2, 2 * HD), BF)


def diagonal_mask(size, keys_first):
    rows = lax.broadcasted_iota(jnp.int32, (size, size), 0)
    columns = lax.broadcasted_iota(jnp.int32, (size, size), 1)
    return rows <= columns if keys_first else columns <= rows


def attend_kernel(place_ref, in_ref, out_ref, lse_ref, q_ref, k_ref, v_ref):
    for p in range(NB):
        block = in_ref[place_ref[p]]
        at = slice(p * ROWS, (p + 1) * ROWS)
        k_ref[at, :] = block[:ROWS, :HD]
        v_ref[at, :] = block[:ROWS, HD:]
        q_ref[at, :] = unfold(block[ROWS:])
    mask = diagonal_mask(TILE, False)
    for tile in range(LEN // TILE):
        at = slice(tile * TILE, (tile + 1) * TILE)
        seen = (tile + 1) * TILE
        scores = against(q_ref[at, :], k_ref[:seen, :]) * HD ** (-0.5)
        last = jnp.where(mask, scores[:, seen - TILE :], -jnp.inf)
        if tile:
            scores = jnp.concatenate([scores[:, : seen - TILE], last], axis=1)
        else:
            scores = last
        peak = jnp.max(scores, axis=-1, keepdims=True)
        terms = jnp.exp(scores - peak)
        total = jnp.sum(terms, axis=-1, keepdims=True)
        attend = (terms * (1.0 / total)).astype(BF)
        mixed = dot(attend, v_ref[:seen, :]).astype(BF)
        lse = peak + jnp.log(total)
        lse_ref[:, at] = jnp.transpose(jnp.broadcast_to(lse, (TILE, 128)))[:8, :]
        for part in range(TILE // ROWS):
            index = place_ref[tile * (TILE // ROWS) + part]
            out_ref[index] = fold(mixed[part * ROWS : (part + 1) * ROWS])


def attend_back_kernel(
    place_ref, in_ref, do_ref, lse_ref, out_ref, q_ref, k_ref, v_ref, g_ref, kt_ref, dq_ref, dk_ref, dv_ref
):
    for p in range(NB):
        block = in_ref[place_ref[p]]
        at = slice(p * ROWS, (p + 1) * ROWS)
        k_ref[at, :] = block[:ROWS, :HD]
        v_ref[at, :] = block[:ROWS, HD:]
        q_ref[at, :] = unfold(block[ROWS:])
        g_ref[at, :] = unfold(do_ref[place_ref[p]])
    kt_ref[...] = jnp.transpose(k_ref[...].astype(F32)).astype(BF)
    dk_ref[...] = jnp.zeros((LEN, HD), F32)
    dv_ref[...] = jnp.zeros((LEN, HD), F32)
    mask = diagonal_mask(TILE, True)
    for tile in range(LEN // TILE):
        at = slice(tile * TILE, (tile + 1) * TILE)
        seen = (tile + 1) * TILE
        query = q_ref[at, :]
        grad = g_ref[at, :]
        scores = against(k_ref[:seen, :], query) * HD ** (-0.5)
        last = jnp.where(mask, scores[seen - TILE :], -jnp.inf)
        if tile:
            scores = jnp.concatenate([scores[: seen - TILE], last], axis=0)
        else:
            scores = last
        full = jnp.exp(scores - lse_ref[0:1, at])
        attend_grad = against(v_ref[:seen, :], grad)
        inner = jnp.sum(full * attend_grad, axis=0, keepdims=True)
        score_grad = (full * (attend_grad - inner)).astype(BF)
        dv_ref[:seen, :] += dot(full.astype(BF), grad)
        dk_ref[:seen, :] += dot(score_grad, query)
        dq_ref[at, :] = jnp.transpose(dot(kt_ref[:, :seen], score_grad))
    for p in range(NB):
        index = place_ref[p]
        at = slice(p * ROWS, (p + 1) * ROWS)
        key_grad = (dk_ref[at, :] * HD ** (-0.5)).astype(BF)
        query_grad = (dq_ref[at, :] * HD ** (-0.5)).astype(BF)
        out_ref[index, 0:ROWS, :] = jnp.concatenate([key_grad, dv_ref[at, :].astype(BF)], axis=1)
        out_ref[index, ROWS:, :] = fold(query_grad)


def mix_kernel(layer, table_ref, in_ref, x_ref, *refs):
    blocks, (o_ref, x2_ref, h_ref, w_ref, gain_ref, sems) = by_block(refs), refs[10:]
    gain = load_blocks(table_ref, layer, blocks, w_ref, sems, gain_ref)
    mixed = jnp.concatenate([unfold(in_ref[index]) for index in range(H)], axis=1)
    o_ref[...] = mixed
    x2 = x_ref[...] + dot(mixed, w_ref[...])
    x2_ref[...] = x2
    h_ref[...] = (x2 * norm_factor(x2) * gain).astype(BF)


def mix_back_kernel(layer, table_ref, dy_ref, dh_ref, x2_ref, *refs):
    blocks, (dx2_ref, out_ref, gg_ref, w_ref, gain_ref, sems) = by_block(refs), refs[10:]
    gain = load_blocks(table_ref, layer, blocks, w_ref, sems, gain_ref)
    part, grad_gain = norm_backward(x2_ref[...], gain, dh_ref[...])
    dx2 = dy_ref[...] + part
    dx2_ref[...] = dx2
    gg_ref[...] = grad_gain
    low = dx2.astype(BF)
    mixed_grad = against(low, w_ref[...]).astype(BF)
    for index in range(H):
        out_ref[index] = fold(mixed_grad[:, index * HD : (index + 1) * HD])
    out_ref[NB - 1] = jnp.zeros((ROWS // 2, 2 * HD), BF)


def project_back_kernel(layer, table_ref, in_ref, dx2_ref, x_ref, cos_ref, sin_ref, gg_ref, *refs):
    blocks, parts, refs = by_block(refs), refs[11:19], refs[10:11] + refs[19:]
    dx_ref, held_ref, w_ref, gain_ref, sems = refs
    gain = load_blocks(table_ref, layer, blocks, w_ref, sems, gain_ref)
    cosine, sine = cos_ref[...], sin_ref[...]
    queries, keys, values = [], [], []
    for group in range(KV):
        pair = None
        for member in range(H // KV):
            index = group * (H // KV) + member
            own = in_ref[index, 0:ROWS, :].astype(F32)
            pair = own if pair is None else pair + own
            query = unfold(in_ref[index, ROWS:, :].astype(F32))
            queries.append(rotate_back(query, cosine, sine).astype(BF))
        keys.append(rotate_back(pair[:, :HD], cosine, sine).astype(BF))
        values.append(pair[:, HD:].astype(BF))
    lin_grad = jnp.concatenate(queries + keys + values, axis=1)
    part, grad_gain = norm_backward(x_ref[...], gain, against(lin_grad, w_ref[:, :QKV]))
    dx_ref[...] = dx2_ref[...] + part
    gains = jnp.concatenate([grad_gain, gg_ref[...], jnp.zeros((14, D), F32)], axis=0).astype(BF)
    low = dx2_ref[...].astype(BF)
    for index in range(8):
        at = slice(index * OUT_PART, (index + 1) * OUT_PART)
        lin = lin_grad[:, index * QKV_PART : (index + 1) * QKV_PART]
        held_ref[index, 0:ROWS, :] = jnp.concatenate(
            [
                lin,
                jnp.zeros((ROWS, OUT_AT - QKV_PART), BF),
                low[:, at],
                jnp.zeros((ROWS, ATT_WIDTH - OUT_AT - OUT_PART), BF),
            ],
            axis=1,
        )
        held_ref[index, ROWS:, 0:OUT_PART] = gains[:, at]
        held_ref[index, ROWS:, OUT_PART:] = jnp.zeros((16, ATT_WIDTH - OUT_PART), BF)
    for number in range(8):
        parts[number][...] = held_ref[4 * table_ref[2 * number] + table_ref[2 * number + 1]]


def feed_kernel(count, layer, table_ref, *refs):
    normed = jnp.concatenate([ref[...] for ref in refs[:count]], axis=0)
    refs = refs[count:]
    kept_ref, other_ref, lin_ref, hidden_ref = refs[8:12]
    wgu_ref, sems = refs[-2:]
    load_blocks(table_ref, layer, [refs[k : k + 1] for k in range(8)], wgu_ref, sems)
    lin = dot(normed, wgu_ref[...])
    lin_ref[...] = lin
    gate, up = lin[:, :UNITS], lin[:, UNITS:]
    hidden = (gate * jax.nn.sigmoid(gate) * up).astype(BF)
    hidden_ref[...] = hidden
    down = jnp.where(table_ref[0] == layer, kept_ref[:, :UNITS], other_ref[:, :UNITS])
    part = against(hidden, down).astype(BF)
    for index, ref in enumerate(refs[12:-2]):
        ref[...] = part[index * ROWS : (index + 1) * ROWS]


def feed_back_kernel(count, layer, table_ref, *refs):
    branch = jnp.concatenate([ref[...] for ref in refs[:count]], axis=0)
    refs = refs[count:]
    kept_ref, other_ref, lin_ref, grad_ref = refs[8:12]
    wgu_ref, sems = refs[-2:]
    load_blocks(table_ref, layer, [refs[k : k + 1] for k in range(8)], wgu_ref, sems)
    down = jnp.where(table_ref[0] == layer, kept_ref[:, :UNITS], other_ref[:, :UNITS])
    hidden_grad = dot(branch, down)
    gate, up = lin_ref[:, :UNITS], lin_ref[:, UNITS:]
    sig = jax.nn.sigmoid(gate)
    up_grad = hidden_grad * (gate * sig)
    gate_grad = hidden_grad * up * (sig + gate * sig * (1.0 - sig))
    lin_grad = jnp.concatenate([gate_grad, up_grad], axis=1).astype(BF)
    grad_ref[...] = lin_grad
    part = against(lin_grad, wgu_ref[...]).astype(BF)
    for index, ref in enumerate(refs[12:-2]):
        ref[...] = part[index * ROWS : (index + 1) * ROWS]


def feed_grads_kernel(*refs):
    normed = jnp.concatenate([ref[...] for ref in refs[:10]], axis=0)
    branch = jnp.concatenate([ref[...] for ref in refs[10:20]], axis=0)
    lin_grad, hidden = refs[20][...], refs[21][...]
    out_ref = refs[22]
    gate_up = across(normed, lin_grad).astype(BF)
    down = across(branch, hidden).astype(BF)
    for piece in range(NB - 1):
        rows = [
            gate_up[w * SHARE + piece * PIECE : w * SHARE + (piece + 1) * PIECE] for w in range(4)
        ]
        lower = down[4 * piece * PIECE : 4 * (piece + 1) * PIECE]
        out_ref[piece] = jnp.concatenate([jnp.concatenate(rows, axis=0), lower], axis=1)
    out_ref[NB - 1] = jnp.zeros((4 * PIECE, FF_WIDTH), BF)


def attend_grads_kernel(index_ref, *refs):
    found, parts, out_ref = by_block(refs), refs[10:18], refs[18]
    normed, mixed = [], []
    for block in found:
        if len(block) == 2:
            normed.append(block[0][...])
            mixed.append(block[1][...])
        else:
            normed.append(block[0][0:ROWS, :])
            mixed.append(block[0][ROWS:, :])
    normed, mixed = jnp.concatenate(normed, axis=0), jnp.concatenate(mixed, axis=0)
    lin_grad = jnp.concatenate([ref[0:ROWS, 0:OUT_AT] for ref in parts], axis=0)
    branch = jnp.concatenate([ref[0:ROWS, OUT_AT:] for ref in parts], axis=0)
    weight = across(normed, lin_grad).astype(BF)
    out_weight = across(mixed, branch).astype(BF)
    for piece in range(NB - 1):
        for w in range(4):
            at = w * SHARE + piece * PIECE
            to = slice(w * PIECE, (w + 1) * PIECE)
            out_ref[piece, to, 0:OUT_AT] = weight[at : at + PIECE]
            out_ref[piece, to, OUT_AT:] = out_weight[at : at + PIECE]
    gains = parts[0][ROWS:, 0:OUT_AT].astype(F32)
    for ref in parts[1:]:
        gains = gains + ref[ROWS:, 0:OUT_AT].astype(F32)
    out_ref[NB - 1] = jnp.zeros((4 * PIECE, ATT_WIDTH), BF)
    at = pl.multiple_of(index_ref[0] * PIECE, PIECE)
    out_ref[NB - 1, pl.ds(at, PIECE), 0:OUT_AT] = gains.astype(BF)


def finish_feed_kernel(in_ref, gate_ref, up_ref, down_ref):
    for piece in range(NB - 1):
        at = slice(piece * PIECE, (piece + 1) * PIECE)
        parts = []
        for w in range(4):
            for s in range(2):
                at_row = (4 * s + w) * PIECE
                parts.append(in_ref[piece, at_row : at_row + PIECE, :].astype(F32))
        gate_ref[at, :] = jnp.concatenate([part[:, :UNITS] for part in parts], axis=1)
        up_ref[at, :] = jnp.concatenate([part[:, UNITS:] for part in parts], axis=1)
        rows = in_ref[piece, 8 * PIECE :, :].astype(F32)
        to = slice(4 * piece * PIECE, 4 * (piece + 1) * PIECE)
        down_ref[to, :] = rows


def finish_attend_kernel(in_ref, q_ref, k_ref, v_ref, o_ref, gain_ref):
    keys, values = [], []
    for piece in range(NB - 1):
        at = slice(piece * PIECE, (piece + 1) * PIECE)
        parts = [in_ref[piece, t * PIECE : (t + 1) * PIECE, :].astype(F32) for t in range(8)]
        lin = jnp.concatenate([part[:, :QKV_PART] for part in parts], axis=1)
        q_ref[at, :] = lin[:, : H * HD]
        keys.append(lin[:, H * HD : (H + KV) * HD])
        values.append(lin[:, (H + KV) * HD :])
        o_ref[at, :] = jnp.concatenate(
            [part[:, OUT_AT : OUT_AT + OUT_PART] for part in parts], axis=1
        )
    k_ref[...] = jnp.transpose(jnp.concatenate(keys, axis=0))
    v_ref[...] = jnp.transpose(jnp.concatenate(values, axis=0))
    sides = []
    for side in range(2):
        total = None
        for w in range(4):
            t = 2 * w + side
            own = in_ref[NB - 1, t * PIECE : (t + 1) * PIECE, 0:OUT_PART].astype(F32)[:8]
            total = own if total is None else total + own
        sides.append(total)
    gain_ref[...] = jnp.concatenate(sides, axis=1)


def whole(shape):
    return pl.BlockSpec(shape, lambda i: (0,) * len(shape))


def layer_of(layer, shape):
    return pl.BlockSpec((None,) + shape, lambda i: (layer,) + (0,) * len(shape))


def call(kernel, in_specs, outs, args, scratch=()):
    return pl.pallas_call(
        kernel,
        grid=(1,),
        in_specs=in_specs,
        out_specs=[whole(shape) for shape, _ in outs],
        out_shape=[jax.ShapeDtypeStruct(shape, dtype) for shape, dtype in outs],
        scratch_shapes=list(scratch),
        compiler_params=pltpu.CompilerParams(vmem_limit_bytes=VMEM_BYTES),
        cost_estimate=pl.CostEstimate(flops=1, bytes_accessed=1, transcendentals=0),
    )(*args)


SMEM = pl.BlockSpec(memory_space=pltpu.SMEM)
HBM = pl.BlockSpec(memory_space=pl.ANY)
PACK = (NB, ROWS + ROWS // 2, 2 * HD)
HEADS = (NB, ROWS // 2, 2 * HD)
GROUPS = ((0, 1, 2, 3),)


def exchange(array):
    return lax.all_to_all(array, "blk", 0, 0, tiled=True)


def sum_over_blocks(pieces):
    return jnp.sum(exchange(pieces).astype(F32), axis=0).astype(BF)


def weight_scratch(width):
    return [
        pltpu.VMEM((D, width), BF),
        pltpu.VMEM((4, 16, 256), BF),
        pltpu.SemaphoreType.DMA((3, 8)),
    ]


def body(
    tokens,
    cotangent,
    span_order,
    norm_one,
    w_query,
    w_key,
    w_value,
    w_out,
    norm_two,
    w_gate,
    w_up,
    w_down,
):
    section = lax.axis_index("section")
    shard = lax.axis_index("wshard")
    core = shard % 2
    y = 2 * (shard // 2) + section

    owners = []
    for step in range(4):
        there = (y + step) % 4
        for flip in range(2):
            owners += [there % 2, 2 * (there // 2) + (core ^ flip)]
    table = jnp.stack(owners).astype(jnp.int32)

    x0 = lax.dynamic_index_in_dim(tokens[:, 0], section, 0, keepdims=False).astype(F32)
    cot = lax.dynamic_index_in_dim(cotangent[:, 0], section, 0, keepdims=False).astype(F32)
    first, second = call(
        pack_attend_kernel,
        [
            whole((SHARE, D)),
            whole((KV * HD, SHARE)),
            whole((KV * HD, SHARE)),
            whole((SHARE, D)),
            whole((1, SHARE)),
            whole((1, SHARE)),
        ],
        [((SHARE + 16, WIDE), BF), ((SHARE + 16, D), BF)],
        (w_query[0], w_key[0].T, w_value[0].T, w_out[0], norm_one, norm_two),
    )
    *pieces, kept, sent = call(
        pack_feed_kernel,
        [SMEM, whole((SHARE, FF)), whole((SHARE, FF)), whole((D, FF // 4))],
        [((SHARE, 2 * UNITS), BF)] * 8 + [((D, 384), BF)] * 2,
        (table, w_gate[0], w_up[0], w_down[0].T),
        [pltpu.VMEM((8, SHARE, 2 * UNITS), BF)],
    )
    wqkv = sum(gather_eight(first), [])
    second, pieces, sent = after((second, pieces, sent), wqkv[4:6])
    wout_near = gather_near(second)
    pieces, sent = after((pieces, sent), wout_near)
    wgu = exchange_eight(pieces)
    other = swap_section(sent)
    wout = sum(arranged(wout_near, gather_far(wout_near)), [])

    block_index = lax.axis_index("blk")
    own_block = lax.dynamic_index_in_dim(span_order, block_index, 0, keepdims=False)
    positions = own_block * ROWS + jnp.arange(ROWS, dtype=jnp.int32)
    exponent = jnp.arange(HD // 2, dtype=F32) * (2.0 / HD)
    angles = positions.astype(F32)[:, None] * (rope_base ** (-exponent))[None, :]
    angles = jnp.concatenate([angles, angles], axis=-1)
    cosine, sine = jnp.cos(angles), jnp.sin(angles)
    slots = jnp.arange(NB, dtype=jnp.int32)
    place = jnp.sum(
        jnp.where(span_order[None, :] == slots[:, None], slots[None, :], 0), axis=1
    ).astype(jnp.int32)

    angle = whole((ROWS, HD))
    rows = whole((ROWS, D))
    row_scratch = pltpu.VMEM((LEN, HD), BF)
    weights = [HBM] * 10
    half_down = whole((D, 384))
    feed_scratch = [pltpu.VMEM((D, 2 * UNITS), BF), pltpu.SemaphoreType.DMA((3, 8))]

    def row_specs(blocks):
        return [whole(block.shape) for block in blocks]

    def forward(layer, x, early, late):
        h1, packed = call(
            functools.partial(project_kernel, layer),
            [SMEM, rows, angle, angle] + weights,
            [((ROWS, D), BF), (PACK, BF)],
            (table, x, cosine, sine, *wqkv),
            weight_scratch(WIDE),
        )
        first = early(packed)
        packed, first = lax.optimization_barrier((exchange(packed), first))
        heads, lse = call(
            attend_kernel,
            [SMEM, whole(PACK)],
            [(HEADS, BF), ((8, LEN), F32)],
            (place, packed),
            [row_scratch] * 3,
        )
        heads = exchange(heads)
        heads, beside = lax.optimization_barrier((heads, late(first)))
        mixed, x2, h2 = call(
            functools.partial(mix_kernel, layer),
            [SMEM, whole(HEADS), rows] + weights,
            [((ROWS, D), BF), ((ROWS, D), F32), ((ROWS, D), BF)],
            (table, heads, x, *wout),
            weight_scratch(D),
        )
        found = gather_eight(h2)
        kept_ff, parts = [], [None] * 4
        for group in GROUPS:
            blocks = sum([found[step] for step in group], [])
            count = len(blocks)
            size = 2 * len(group)
            if kept_ff:
                blocks = after(blocks, kept_ff[-1][1])
            lin, hidden, *part = call(
                functools.partial(feed_kernel, count, layer),
                [SMEM] + row_specs(blocks) + [HBM] * 8 + [half_down, half_down],
                [((size * ROWS, 2 * UNITS), F32), ((size * ROWS, UNITS), BF)]
                + [((ROWS, D), BF)] * size,
                (table, *blocks, *wgu, kept, other),
                feed_scratch,
            )
            kept_ff.append((blocks, lin, hidden))
            for number, step in enumerate(group):
                parts[step] = part[2 * number : 2 * number + 2]
        both = jnp.concatenate([h1, mixed], axis=0)
        return parts, beside, (x, both, packed, lse, x2, kept_ff)

    def backward(layer, dy, found, kept_state, early, late):
        x, _, packed, lse, x2, kept_ff = kept_state
        parts, branches, lin_grads = [None] * 4, [], []
        for group, (_, lin, _) in zip(GROUPS, kept_ff):
            blocks = sum([found[step] for step in group], [])
            count = len(blocks)
            size = 2 * len(group)
            if lin_grads:
                blocks = after(blocks, lin_grads[-1])
            lin_grad, *part = call(
                functools.partial(feed_back_kernel, count, layer),
                [SMEM]
                + row_specs(blocks)
                + [HBM] * 8
                + [half_down, half_down]
                + [whole((size * ROWS, 2 * UNITS))],
                [((size * ROWS, 2 * UNITS), BF)] + [((ROWS, D), BF)] * size,
                (table, *blocks, *wgu, kept, other, lin),
                feed_scratch,
            )
            branches += blocks
            lin_grads.append(lin_grad)
            for number, step in enumerate(group):
                parts[step] = part[2 * number : 2 * number + 2]
        dh2 = scatter_eight(parts)
        dx2, heads_grad, grad_gain_two = call(
            functools.partial(mix_back_kernel, layer),
            [SMEM, rows, rows, rows] + weights,
            [((ROWS, D), F32), (HEADS, BF), ((1, D), F32)],
            (table, dy, dh2, x2, *wout),
            weight_scratch(D),
        )
        normed = sum([item[0] for item in kept_ff], [])
        sizes = [len(group) * 2 * ROWS for group in GROUPS]
        lin_grads = after(lin_grads, dx2)
        grad_ff = call(
            feed_grads_kernel,
            row_specs(normed + branches)
            + [whole((size, 2 * UNITS)) for size in sizes]
            + [whole((size, UNITS)) for size in sizes],
            [((NB, 4 * PIECE, FF_WIDTH), BF)],
            (*normed, *branches, *lin_grads, *[item[2] for item in kept_ff]),
        )[0]
        first = early(dx2)
        heads_grad, first, grad_ff = lax.optimization_barrier(
            (exchange(heads_grad), first, grad_ff)
        )
        packed_grad = call(
            attend_back_kernel,
            [SMEM, whole(PACK), whole(HEADS), whole((8, LEN))],
            [(PACK, BF)],
            (place, packed, heads_grad, lse),
            [row_scratch] * 4
            + [pltpu.VMEM((HD, LEN), BF)]
            + [pltpu.VMEM((LEN, HD), F32)] * 3,
        )[0]
        packed_grad, second = lax.optimization_barrier((exchange(packed_grad), late(first)))
        dx, *lin_parts = call(
            functools.partial(project_back_kernel, layer),
            [SMEM, whole(PACK), rows, rows, angle, angle, whole((1, D))] + weights,
            [((ROWS, D), F32)] + [((ROWS + 16, ATT_WIDTH), BF)] * 8,
            (table, packed_grad, dx2, x, cosine, sine, grad_gain_two, *wqkv),
            [pltpu.VMEM((8, ROWS + 16, ATT_WIDTH), BF)] + weight_scratch(WIDE),
        )
        return dx, lin_parts, grad_ff, second

    def attend_grads(blocks, lin_all):
        return call(
            attend_grads_kernel,
            [SMEM] + row_specs(blocks) + [whole((ROWS + 16, ATT_WIDTH))] * 8,
            [((NB, 4 * PIECE, ATT_WIDTH), BF)],
            (gain_owner, *blocks, *lin_all),
        )[0]

    def sum_feed(pieces):
        flat = pieces.reshape(NB * 4 * PIECE, FF_WIDTH)
        return lax.psum_scatter(flat, "blk", scatter_dimension=0, tiled=True)

    def by_section(of_first, of_second):
        own = jnp.where(section == 0, of_first, of_second)
        other = swap_section(jnp.where(section == 0, of_second, of_first))
        return jnp.where(section == 0, jnp.stack([own, other]), jnp.stack([other, own]))

    gain_owner = ((4 * section + shard) // 2).astype(jnp.int32).reshape(1)
    parts, (wout, wgu, other), kept0 = forward(
        0, x0, lambda packed: wout_near, lambda first: (wout, wgu, other)
    )
    y0 = (kept0[4] + scatter_eight(parts)).astype(BF)
    cot_low = cot.astype(BF)
    parts1, (found_cot, near0), kept1 = forward(
        1,
        y0.astype(F32),
        lambda packed: gather_near(after(cot_low, packed)),
        lambda near: (arranged(near, gather_far(near)), gather_near(after(kept0[1], near))),
    )
    dx1, lin1, grad_ff1, (both0, near1, y1) = backward(
        1,
        cot,
        found_cot,
        kept1,
        lambda dx2: (arranged(near0, gather_far(after(near0, dx2))), dx2),
        lambda first: (
            first[0],
            gather_near(after(kept1[1], first[1])),
            kept1[4] + scatter_eight(after(parts1, first[1])),
        ),
    )
    y1 = y1.astype(BF)
    dy0 = dx1.astype(BF)
    ff1 = sum_feed(grad_ff1)
    dx0, lin0, grad_ff0, (both1, lin1, layer_outputs) = backward(
        0,
        dy0.astype(F32),
        gather_eight(dy0),
        kept0,
        lambda dx2: (arranged(near1, gather_far(after(near1, dx2))), dx2),
        lambda first: (
            first[0],
            exchange_eight(after(lin1, first[1])),
            by_section(y0, after(y1, first[1])),
        ),
    )
    ff0, ff1 = after((sum_feed(grad_ff0), ff1), dx0)
    upper = 2 * UNITS
    spread = jnp.stack([ff0[:, :upper], ff1[:, :upper]]).reshape(8, PIECE, upper)
    spread = lax.all_to_all(spread, EIGHT, 0, 0, tiled=True).reshape(8 * PIECE, upper)
    lower = by_section(ff0[:, upper:], ff1[:, upper:])
    lower = jnp.concatenate([lower[0], lower[1]], axis=1)
    found = lax.all_gather(jnp.concatenate([spread, lower], axis=0), "blk", axis=0)
    att1 = sum_over_blocks(after(attend_grads(sum(both1, []), after(lin1, dx0)), spread))
    att0 = attend_grads(sum(both0, []), exchange_eight(lin0))
    input_grads = by_section(dx0, dx1)
    att0 = sum_over_blocks(att0)
    grad_gate, grad_up, grad_down = call(
        finish_feed_kernel,
        [whole(found.shape)],
        [((SHARE, FF), F32), ((SHARE, FF), F32), ((D, FF // 4), F32)],
        (found,),
    )
    spread = jnp.stack([att0, att1]).reshape(8, PIECE, ATT_WIDTH)
    spread = lax.all_to_all(spread, EIGHT, 0, 0, tiled=True).reshape(1, 8 * PIECE, ATT_WIDTH)
    found = exchange(jnp.broadcast_to(spread, (NB, 8 * PIECE, ATT_WIDTH)))
    grad_query, grad_key, grad_value, grad_out, gain_grads = call(
        finish_attend_kernel,
        [whole(found.shape)],
        [
            ((SHARE, H * HD), F32),
            ((KV * HD, SHARE), F32),
            ((KV * HD, SHARE), F32),
            ((SHARE, D), F32),
            ((8, SHARE), F32),
        ],
        (found,),
    )
    return (
        layer_outputs[None, :, None],
        input_grads[None, :, None],
        gain_grads[0][None],
        grad_query[None],
        grad_key.T[None],
        grad_value.T[None],
        grad_out[None],
        gain_grads[1][None],
        grad_gate[None],
        grad_up[None],
        grad_down.T[None],
    )


def solution(mesh):
    return jax.shard_map(
        body,
        mesh=mesh,
        in_specs=(
            P(None, "wshard", "blk", None),
            P(None, "wshard", "blk", None),
            P(),
            P("section", "wshard"),
            P("section", "wshard", None),
            P("section", "wshard", None),
            P("section", "wshard", None),
            P("section", "wshard", None),
            P("section", "wshard"),
            P("section", "wshard", None),
            P("section", "wshard", None),
            P("section", "wshard", None),
        ),
        out_specs=(
            P("section", None, "wshard", "blk", None),
            P("section", None, "wshard", "blk", None),
            P("section", "wshard"),
            P("section", "wshard", None),
            P("section", "wshard", None),
            P("section", "wshard", None),
            P("section", "wshard", None),
            P("section", "wshard"),
            P("section", "wshard", None),
            P("section", "wshard", None),
            P("section", "wshard", None),
        ),
        check_vma=False,
    )
```

```python
import functools

import jax
import jax.numpy as jnp
from jax import lax
from jax.experimental import pallas as pl
from jax.experimental.pallas import tpu as pltpu
from jax.sharding import PartitionSpec as P

D = 960
H = 15
KV = 5
HD = 64
FF = 2560
ROWS = 128
NB = 16
LEN = ROWS * NB
QKV = H * HD + 2 * KV * HD
UNITS = FF // 8
WIDE = 1664
SHARE = D // 4
PIECE = 16
QKV_PART = QKV // 8
OUT_PART = D // 8
OUT_AT = 256
ATT_WIDTH = 384
FF_WIDTH = D
TILE = 256

EIGHT = ("section", "wshard")
eps_norm = 1e-05
rope_base = 10000.0
BF = jnp.bfloat16
F32 = jnp.float32
VMEM_BYTES = 56 * 1024 * 1024


def place_of(y, core):
    return (y % 2) * 4 + (y // 2) * 2 + core


def ring_pairs(step, flip):
    return [
        (place_of(y, c), place_of((y + step) % 4, c ^ flip)) for y in range(4) for c in range(2)
    ]


def hop(array, step, flip=0):
    return lax.ppermute(array, EIGHT, ring_pairs(step, flip))


def swap_section(array):
    return lax.ppermute(array, "section", [(0, 1), (1, 0)])


def after(values, *others):
    return lax.optimization_barrier((values, others))[0]


def gather_near(block):
    before = hop(block, 1)
    after_it = hop(block, -1)
    return block, hop(block, 0, 1), after_it, before


def gather_far(near):
    half = near[0].shape[0] // 2
    low, high = hop(near[3][:half], 1), hop(near[2][half:], -1)
    beside = [hop(near[2], 0, 1), hop(near[3], 0, 1)]
    return low, high, hop(low, 0, 1), hop(high, 0, 1), *beside


def arranged(near, far):
    return [[near[0], near[1]], [near[2], far[4]], list(far[:4]), [near[3], far[5]]]


def gather_eight(block):
    near = gather_near(block)
    return arranged(near, gather_far(near))


def exchange_eight(parts):
    found = [parts[0]] + [None] * 7
    for step, flip in ((0, 1), (1, 0), (3, 0), (1, 1), (3, 1)):
        found[2 * ((4 - step) % 4) + flip] = hop(parts[2 * step + flip], step, flip)
    found[4] = hop(hop(parts[4], 1), 1)
    found[5] = hop(hop(parts[5], -1), -1, 1)
    return found


def scatter_eight(parts):
    half = parts[0][0].shape[0] // 2
    total = [None] * 4
    for step in (2, 1, 3, 0):
        total[step] = parts[step][0].astype(F32) + hop(parts[step][1], 0, 1).astype(F32)
    far = total[2].astype(BF)
    low = hop(far[:half], 1).astype(F32)
    high = hop(far[half:], -1).astype(F32)
    forth = jnp.concatenate([total[1][:half] + low, total[1][half:]], axis=0).astype(BF)
    back = jnp.concatenate([total[3][:half], total[3][half:] + high], axis=0).astype(BF)
    return total[0] + hop(forth, 1).astype(F32) + hop(back, -1).astype(F32)


def norm_factor(values):
    return lax.rsqrt(jnp.mean(values * values, axis=-1, keepdims=True) + eps_norm)


def norm_backward(values, gain, grad):
    factor = norm_factor(values)
    scaled = grad * gain
    inner = jnp.mean(values * scaled, axis=-1, keepdims=True)
    grad_values = factor * scaled - values * (factor * factor * factor * inner)
    grad_gain = jnp.sum(grad * values * factor, axis=0, keepdims=True)
    return grad_values, grad_gain


def dot(left, right):
    return jnp.dot(left, right, preferred_element_type=F32)


def against(left, right):
    return lax.dot_general(left, right, (((1,), (1,)), ((), ())), preferred_element_type=F32)


def across(left, right):
    return lax.dot_general(left, right, (((0,), (0,)), ((), ())), preferred_element_type=F32)


def rotate(values, cosine, sine):
    half = HD // 2
    turned = jnp.concatenate([-values[:, half:], values[:, :half]], axis=1)
    return values * cosine + turned * sine


def rotate_back(grad, cosine, sine):
    half = HD // 2
    part = grad * sine
    return grad * cosine + jnp.concatenate([part[:, half:], -part[:, :half]], axis=1)


def fold(rows):
    half = rows.shape[0] // 2
    return jnp.concatenate([rows[:half], rows[half:]], axis=1)


def unfold(block):
    return jnp.concatenate([block[:, :HD], block[:, HD:]], axis=0)


def pack_attend_kernel(q_ref, k_ref, v_ref, o_ref, one_ref, two_ref, first_ref, second_ref):
    gap = jnp.zeros((SHARE, WIDE - QKV), BF)
    keys, values = jnp.transpose(k_ref[...]), jnp.transpose(v_ref[...])
    first_ref[0:SHARE, :] = jnp.concatenate([q_ref[...], keys, values, gap], axis=1)
    second_ref[0:SHARE, :] = o_ref[...]
    for ref, gain in ((first_ref, one_ref), (second_ref, two_ref)):
        row = jnp.concatenate([gain[...], jnp.zeros((15, SHARE), BF)], axis=0)
        width = ref.shape[1]
        ref[SHARE:, :] = jnp.concatenate([row, jnp.zeros((16, width - SHARE), BF)], axis=1)


def pack_feed_kernel(table_ref, gate_ref, up_ref, down_ref, *refs):
    pieces, (kept_ref, sent_ref, held_ref) = refs[:8], refs[8:]
    for s in range(2):
        for w in range(4):
            at = 2 * w + s
            at = slice(at * UNITS, (at + 1) * UNITS)
            held_ref[4 * s + w] = jnp.concatenate([gate_ref[:, at], up_ref[:, at]], axis=1)
    for number in range(8):
        pieces[number][...] = held_ref[4 * table_ref[2 * number] + table_ref[2 * number + 1]]
    first, second = down_ref[:, :UNITS], down_ref[:, UNITS:]
    gap = jnp.zeros((D, 384 - UNITS), BF)

    @pl.when(table_ref[0] == 0)
    def _():
        kept_ref[...] = jnp.concatenate([first, gap], axis=1)
        sent_ref[...] = jnp.concatenate([second, gap], axis=1)

    @pl.when(table_ref[0] == 1)
    def _():
        kept_ref[...] = jnp.concatenate([second, gap], axis=1)
        sent_ref[...] = jnp.concatenate([first, gap], axis=1)


def load_blocks(table_ref, layer, blocks, weight_ref, sems, gain_ref=None):
    def copies(number):
        place = table_ref[2 * number + 1]
        done = 0
        for part, block in enumerate(blocks[number]):
            rows = min(block.shape[0], SHARE - done)
            yield pltpu.make_async_copy(
                block.at[pl.ds(0, rows)],
                weight_ref.at[pl.ds(pl.multiple_of(place * SHARE + done, 16), rows)],
                sems.at[part, number],
            )
            done += rows
        if gain_ref is not None:
            last = block.shape[0] - 16
            yield pltpu.make_async_copy(
                block.at[pl.ds(last, 16), pl.ds(0, 256)], gain_ref.at[place], sems.at[2, number]
            )

    for number in range(8):

        @pl.when(table_ref[2 * number] == layer)
        def _():
            for copy in copies(number):
                copy.start()

    for number in range(8):

        @pl.when(table_ref[2 * number] == layer)
        def _():
            for copy in copies(number):
                copy.wait()

    if gain_ref is not None:
        return jnp.concatenate([gain_ref[w, 0:1, :SHARE] for w in range(4)], axis=1).astype(F32)


def by_block(refs):
    return [refs[0:1], refs[1:2], refs[2:3], refs[3:4], refs[4:6], refs[6:8], refs[8:9], refs[9:10]]


def project_kernel(layer, table_ref, x_ref, cos_ref, sin_ref, *refs):
    blocks, (h_ref, out_ref, w_ref, gain_ref, sems) = by_block(refs), refs[10:]
    gain = load_blocks(table_ref, layer, blocks, w_ref, sems, gain_ref)
    x = x_ref[...].astype(F32)
    h = (x * norm_factor(x) * gain).astype(BF)
    h_ref[...] = h
    cosine, sine = cos_ref[...], sin_ref[...]
    lin = dot(h, w_ref[:, :QKV])

    def head(at):
        return lin[:, at * HD : (at + 1) * HD]

    for group in range(KV):
        key = rotate(head(H + group), cosine, sine).astype(BF)
        pair = jnp.concatenate([key, head(H + KV + group).astype(BF)], axis=1)
        for member in range(H // KV):
            index = group * (H // KV) + member
            out_ref[index, 0:ROWS, :] = pair
            query = rotate(head(index), cosine, sine).astype(BF)
            out_ref[index, ROWS:, :] = fold(query)
    out_ref[NB - 1] = jnp.zeros((ROWS + ROWS // 2, 2 * HD), BF)


def diagonal_mask(size, keys_first):
    rows = lax.broadcasted_iota(jnp.int32, (size, size), 0)
    columns = lax.broadcasted_iota(jnp.int32, (size, size), 1)
    return rows <= columns if keys_first else columns <= rows


def attend_kernel(place_ref, in_ref, out_ref, lse_ref, q_ref, k_ref, v_ref):
    for p in range(NB):
        block = in_ref[place_ref[p]]
        at = slice(p * ROWS, (p + 1) * ROWS)
        k_ref[at, :] = block[:ROWS, :HD]
        v_ref[at, :] = block[:ROWS, HD:]
        q_ref[at, :] = unfold(block[ROWS:])
    mask = diagonal_mask(TILE, False)
    for tile in range(LEN // TILE):
        at = slice(tile * TILE, (tile + 1) * TILE)
        seen = (tile + 1) * TILE
        scores = against(q_ref[at, :], k_ref[:seen, :]) * HD ** (-0.5)
        last = jnp.where(mask, scores[:, seen - TILE :], -jnp.inf)
        if tile:
            scores = jnp.concatenate([scores[:, : seen - TILE], last], axis=1)
        else:
            scores = last
        peak = jnp.max(scores, axis=-1, keepdims=True)
        terms = jnp.exp(scores - peak)
        total = jnp.sum(terms, axis=-1, keepdims=True)
        attend = (terms * (1.0 / total)).astype(BF)
        mixed = dot(attend, v_ref[:seen, :]).astype(BF)
        lse = peak + jnp.log(total)
        lse_ref[:, at] = jnp.transpose(jnp.broadcast_to(lse, (TILE, 128)))[:8, :]
        for part in range(TILE // ROWS):
            index = place_ref[tile * (TILE // ROWS) + part]
            out_ref[index] = fold(mixed[part * ROWS : (part + 1) * ROWS])


def attend_back_kernel(
    place_ref, in_ref, do_ref, lse_ref, out_ref, q_ref, k_ref, v_ref, g_ref, kt_ref, dq_ref, dk_ref, dv_ref
):
    for p in range(NB):
        block = in_ref[place_ref[p]]
        at = slice(p * ROWS, (p + 1) * ROWS)
        k_ref[at, :] = block[:ROWS, :HD]
        v_ref[at, :] = block[:ROWS, HD:]
        q_ref[at, :] = unfold(block[ROWS:])
        g_ref[at, :] = unfold(do_ref[place_ref[p]])
    kt_ref[...] = jnp.transpose(k_ref[...].astype(F32)).astype(BF)
    dk_ref[...] = jnp.zeros((LEN, HD), F32)
    dv_ref[...] = jnp.zeros((LEN, HD), F32)
    mask = diagonal_mask(TILE, True)
    for tile in range(LEN // TILE):
        at = slice(tile * TILE, (tile + 1) * TILE)
        seen = (tile + 1) * TILE
        query = q_ref[at, :]
        grad = g_ref[at, :]
        scores = against(k_ref[:seen, :], query) * HD ** (-0.5)
        last = jnp.where(mask, scores[seen - TILE :], -jnp.inf)
        if tile:
            scores = jnp.concatenate([scores[: seen - TILE], last], axis=0)
        else:
            scores = last
        full = jnp.exp(scores - lse_ref[0:1, at])
        attend_grad = against(v_ref[:seen, :], grad)
        inner = jnp.sum(full * attend_grad, axis=0, keepdims=True)
        score_grad = (full * (attend_grad - inner)).astype(BF)
        dv_ref[:seen, :] += dot(full.astype(BF), grad)
        dk_ref[:seen, :] += dot(score_grad, query)
        dq_ref[at, :] = jnp.transpose(dot(kt_ref[:, :seen], score_grad))
    for p in range(NB):
        index = place_ref[p]
        at = slice(p * ROWS, (p + 1) * ROWS)
        key_grad = (dk_ref[at, :] * HD ** (-0.5)).astype(BF)
        query_grad = (dq_ref[at, :] * HD ** (-0.5)).astype(BF)
        out_ref[index, 0:ROWS, :] = jnp.concatenate([key_grad, dv_ref[at, :].astype(BF)], axis=1)
        out_ref[index, ROWS:, :] = fold(query_grad)


def mix_kernel(layer, table_ref, in_ref, x_ref, *refs):
    blocks, (o_ref, x2_ref, h_ref, w_ref, gain_ref, sems) = by_block(refs), refs[10:]
    gain = load_blocks(table_ref, layer, blocks, w_ref, sems, gain_ref)
    mixed = jnp.concatenate([unfold(in_ref[index]) for index in range(H)], axis=1)
    o_ref[...] = mixed
    x2 = x_ref[...].astype(F32) + dot(mixed, w_ref[...])
    x2_ref[...] = x2
    h_ref[...] = (x2 * norm_factor(x2) * gain).astype(BF)


def mix_back_kernel(layer, table_ref, dy_ref, dh_ref, x2_ref, *refs):
    blocks, (dx2_ref, out_ref, gg_ref, w_ref, gain_ref, sems) = by_block(refs), refs[10:]
    gain = load_blocks(table_ref, layer, blocks, w_ref, sems, gain_ref)
    part, grad_gain = norm_backward(x2_ref[...], gain, dh_ref[...])
    dx2 = dy_ref[...].astype(F32) + part
    dx2_ref[...] = dx2
    gg_ref[...] = grad_gain
    low = dx2.astype(BF)
    mixed_grad = against(low, w_ref[...]).astype(BF)
    for index in range(H):
        out_ref[index] = fold(mixed_grad[:, index * HD : (index + 1) * HD])
    out_ref[NB - 1] = jnp.zeros((ROWS // 2, 2 * HD), BF)


def project_back_kernel(layer, table_ref, in_ref, dx2_ref, x_ref, cos_ref, sin_ref, gg_ref, *refs):
    blocks, parts, refs = by_block(refs), refs[11:19], refs[10:11] + refs[19:]
    dx_ref, held_ref, w_ref, gain_ref, sems = refs
    gain = load_blocks(table_ref, layer, blocks, w_ref, sems, gain_ref)
    cosine, sine = cos_ref[...], sin_ref[...]
    queries, keys, values = [], [], []
    for group in range(KV):
        pair = None
        for member in range(H // KV):
            index = group * (H // KV) + member
            own = in_ref[index, 0:ROWS, :].astype(F32)
            pair = own if pair is None else pair + own
            query = unfold(in_ref[index, ROWS:, :].astype(F32))
            queries.append(rotate_back(query, cosine, sine).astype(BF))
        keys.append(rotate_back(pair[:, :HD], cosine, sine).astype(BF))
        values.append(pair[:, HD:].astype(BF))
    lin_grad = jnp.concatenate(queries + keys + values, axis=1)
    part, grad_gain = norm_backward(x_ref[...].astype(F32), gain, against(lin_grad, w_ref[:, :QKV]))
    dx_ref[...] = dx2_ref[...] + part
    gains = jnp.concatenate([grad_gain, gg_ref[...], jnp.zeros((14, D), F32)], axis=0).astype(BF)
    low = dx2_ref[...].astype(BF)
    for index in range(8):
        at = slice(index * OUT_PART, (index + 1) * OUT_PART)
        lin = lin_grad[:, index * QKV_PART : (index + 1) * QKV_PART]
        held_ref[index, 0:ROWS, :] = jnp.concatenate(
            [
                lin,
                jnp.zeros((ROWS, OUT_AT - QKV_PART), BF),
                low[:, at],
                jnp.zeros((ROWS, ATT_WIDTH - OUT_AT - OUT_PART), BF),
            ],
            axis=1,
        )
        held_ref[index, ROWS:, 0:OUT_PART] = gains[:, at]
        held_ref[index, ROWS:, OUT_PART:] = jnp.zeros((16, ATT_WIDTH - OUT_PART), BF)
    for number in range(8):
        parts[number][...] = held_ref[4 * table_ref[2 * number] + table_ref[2 * number + 1]]


def feed_kernel(count, layer, table_ref, *refs):
    normed = jnp.concatenate([ref[...] for ref in refs[:count]], axis=0)
    refs = refs[count:]
    kept_ref, other_ref, lin_ref, hidden_ref = refs[8:12]
    wgu_ref, sems = refs[-2:]
    load_blocks(table_ref, layer, [refs[k : k + 1] for k in range(8)], wgu_ref, sems)
    lin = dot(normed, wgu_ref[...])
    lin_ref[...] = lin
    gate, up = lin[:, :UNITS], lin[:, UNITS:]
    hidden = (gate * jax.nn.sigmoid(gate) * up).astype(BF)
    hidden_ref[...] = hidden
    down = jnp.where(table_ref[0] == layer, kept_ref[:, :UNITS], other_ref[:, :UNITS])
    part = against(hidden, down).astype(BF)
    for index, ref in enumerate(refs[12:-2]):
        ref[...] = part[index * ROWS : (index + 1) * ROWS]


def feed_back_kernel(count, layer, table_ref, *refs):
    branch = jnp.concatenate([ref[...] for ref in refs[:count]], axis=0)
    refs = refs[count:]
    kept_ref, other_ref, lin_ref, grad_ref = refs[8:12]
    wgu_ref, sems = refs[-2:]
    load_blocks(table_ref, layer, [refs[k : k + 1] for k in range(8)], wgu_ref, sems)
    down = jnp.where(table_ref[0] == layer, kept_ref[:, :UNITS], other_ref[:, :UNITS])
    hidden_grad = dot(branch, down)
    gate, up = lin_ref[:, :UNITS], lin_ref[:, UNITS:]
    sig = jax.nn.sigmoid(gate)
    up_grad = hidden_grad * (gate * sig)
    gate_grad = hidden_grad * up * (sig + gate * sig * (1.0 - sig))
    lin_grad = jnp.concatenate([gate_grad, up_grad], axis=1).astype(BF)
    grad_ref[...] = lin_grad
    part = against(lin_grad, wgu_ref[...]).astype(BF)
    for index, ref in enumerate(refs[12:-2]):
        ref[...] = part[index * ROWS : (index + 1) * ROWS]


def feed_grads_kernel(*refs):
    normed = jnp.concatenate([ref[...] for ref in refs[:10]], axis=0)
    branch = jnp.concatenate([ref[...] for ref in refs[10:20]], axis=0)
    lin_grad, hidden = refs[20][...], refs[21][...]
    out_ref = refs[22]
    gate_up = across(normed, lin_grad).astype(BF)
    down = across(branch, hidden).astype(BF)
    for piece in range(NB - 1):
        rows = [
            gate_up[w * SHARE + piece * PIECE : w * SHARE + (piece + 1) * PIECE] for w in range(4)
        ]
        lower = down[4 * piece * PIECE : 4 * (piece + 1) * PIECE]
        out_ref[piece] = jnp.concatenate([jnp.concatenate(rows, axis=0), lower], axis=1)
    out_ref[NB - 1] = jnp.zeros((4 * PIECE, FF_WIDTH), BF)


def attend_grads_kernel(index_ref, *refs):
    found, parts, out_ref = by_block(refs), refs[10:18], refs[18]
    normed, mixed = [], []
    for block in found:
        if len(block) == 2:
            normed.append(block[0][...])
            mixed.append(block[1][...])
        else:
            normed.append(block[0][0:ROWS, :])
            mixed.append(block[0][ROWS:, :])
    normed, mixed = jnp.concatenate(normed, axis=0), jnp.concatenate(mixed, axis=0)
    lin_grad = jnp.concatenate([ref[0:ROWS, 0:OUT_AT] for ref in parts], axis=0)
    branch = jnp.concatenate([ref[0:ROWS, OUT_AT:] for ref in parts], axis=0)
    weight = across(normed, lin_grad).astype(BF)
    out_weight = across(mixed, branch).astype(BF)
    for piece in range(NB - 1):
        for w in range(4):
            at = w * SHARE + piece * PIECE
            to = slice(w * PIECE, (w + 1) * PIECE)
            out_ref[piece, to, 0:OUT_AT] = weight[at : at + PIECE]
            out_ref[piece, to, OUT_AT:] = out_weight[at : at + PIECE]
    gains = parts[0][ROWS:, 0:OUT_AT].astype(F32)
    for ref in parts[1:]:
        gains = gains + ref[ROWS:, 0:OUT_AT].astype(F32)
    out_ref[NB - 1] = jnp.zeros((4 * PIECE, ATT_WIDTH), BF)
    at = pl.multiple_of(index_ref[0] * PIECE, PIECE)
    out_ref[NB - 1, pl.ds(at, PIECE), 0:OUT_AT] = gains.astype(BF)


def finish_feed_kernel(in_ref, gate_ref, up_ref, down_ref):
    for piece in range(NB - 1):
        at = slice(piece * PIECE, (piece + 1) * PIECE)
        parts = []
        for w in range(4):
            for s in range(2):
                at_row = (4 * s + w) * PIECE
                parts.append(in_ref[piece, at_row : at_row + PIECE, :].astype(F32))
        gate_ref[at, :] = jnp.concatenate([part[:, :UNITS] for part in parts], axis=1)
        up_ref[at, :] = jnp.concatenate([part[:, UNITS:] for part in parts], axis=1)
        rows = in_ref[piece, 8 * PIECE :, :].astype(F32)
        to = slice(4 * piece * PIECE, 4 * (piece + 1) * PIECE)
        down_ref[to, :] = rows


def finish_attend_kernel(in_ref, q_ref, k_ref, v_ref, o_ref, gain_ref):
    keys, values = [], []
    for piece in range(NB - 1):
        at = slice(piece * PIECE, (piece + 1) * PIECE)
        parts = [in_ref[piece, t * PIECE : (t + 1) * PIECE, :].astype(F32) for t in range(8)]
        lin = jnp.concatenate([part[:, :QKV_PART] for part in parts], axis=1)
        q_ref[at, :] = lin[:, : H * HD]
        keys.append(lin[:, H * HD : (H + KV) * HD])
        values.append(lin[:, (H + KV) * HD :])
        o_ref[at, :] = jnp.concatenate(
            [part[:, OUT_AT : OUT_AT + OUT_PART] for part in parts], axis=1
        )
    k_ref[...] = jnp.transpose(jnp.concatenate(keys, axis=0))
    v_ref[...] = jnp.transpose(jnp.concatenate(values, axis=0))
    sides = []
    for side in range(2):
        total = None
        for w in range(4):
            t = 2 * w + side
            own = in_ref[NB - 1, t * PIECE : (t + 1) * PIECE, 0:OUT_PART].astype(F32)[:8]
            total = own if total is None else total + own
        sides.append(total)
    gain_ref[...] = jnp.concatenate(sides, axis=1)


def whole(shape):
    return pl.BlockSpec(shape, lambda i: (0,) * len(shape))


def layer_of(layer, shape):
    return pl.BlockSpec((None,) + shape, lambda i: (layer,) + (0,) * len(shape))


def call(kernel, in_specs, outs, args, scratch=()):
    return pl.pallas_call(
        kernel,
        grid=(1,),
        in_specs=in_specs,
        out_specs=[whole(shape) for shape, _ in outs],
        out_shape=[jax.ShapeDtypeStruct(shape, dtype) for shape, dtype in outs],
        scratch_shapes=list(scratch),
        compiler_params=pltpu.CompilerParams(vmem_limit_bytes=VMEM_BYTES),
        cost_estimate=pl.CostEstimate(flops=1, bytes_accessed=1, transcendentals=0),
    )(*args)


SMEM = pl.BlockSpec(memory_space=pltpu.SMEM)
HBM = pl.BlockSpec(memory_space=pl.ANY)
PACK = (NB, ROWS + ROWS // 2, 2 * HD)
HEADS = (NB, ROWS // 2, 2 * HD)
GROUPS = ((0, 1, 2, 3),)


def exchange(array):
    return lax.all_to_all(array, "blk", 0, 0, tiled=True)


def sum_over_blocks(pieces):
    return jnp.sum(exchange(pieces).astype(F32), axis=0).astype(BF)


def weight_scratch(width):
    return [
        pltpu.VMEM((D, width), BF),
        pltpu.VMEM((4, 16, 256), BF),
        pltpu.SemaphoreType.DMA((3, 8)),
    ]


def body(
    tokens,
    cotangent,
    span_order,
    norm_one,
    w_query,
    w_key,
    w_value,
    w_out,
    norm_two,
    w_gate,
    w_up,
    w_down,
):
    section = lax.axis_index("section")
    shard = lax.axis_index("wshard")
    core = shard % 2
    y = 2 * (shard // 2) + section

    owners = []
    for step in range(4):
        there = (y + step) % 4
        for flip in range(2):
            owners += [there % 2, 2 * (there // 2) + (core ^ flip)]
    table = jnp.stack(owners).astype(jnp.int32)

    x0 = lax.dynamic_index_in_dim(tokens[:, 0], section, 0, keepdims=False)
    cot = lax.dynamic_index_in_dim(cotangent[:, 0], section, 0, keepdims=False)
    first, second = call(
        pack_attend_kernel,
        [
            whole((SHARE, D)),
            whole((KV * HD, SHARE)),
            whole((KV * HD, SHARE)),
            whole((SHARE, D)),
            whole((1, SHARE)),
            whole((1, SHARE)),
        ],
        [((SHARE + 16, WIDE), BF), ((SHARE + 16, D), BF)],
        (w_query[0], w_key[0].T, w_value[0].T, w_out[0], norm_one, norm_two),
    )
    *pieces, kept, sent = call(
        pack_feed_kernel,
        [SMEM, whole((SHARE, FF)), whole((SHARE, FF)), whole((D, FF // 4))],
        [((SHARE, 2 * UNITS), BF)] * 8 + [((D, 384), BF)] * 2,
        (table, w_gate[0], w_up[0], w_down[0].T),
        [pltpu.VMEM((8, SHARE, 2 * UNITS), BF)],
    )
    wqkv = sum(gather_eight(first), [])
    later = {}

    block_index = lax.axis_index("blk")
    own_block = lax.dynamic_index_in_dim(span_order, block_index, 0, keepdims=False)
    positions = own_block * ROWS + jnp.arange(ROWS, dtype=jnp.int32)
    exponent = jnp.arange(HD // 2, dtype=F32) * (2.0 / HD)
    angles = positions.astype(F32)[:, None] * (rope_base ** (-exponent))[None, :]
    angles = jnp.concatenate([angles, angles], axis=-1)
    cosine, sine = jnp.cos(angles), jnp.sin(angles)
    slots = jnp.arange(NB, dtype=jnp.int32)
    place = jnp.sum(
        jnp.where(span_order[None, :] == slots[:, None], slots[None, :], 0), axis=1
    ).astype(jnp.int32)

    angle = whole((ROWS, HD))
    rows = whole((ROWS, D))
    row_scratch = pltpu.VMEM((LEN, HD), BF)
    weights = [HBM] * 10
    half_down = whole((D, 384))
    feed_scratch = [pltpu.VMEM((D, 2 * UNITS), BF), pltpu.SemaphoreType.DMA((3, 8))]

    def row_specs(blocks):
        return [whole(block.shape) for block in blocks]

    def forward(layer, x, early, late):
        h1, packed = call(
            functools.partial(project_kernel, layer),
            [SMEM, rows, angle, angle] + weights,
            [((ROWS, D), BF), (PACK, BF)],
            (table, x, cosine, sine, *wqkv),
            weight_scratch(WIDE),
        )
        first = early(packed)
        packed, first = lax.optimization_barrier((exchange(packed), first))
        heads, lse = call(
            attend_kernel,
            [SMEM, whole(PACK)],
            [(HEADS, BF), ((8, LEN), F32)],
            (place, packed),
            [row_scratch] * 3,
        )
        heads = exchange(heads)
        heads, beside = lax.optimization_barrier((heads, late(first)))
        if layer == 0:
            later.update(beside)
        mixed, x2, h2 = call(
            functools.partial(mix_kernel, layer),
            [SMEM, whole(HEADS), rows] + weights,
            [((ROWS, D), BF), ((ROWS, D), F32), ((ROWS, D), BF)],
            (table, heads, x, *later["out"]),
            weight_scratch(D),
        )
        found = gather_eight(h2)
        kept_ff, parts = [], [None] * 4
        for group in GROUPS:
            blocks = sum([found[step] for step in group], [])
            count = len(blocks)
            size = 2 * len(group)
            if kept_ff:
                blocks = after(blocks, kept_ff[-1][1])
            lin, hidden, *part = call(
                functools.partial(feed_kernel, count, layer),
                [SMEM] + row_specs(blocks) + [HBM] * 8 + [half_down, half_down],
                [((size * ROWS, 2 * UNITS), F32), ((size * ROWS, UNITS), BF)]
                + [((ROWS, D), BF)] * size,
                (table, *blocks, *later["feed"], kept, later["down"]),
                feed_scratch,
            )
            kept_ff.append((blocks, lin, hidden))
            for number, step in enumerate(group):
                parts[step] = part[2 * number : 2 * number + 2]
        both = jnp.concatenate([h1, mixed], axis=0)
        return parts, beside, (x, both, packed, lse, x2, kept_ff)

    def backward(layer, dy, found, kept_state, early, late):
        x, _, packed, lse, x2, kept_ff = kept_state
        parts, branches, lin_grads = [None] * 4, [], []
        for group, (_, lin, _) in zip(GROUPS, kept_ff):
            blocks = sum([found[step] for step in group], [])
            count = len(blocks)
            size = 2 * len(group)
            if lin_grads:
                blocks = after(blocks, lin_grads[-1])
            lin_grad, *part = call(
                functools.partial(feed_back_kernel, count, layer),
                [SMEM]
                + row_specs(blocks)
                + [HBM] * 8
                + [half_down, half_down]
                + [whole((size * ROWS, 2 * UNITS))],
                [((size * ROWS, 2 * UNITS), BF)] + [((ROWS, D), BF)] * size,
                (table, *blocks, *later["feed"], kept, later["down"], lin),
                feed_scratch,
            )
            branches += blocks
            lin_grads.append(lin_grad)
            for number, step in enumerate(group):
                parts[step] = part[2 * number : 2 * number + 2]
        dh2 = scatter_eight(parts)
        dx2, heads_grad, grad_gain_two = call(
            functools.partial(mix_back_kernel, layer),
            [SMEM, rows, rows, rows] + weights,
            [((ROWS, D), F32), (HEADS, BF), ((1, D), F32)],
            (table, dy, dh2, x2, *later["out"]),
            weight_scratch(D),
        )
        normed = sum([item[0] for item in kept_ff], [])
        sizes = [len(group) * 2 * ROWS for group in GROUPS]
        lin_grads = after(lin_grads, dx2)
        grad_ff = call(
            feed_grads_kernel,
            row_specs(normed + branches)
            + [whole((size, 2 * UNITS)) for size in sizes]
            + [whole((size, UNITS)) for size in sizes],
            [((NB, 4 * PIECE, FF_WIDTH), BF)],
            (*normed, *branches, *lin_grads, *[item[2] for item in kept_ff]),
        )[0]
        first = early(dx2)
        heads_grad, first, grad_ff = lax.optimization_barrier(
            (exchange(heads_grad), first, grad_ff)
        )
        packed_grad = call(
            attend_back_kernel,
            [SMEM, whole(PACK), whole(HEADS), whole((8, LEN))],
            [(PACK, BF)],
            (place, packed, heads_grad, lse),
            [row_scratch] * 4
            + [pltpu.VMEM((HD, LEN), BF)]
            + [pltpu.VMEM((LEN, HD), F32)] * 3,
        )[0]
        packed_grad, second = lax.optimization_barrier((exchange(packed_grad), late(first)))
        dx, *lin_parts = call(
            functools.partial(project_back_kernel, layer),
            [SMEM, whole(PACK), rows, rows, angle, angle, whole((1, D))] + weights,
            [((ROWS, D), F32)] + [((ROWS + 16, ATT_WIDTH), BF)] * 8,
            (table, packed_grad, dx2, x, cosine, sine, grad_gain_two, *wqkv),
            [pltpu.VMEM((8, ROWS + 16, ATT_WIDTH), BF)] + weight_scratch(WIDE),
        )
        return dx, lin_parts, grad_ff, second

    def attend_grads(blocks, lin_all):
        return call(
            attend_grads_kernel,
            [SMEM] + row_specs(blocks) + [whole((ROWS + 16, ATT_WIDTH))] * 8,
            [((NB, 4 * PIECE, ATT_WIDTH), BF)],
            (gain_owner, *blocks, *lin_all),
        )[0]

    def sum_feed(pieces):
        flat = pieces.reshape(NB * 4 * PIECE, FF_WIDTH)
        return lax.psum_scatter(flat, "blk", scatter_dimension=0, tiled=True)

    def by_section(of_first, of_second):
        own = jnp.where(section == 0, of_first, of_second)
        other = swap_section(jnp.where(section == 0, of_second, of_first))
        return jnp.where(section == 0, jnp.stack([own, other]), jnp.stack([other, own]))

    gain_owner = ((4 * section + shard) // 2).astype(jnp.int32).reshape(1)
    def first_weights(packed):
        later["near"] = gather_near(after(second, packed))
        return later["near"]

    def last_weights(first):
        near = later.pop("near")
        ready = after(pieces, near)
        for number in (3, 4, 5, 7):
            ready[number] = after(pieces[number], first)
        halves = after(sent, first)
        return {
            "out": sum(arranged(near, gather_far(near)), []),
            "feed": exchange_eight(ready),
            "down": swap_section(halves),
        }

    parts, _, kept0 = forward(0, x0, first_weights, last_weights)
    y0 = (kept0[4] + scatter_eight(parts)).astype(BF)
    parts1, (found_cot, near0), kept1 = forward(
        1,
        y0,
        lambda packed: gather_near(after(cot, packed)),
        lambda near: (arranged(near, gather_far(near)), gather_near(after(kept0[1], near))),
    )
    dx1, lin1, grad_ff1, (both0, near1) = backward(
        1,
        cot,
        found_cot,
        kept1,
        lambda dx2: (arranged(near0, gather_far(after(near0, dx2))), dx2),
        lambda first: (
            first[0],
            gather_near(after(kept1[1], first[1])),
        ),
    )
    dy0 = dx1.astype(BF)
    ff1 = sum_feed(grad_ff1)
    dx0, lin0, grad_ff0, (both1, lin1) = backward(
        0,
        dy0,
        gather_eight(dy0),
        kept0,
        lambda dx2: (arranged(near1, gather_far(after(near1, dx2))), dx2),
        lambda first: (
            first[0],
            exchange_eight(after(lin1, first[1])),
        ),
    )
    att1 = attend_grads(sum(both1, []), after(lin1, dx0))
    lin0 = exchange_eight(lin0)
    ff0, ff1, lin0 = after((sum_feed(grad_ff0), ff1, lin0), att1)
    att0 = attend_grads(sum(both0, []), lin0)
    y1 = (kept1[4] + scatter_eight(after(parts1, att0))).astype(BF)
    layer_outputs = by_section(y0, y1)
    upper = 2 * UNITS
    spread = jnp.stack([ff0[:, :upper], ff1[:, :upper]]).reshape(8, PIECE, upper)
    spread = lax.all_to_all(spread, EIGHT, 0, 0, tiled=True).reshape(8 * PIECE, upper)
    lower = by_section(ff0[:, upper:], ff1[:, upper:])
    lower = jnp.concatenate([lower[0], lower[1]], axis=1)
    found = lax.all_gather(jnp.concatenate([spread, lower], axis=0), "blk", axis=0)
    input_grads = by_section(dx0, dx1)
    att1, att0 = sum_over_blocks(att1), sum_over_blocks(att0)
    grad_gate, grad_up, grad_down = call(
        finish_feed_kernel,
        [whole(found.shape)],
        [((SHARE, FF), F32), ((SHARE, FF), F32), ((D, FF // 4), F32)],
        (found,),
    )
    spread = jnp.stack([att0, att1]).reshape(8, PIECE, ATT_WIDTH)
    spread = lax.all_to_all(spread, EIGHT, 0, 0, tiled=True).reshape(1, 8 * PIECE, ATT_WIDTH)
    found = exchange(jnp.broadcast_to(spread, (NB, 8 * PIECE, ATT_WIDTH)))
    grad_query, grad_key, grad_value, grad_out, gain_grads = call(
        finish_attend_kernel,
        [whole(found.shape)],
        [
            ((SHARE, H * HD), F32),
            ((KV * HD, SHARE), F32),
            ((KV * HD, SHARE), F32),
            ((SHARE, D), F32),
            ((8, SHARE), F32),
        ],
        (found,),
    )
    return (
        layer_outputs[None, :, None],
        input_grads[None, :, None],
        gain_grads[0][None],
        grad_query[None],
        grad_key.T[None],
        grad_value.T[None],
        grad_out[None],
        gain_grads[1][None],
        grad_gate[None],
        grad_up[None],
        grad_down.T[None],
    )


def solution(mesh):
    return jax.shard_map(
        body,
        mesh=mesh,
        in_specs=(
            P(None, "wshard", "blk", None),
            P(None, "wshard", "blk", None),
            P(),
            P("section", "wshard"),
            P("section", "wshard", None),
            P("section", "wshard", None),
            P("section", "wshard", None),
            P("section", "wshard", None),
            P("section", "wshard"),
            P("section", "wshard", None),
            P("section", "wshard", None),
            P("section", "wshard", None),
        ),
        out_specs=(
            P("section", None, "wshard", "blk", None),
            P("section", None, "wshard", "blk", None),
            P("section", "wshard"),
            P("section", "wshard", None),
            P("section", "wshard", None),
            P("section", "wshard", None),
            P("section", "wshard", None),
            P("section", "wshard"),
            P("section", "wshard", None),
            P("section", "wshard", None),
            P("section", "wshard", None),
        ),
        check_vma=False,
    )
```

```python
import functools

import jax
import jax.numpy as jnp
from jax import lax
from jax.experimental import pallas as pl
from jax.experimental.pallas import tpu as pltpu
from jax.sharding import PartitionSpec as P

D = 960
H = 15
KV = 5
HD = 64
FF = 2560
ROWS = 128
NB = 16
LEN = ROWS * NB
QKV = H * HD + 2 * KV * HD
UNITS = FF // 8
WIDE = 1664
SHARE = D // 4
PIECE = 16
QKV_PART = QKV // 8
OUT_PART = D // 8
OUT_AT = 256
ATT_WIDTH = 384
FF_WIDTH = D
TILE = 256

EIGHT = ("section", "wshard")
eps_norm = 1e-05
rope_base = 10000.0
BF = jnp.bfloat16
F32 = jnp.float32
VMEM_BYTES = 56 * 1024 * 1024


def place_of(y, core):
    return (y % 2) * 4 + (y // 2) * 2 + core


def ring_pairs(step, flip):
    return [
        (place_of(y, c), place_of((y + step) % 4, c ^ flip)) for y in range(4) for c in range(2)
    ]


def hop(array, step, flip=0):
    return lax.ppermute(array, EIGHT, ring_pairs(step, flip))


def swap_section(array):
    return lax.ppermute(array, "section", [(0, 1), (1, 0)])


def after(values, *others):
    return lax.optimization_barrier((values, others))[0]


def gather_near(block):
    before = hop(block, 1)
    after_it = hop(block, -1)
    return block, hop(block, 0, 1), after_it, before


def gather_far(near):
    half = near[0].shape[0] // 2
    low, high = hop(near[3][:half], 1), hop(near[2][half:], -1)
    beside = [hop(near[2], 0, 1), hop(near[3], 0, 1)]
    return low, high, hop(low, 0, 1), hop(high, 0, 1), *beside


def arranged(near, far):
    return [[near[0], near[1]], [near[2], far[4]], list(far[:4]), [near[3], far[5]]]


def gather_eight(block):
    near = gather_near(block)
    return arranged(near, gather_far(near))


def exchange_eight(parts):
    found = [parts[0]] + [None] * 7
    for step, flip in ((0, 1), (1, 0), (3, 0), (1, 1), (3, 1), (2, 0), (2, 1)):
        found[2 * ((4 - step) % 4) + flip] = hop(parts[2 * step + flip], step, flip)
    return found


def scatter_eight(parts):
    half = parts[0][0].shape[0] // 2
    total = [None] * 4
    for step in (2, 1, 3, 0):
        total[step] = parts[step][0].astype(F32) + hop(parts[step][1], 0, 1).astype(F32)
    far = total[2].astype(BF)
    low = hop(far[:half], 1).astype(F32)
    high = hop(far[half:], -1).astype(F32)
    forth = jnp.concatenate([total[1][:half] + low, total[1][half:]], axis=0).astype(BF)
    back = jnp.concatenate([total[3][:half], total[3][half:] + high], axis=0).astype(BF)
    return total[0] + hop(forth, 1).astype(F32) + hop(back, -1).astype(F32)


def norm_factor(values):
    return lax.rsqrt(jnp.mean(values * values, axis=-1, keepdims=True) + eps_norm)


def norm_backward(values, gain, grad):
    factor = norm_factor(values)
    scaled = grad * gain
    inner = jnp.mean(values * scaled, axis=-1, keepdims=True)
    grad_values = factor * scaled - values * (factor * factor * factor * inner)
    grad_gain = jnp.sum(grad * values * factor, axis=0, keepdims=True)
    return grad_values, grad_gain


def dot(left, right):
    return jnp.dot(left, right, preferred_element_type=F32)


def against(left, right):
    return lax.dot_general(left, right, (((1,), (1,)), ((), ())), preferred_element_type=F32)


def across(left, right):
    return lax.dot_general(left, right, (((0,), (0,)), ((), ())), preferred_element_type=F32)


def rotate(values, cosine, sine):
    half = HD // 2
    turned = jnp.concatenate([-values[:, half:], values[:, :half]], axis=1)
    return values * cosine + turned * sine


def rotate_back(grad, cosine, sine):
    half = HD // 2
    part = grad * sine
    return grad * cosine + jnp.concatenate([part[:, half:], -part[:, :half]], axis=1)


def fold(rows):
    half = rows.shape[0] // 2
    return jnp.concatenate([rows[:half], rows[half:]], axis=1)


def unfold(block):
    return jnp.concatenate([block[:, :HD], block[:, HD:]], axis=0)


def pack_attend_kernel(q_ref, k_ref, v_ref, o_ref, one_ref, two_ref, first_ref, second_ref):
    gap = jnp.zeros((SHARE, WIDE - QKV), BF)
    keys, values = jnp.transpose(k_ref[...]), jnp.transpose(v_ref[...])
    first_ref[0:SHARE, :] = jnp.concatenate([q_ref[...], keys, values, gap], axis=1)
    second_ref[0:SHARE, :] = o_ref[...]
    for ref, gain in ((first_ref, one_ref), (second_ref, two_ref)):
        row = jnp.concatenate([gain[...], jnp.zeros((15, SHARE), BF)], axis=0)
        width = ref.shape[1]
        ref[SHARE:, :] = jnp.concatenate([row, jnp.zeros((16, width - SHARE), BF)], axis=1)


def pack_feed_kernel(table_ref, gate_ref, up_ref, down_ref, *refs):
    pieces, (kept_ref, sent_ref, held_ref) = refs[:8], refs[8:]
    for s in range(2):
        for w in range(4):
            at = 2 * w + s
            at = slice(at * UNITS, (at + 1) * UNITS)
            held_ref[4 * s + w] = jnp.concatenate([gate_ref[:, at], up_ref[:, at]], axis=1)
    for number in range(8):
        pieces[number][...] = held_ref[4 * table_ref[2 * number] + table_ref[2 * number + 1]]
    first, second = down_ref[:, :UNITS], down_ref[:, UNITS:]
    gap = jnp.zeros((D, 384 - UNITS), BF)

    @pl.when(table_ref[0] == 0)
    def _():
        kept_ref[...] = jnp.concatenate([first, gap], axis=1)
        sent_ref[...] = jnp.concatenate([second, gap], axis=1)

    @pl.when(table_ref[0] == 1)
    def _():
        kept_ref[...] = jnp.concatenate([second, gap], axis=1)
        sent_ref[...] = jnp.concatenate([first, gap], axis=1)


def load_blocks(table_ref, layer, blocks, weight_ref, sems, gain_ref=None):
    def copies(number):
        place = table_ref[2 * number + 1]
        done = 0
        for part, block in enumerate(blocks[number]):
            rows = min(block.shape[0], SHARE - done)
            yield pltpu.make_async_copy(
                block.at[pl.ds(0, rows)],
                weight_ref.at[pl.ds(pl.multiple_of(place * SHARE + done, 16), rows)],
                sems.at[part, number],
            )
            done += rows
        if gain_ref is not None:
            last = block.shape[0] - 16
            yield pltpu.make_async_copy(
                block.at[pl.ds(last, 16), pl.ds(0, 256)], gain_ref.at[place], sems.at[2, number]
            )

    for number in range(8):

        @pl.when(table_ref[2 * number] == layer)
        def _():
            for copy in copies(number):
                copy.start()

    for number in range(8):

        @pl.when(table_ref[2 * number] == layer)
        def _():
            for copy in copies(number):
                copy.wait()

    if gain_ref is not None:
        return jnp.concatenate([gain_ref[w, 0:1, :SHARE] for w in range(4)], axis=1).astype(F32)


def by_block(refs):
    return [refs[0:1], refs[1:2], refs[2:3], refs[3:4], refs[4:6], refs[6:8], refs[8:9], refs[9:10]]


def project_kernel(layer, table_ref, x_ref, cos_ref, sin_ref, *refs):
    blocks, (h_ref, out_ref, w_ref, gain_ref, sems) = by_block(refs), refs[10:]
    gain = load_blocks(table_ref, layer, blocks, w_ref, sems, gain_ref)
    x = x_ref[...].astype(F32)
    h = (x * norm_factor(x) * gain).astype(BF)
    h_ref[...] = h
    cosine, sine = cos_ref[...], sin_ref[...]
    lin = dot(h, w_ref[:, :QKV])

    def head(at):
        return lin[:, at * HD : (at + 1) * HD]

    for group in range(KV):
        key = rotate(head(H + group), cosine, sine).astype(BF)
        pair = jnp.concatenate([key, head(H + KV + group).astype(BF)], axis=1)
        for member in range(H // KV):
            index = group * (H // KV) + member
            out_ref[index, 0:ROWS, :] = pair
            query = rotate(head(index), cosine, sine).astype(BF)
            out_ref[index, ROWS:, :] = fold(query)
    out_ref[NB - 1] = jnp.zeros((ROWS + ROWS // 2, 2 * HD), BF)


def diagonal_mask(size, keys_first):
    rows = lax.broadcasted_iota(jnp.int32, (size, size), 0)
    columns = lax.broadcasted_iota(jnp.int32, (size, size), 1)
    return rows <= columns if keys_first else columns <= rows


def attend_kernel(place_ref, in_ref, out_ref, lse_ref, q_ref, k_ref, v_ref):
    for p in range(NB):
        block = in_ref[place_ref[p]]
        at = slice(p * ROWS, (p + 1) * ROWS)
        k_ref[at, :] = block[:ROWS, :HD]
        v_ref[at, :] = block[:ROWS, HD:]
        q_ref[at, :] = unfold(block[ROWS:])
    mask = diagonal_mask(TILE, False)
    for tile in range(LEN // TILE):
        at = slice(tile * TILE, (tile + 1) * TILE)
        seen = (tile + 1) * TILE
        scores = against(q_ref[at, :], k_ref[:seen, :]) * HD ** (-0.5)
        last = jnp.where(mask, scores[:, seen - TILE :], -jnp.inf)
        if tile:
            scores = jnp.concatenate([scores[:, : seen - TILE], last], axis=1)
        else:
            scores = last
        peak = jnp.max(scores, axis=-1, keepdims=True)
        terms = jnp.exp(scores - peak)
        total = jnp.sum(terms, axis=-1, keepdims=True)
        attend = (terms * (1.0 / total)).astype(BF)
        mixed = dot(attend, v_ref[:seen, :]).astype(BF)
        lse = peak + jnp.log(total)
        lse_ref[:, at] = jnp.transpose(jnp.broadcast_to(lse, (TILE, 128)))[:8, :]
        for part in range(TILE // ROWS):
            index = place_ref[tile * (TILE // ROWS) + part]
            out_ref[index] = fold(mixed[part * ROWS : (part + 1) * ROWS])


def attend_back_kernel(
    place_ref, in_ref, do_ref, lse_ref, out_ref, q_ref, k_ref, v_ref, g_ref, kt_ref, dq_ref, dk_ref, dv_ref
):
    for p in range(NB):
        block = in_ref[place_ref[p]]
        at = slice(p * ROWS, (p + 1) * ROWS)
        k_ref[at, :] = block[:ROWS, :HD]
        v_ref[at, :] = block[:ROWS, HD:]
        q_ref[at, :] = unfold(block[ROWS:])
        g_ref[at, :] = unfold(do_ref[place_ref[p]])
    kt_ref[...] = jnp.transpose(k_ref[...].astype(F32)).astype(BF)
    dk_ref[...] = jnp.zeros((LEN, HD), F32)
    dv_ref[...] = jnp.zeros((LEN, HD), F32)
    mask = diagonal_mask(TILE, True)
    for tile in range(LEN // TILE):
        at = slice(tile * TILE, (tile + 1) * TILE)
        seen = (tile + 1) * TILE
        query = q_ref[at, :]
        grad = g_ref[at, :]
        scores = against(k_ref[:seen, :], query) * HD ** (-0.5)
        last = jnp.where(mask, scores[seen - TILE :], -jnp.inf)
        if tile:
            scores = jnp.concatenate([scores[: seen - TILE], last], axis=0)
        else:
            scores = last
        full = jnp.exp(scores - lse_ref[0:1, at])
        attend_grad = against(v_ref[:seen, :], grad)
        inner = jnp.sum(full * attend_grad, axis=0, keepdims=True)
        score_grad = (full * (attend_grad - inner)).astype(BF)
        dv_ref[:seen, :] += dot(full.astype(BF), grad)
        dk_ref[:seen, :] += dot(score_grad, query)
        dq_ref[at, :] = jnp.transpose(dot(kt_ref[:, :seen], score_grad))
    for p in range(NB):
        index = place_ref[p]
        at = slice(p * ROWS, (p + 1) * ROWS)
        key_grad = (dk_ref[at, :] * HD ** (-0.5)).astype(BF)
        query_grad = (dq_ref[at, :] * HD ** (-0.5)).astype(BF)
        out_ref[index, 0:ROWS, :] = jnp.concatenate([key_grad, dv_ref[at, :].astype(BF)], axis=1)
        out_ref[index, ROWS:, :] = fold(query_grad)


def mix_kernel(layer, table_ref, in_ref, x_ref, *refs):
    blocks, (o_ref, x2_ref, h_ref, w_ref, gain_ref, sems) = by_block(refs), refs[10:]
    gain = load_blocks(table_ref, layer, blocks, w_ref, sems, gain_ref)
    mixed = jnp.concatenate([unfold(in_ref[index]) for index in range(H)], axis=1)
    o_ref[...] = mixed
    x2 = x_ref[...].astype(F32) + dot(mixed, w_ref[...])
    x2_ref[...] = x2
    h_ref[...] = (x2 * norm_factor(x2) * gain).astype(BF)


def mix_back_kernel(layer, table_ref, dy_ref, dh_ref, x2_ref, *refs):
    blocks, (dx2_ref, out_ref, gg_ref, w_ref, gain_ref, sems) = by_block(refs), refs[10:]
    gain = load_blocks(table_ref, layer, blocks, w_ref, sems, gain_ref)
    part, grad_gain = norm_backward(x2_ref[...], gain, dh_ref[...])
    dx2 = dy_ref[...].astype(F32) + part
    dx2_ref[...] = dx2
    gg_ref[...] = grad_gain
    low = dx2.astype(BF)
    mixed_grad = against(low, w_ref[...]).astype(BF)
    for index in range(H):
        out_ref[index] = fold(mixed_grad[:, index * HD : (index + 1) * HD])
    out_ref[NB - 1] = jnp.zeros((ROWS // 2, 2 * HD), BF)


def project_back_kernel(layer, table_ref, in_ref, dx2_ref, x_ref, cos_ref, sin_ref, gg_ref, *refs):
    blocks, parts, refs = by_block(refs), refs[11:19], refs[10:11] + refs[19:]
    dx_ref, held_ref, w_ref, gain_ref, sems = refs
    gain = load_blocks(table_ref, layer, blocks, w_ref, sems, gain_ref)
    cosine, sine = cos_ref[...], sin_ref[...]
    queries, keys, values = [], [], []
    for group in range(KV):
        pair = None
        for member in range(H // KV):
            index = group * (H // KV) + member
            own = in_ref[index, 0:ROWS, :].astype(F32)
            pair = own if pair is None else pair + own
            query = unfold(in_ref[index, ROWS:, :].astype(F32))
            queries.append(rotate_back(query, cosine, sine).astype(BF))
        keys.append(rotate_back(pair[:, :HD], cosine, sine).astype(BF))
        values.append(pair[:, HD:].astype(BF))
    lin_grad = jnp.concatenate(queries + keys + values, axis=1)
    part, grad_gain = norm_backward(x_ref[...].astype(F32), gain, against(lin_grad, w_ref[:, :QKV]))
    dx_ref[...] = dx2_ref[...] + part
    gains = jnp.concatenate([grad_gain, gg_ref[...], jnp.zeros((14, D), F32)], axis=0).astype(BF)
    low = dx2_ref[...].astype(BF)
    for index in range(8):
        at = slice(index * OUT_PART, (index + 1) * OUT_PART)
        lin = lin_grad[:, index * QKV_PART : (index + 1) * QKV_PART]
        held_ref[index, 0:ROWS, :] = jnp.concatenate(
            [
                lin,
                jnp.zeros((ROWS, OUT_AT - QKV_PART), BF),
                low[:, at],
                jnp.zeros((ROWS, ATT_WIDTH - OUT_AT - OUT_PART), BF),
            ],
            axis=1,
        )
        held_ref[index, ROWS:, 0:OUT_PART] = gains[:, at]
        held_ref[index, ROWS:, OUT_PART:] = jnp.zeros((16, ATT_WIDTH - OUT_PART), BF)
    for number in range(8):
        parts[number][...] = held_ref[4 * table_ref[2 * number] + table_ref[2 * number + 1]]


def feed_kernel(count, layer, table_ref, *refs):
    normed = jnp.concatenate([ref[...] for ref in refs[:count]], axis=0)
    refs = refs[count:]
    kept_ref, other_ref, lin_ref, hidden_ref = refs[8:12]
    wgu_ref, sems = refs[-2:]
    load_blocks(table_ref, layer, [refs[k : k + 1] for k in range(8)], wgu_ref, sems)
    lin = dot(normed, wgu_ref[...])
    lin_ref[...] = lin
    gate, up = lin[:, :UNITS], lin[:, UNITS:]
    hidden = (gate * jax.nn.sigmoid(gate) * up).astype(BF)
    hidden_ref[...] = hidden
    down = jnp.where(table_ref[0] == layer, kept_ref[:, :UNITS], other_ref[:, :UNITS])
    part = against(hidden, down).astype(BF)
    for index, ref in enumerate(refs[12:-2]):
        ref[...] = part[index * ROWS : (index + 1) * ROWS]


def feed_back_kernel(count, layer, table_ref, *refs):
    branch = jnp.concatenate([ref[...] for ref in refs[:count]], axis=0)
    refs = refs[count:]
    kept_ref, other_ref, lin_ref, grad_ref = refs[8:12]
    wgu_ref, sems = refs[-2:]
    load_blocks(table_ref, layer, [refs[k : k + 1] for k in range(8)], wgu_ref, sems)
    down = jnp.where(table_ref[0] == layer, kept_ref[:, :UNITS], other_ref[:, :UNITS])
    hidden_grad = dot(branch, down)
    gate, up = lin_ref[:, :UNITS], lin_ref[:, UNITS:]
    sig = jax.nn.sigmoid(gate)
    up_grad = hidden_grad * (gate * sig)
    gate_grad = hidden_grad * up * (sig + gate * sig * (1.0 - sig))
    lin_grad = jnp.concatenate([gate_grad, up_grad], axis=1).astype(BF)
    grad_ref[...] = lin_grad
    part = against(lin_grad, wgu_ref[...]).astype(BF)
    for index, ref in enumerate(refs[12:-2]):
        ref[...] = part[index * ROWS : (index + 1) * ROWS]


def feed_grads_kernel(*refs):
    normed = jnp.concatenate([ref[...] for ref in refs[:10]], axis=0)
    branch = jnp.concatenate([ref[...] for ref in refs[10:20]], axis=0)
    lin_grad, hidden = refs[20][...], refs[21][...]
    out_ref = refs[22]
    gate_up = across(normed, lin_grad).astype(BF)
    down = across(branch, hidden).astype(BF)
    for piece in range(NB - 1):
        rows = [
            gate_up[w * SHARE + piece * PIECE : w * SHARE + (piece + 1) * PIECE] for w in range(4)
        ]
        lower = down[4 * piece * PIECE : 4 * (piece + 1) * PIECE]
        out_ref[piece] = jnp.concatenate([jnp.concatenate(rows, axis=0), lower], axis=1)
    out_ref[NB - 1] = jnp.zeros((4 * PIECE, FF_WIDTH), BF)


def attend_grads_kernel(index_ref, *refs):
    found, parts, out_ref = by_block(refs), refs[10:18], refs[18]
    normed, mixed = [], []
    for block in found:
        if len(block) == 2:
            normed.append(block[0][...])
            mixed.append(block[1][...])
        else:
            normed.append(block[0][0:ROWS, :])
            mixed.append(block[0][ROWS:, :])
    normed, mixed = jnp.concatenate(normed, axis=0), jnp.concatenate(mixed, axis=0)
    lin_grad = jnp.concatenate([ref[0:ROWS, 0:OUT_AT] for ref in parts], axis=0)
    branch = jnp.concatenate([ref[0:ROWS, OUT_AT:] for ref in parts], axis=0)
    weight = across(normed, lin_grad).astype(BF)
    out_weight = across(mixed, branch).astype(BF)
    for piece in range(NB - 1):
        for w in range(4):
            at = w * SHARE + piece * PIECE
            to = slice(w * PIECE, (w + 1) * PIECE)
            out_ref[piece, to, 0:OUT_AT] = weight[at : at + PIECE]
            out_ref[piece, to, OUT_AT:] = out_weight[at : at + PIECE]
    gains = parts[0][ROWS:, 0:OUT_AT].astype(F32)
    for ref in parts[1:]:
        gains = gains + ref[ROWS:, 0:OUT_AT].astype(F32)
    out_ref[NB - 1] = jnp.zeros((4 * PIECE, ATT_WIDTH), BF)
    at = pl.multiple_of(index_ref[0] * PIECE, PIECE)
    out_ref[NB - 1, pl.ds(at, PIECE), 0:OUT_AT] = gains.astype(BF)


def finish_feed_kernel(in_ref, gate_ref, up_ref, down_ref):
    for piece in range(NB - 1):
        at = slice(piece * PIECE, (piece + 1) * PIECE)
        parts = []
        for w in range(4):
            for s in range(2):
                at_row = (4 * s + w) * PIECE
                parts.append(in_ref[piece, at_row : at_row + PIECE, :].astype(F32))
        gate_ref[at, :] = jnp.concatenate([part[:, :UNITS] for part in parts], axis=1)
        up_ref[at, :] = jnp.concatenate([part[:, UNITS:] for part in parts], axis=1)
        rows = in_ref[piece, 8 * PIECE :, :].astype(F32)
        to = slice(4 * piece * PIECE, 4 * (piece + 1) * PIECE)
        down_ref[to, :] = rows


def finish_attend_kernel(in_ref, q_ref, k_ref, v_ref, o_ref, gain_ref):
    keys, values = [], []
    for piece in range(NB - 1):
        at = slice(piece * PIECE, (piece + 1) * PIECE)
        parts = [in_ref[piece, t * PIECE : (t + 1) * PIECE, :].astype(F32) for t in range(8)]
        lin = jnp.concatenate([part[:, :QKV_PART] for part in parts], axis=1)
        q_ref[at, :] = lin[:, : H * HD]
        keys.append(lin[:, H * HD : (H + KV) * HD])
        values.append(lin[:, (H + KV) * HD :])
        o_ref[at, :] = jnp.concatenate(
            [part[:, OUT_AT : OUT_AT + OUT_PART] for part in parts], axis=1
        )
    k_ref[...] = jnp.transpose(jnp.concatenate(keys, axis=0))
    v_ref[...] = jnp.transpose(jnp.concatenate(values, axis=0))
    sides = []
    for side in range(2):
        total = None
        for w in range(4):
            t = 2 * w + side
            own = in_ref[NB - 1, t * PIECE : (t + 1) * PIECE, 0:OUT_PART].astype(F32)[:8]
            total = own if total is None else total + own
        sides.append(total)
    gain_ref[...] = jnp.concatenate(sides, axis=1)


def whole(shape):
    return pl.BlockSpec(shape, lambda i: (0,) * len(shape))


def layer_of(layer, shape):
    return pl.BlockSpec((None,) + shape, lambda i: (layer,) + (0,) * len(shape))


def call(kernel, in_specs, outs, args, scratch=()):
    return pl.pallas_call(
        kernel,
        grid=(1,),
        in_specs=in_specs,
        out_specs=[whole(shape) for shape, _ in outs],
        out_shape=[jax.ShapeDtypeStruct(shape, dtype) for shape, dtype in outs],
        scratch_shapes=list(scratch),
        compiler_params=pltpu.CompilerParams(vmem_limit_bytes=VMEM_BYTES),
        cost_estimate=pl.CostEstimate(flops=1, bytes_accessed=1, transcendentals=0),
    )(*args)


SMEM = pl.BlockSpec(memory_space=pltpu.SMEM)
HBM = pl.BlockSpec(memory_space=pl.ANY)
PACK = (NB, ROWS + ROWS // 2, 2 * HD)
HEADS = (NB, ROWS // 2, 2 * HD)
GROUPS = ((0, 1, 2, 3),)


def exchange(array):
    return lax.all_to_all(array, "blk", 0, 0, tiled=True)


def sum_over_blocks(pieces):
    return jnp.sum(exchange(pieces).astype(F32), axis=0).astype(BF)


def weight_scratch(width):
    return [
        pltpu.VMEM((D, width), BF),
        pltpu.VMEM((4, 16, 256), BF),
        pltpu.SemaphoreType.DMA((3, 8)),
    ]


def body(
    tokens,
    cotangent,
    span_order,
    norm_one,
    w_query,
    w_key,
    w_value,
    w_out,
    norm_two,
    w_gate,
    w_up,
    w_down,
):
    section = lax.axis_index("section")
    shard = lax.axis_index("wshard")
    core = shard % 2
    y = 2 * (shard // 2) + section

    owners = []
    for step in range(4):
        there = (y + step) % 4
        for flip in range(2):
            owners += [there % 2, 2 * (there // 2) + (core ^ flip)]
    table = jnp.stack(owners).astype(jnp.int32)

    x0 = lax.dynamic_index_in_dim(tokens[:, 0], section, 0, keepdims=False)
    cot = lax.dynamic_index_in_dim(cotangent[:, 0], section, 0, keepdims=False)
    first, second = call(
        pack_attend_kernel,
        [
            whole((SHARE, D)),
            whole((KV * HD, SHARE)),
            whole((KV * HD, SHARE)),
            whole((SHARE, D)),
            whole((1, SHARE)),
            whole((1, SHARE)),
        ],
        [((SHARE + 16, WIDE), BF), ((SHARE + 16, D), BF)],
        (w_query[0], w_key[0].T, w_value[0].T, w_out[0], norm_one, norm_two),
    )
    *pieces, kept, sent = call(
        pack_feed_kernel,
        [SMEM, whole((SHARE, FF)), whole((SHARE, FF)), whole((D, FF // 4))],
        [((SHARE, 2 * UNITS), BF)] * 8 + [((D, 384), BF)] * 2,
        (table, w_gate[0], w_up[0], w_down[0].T),
        [pltpu.VMEM((8, SHARE, 2 * UNITS), BF)],
    )
    wqkv = sum(gather_eight(first), [])
    later = {}

    block_index = lax.axis_index("blk")
    own_block = lax.dynamic_index_in_dim(span_order, block_index, 0, keepdims=False)
    positions = own_block * ROWS + jnp.arange(ROWS, dtype=jnp.int32)
    exponent = jnp.arange(HD // 2, dtype=F32) * (2.0 / HD)
    angles = positions.astype(F32)[:, None] * (rope_base ** (-exponent))[None, :]
    angles = jnp.concatenate([angles, angles], axis=-1)
    cosine, sine = jnp.cos(angles), jnp.sin(angles)
    slots = jnp.arange(NB, dtype=jnp.int32)
    place = jnp.sum(
        jnp.where(span_order[None, :] == slots[:, None], slots[None, :], 0), axis=1
    ).astype(jnp.int32)

    angle = whole((ROWS, HD))
    rows = whole((ROWS, D))
    row_scratch = pltpu.VMEM((LEN, HD), BF)
    weights = [HBM] * 10
    half_down = whole((D, 384))
    feed_scratch = [pltpu.VMEM((D, 2 * UNITS), BF), pltpu.SemaphoreType.DMA((3, 8))]

    def row_specs(blocks):
        return [whole(block.shape) for block in blocks]

    def forward(layer, x, early, late):
        h1, packed = call(
            functools.partial(project_kernel, layer),
            [SMEM, rows, angle, angle] + weights,
            [((ROWS, D), BF), (PACK, BF)],
            (table, x, cosine, sine, *wqkv),
            weight_scratch(WIDE),
        )
        first = early(packed)
        packed, first = lax.optimization_barrier((exchange(packed), first))
        heads, lse = call(
            attend_kernel,
            [SMEM, whole(PACK)],
            [(HEADS, BF), ((8, LEN), F32)],
            (place, packed),
            [row_scratch] * 3,
        )
        heads = exchange(heads)
        heads, beside = lax.optimization_barrier((heads, late(first)))
        if layer == 0:
            later.update(beside)
        mixed, x2, h2 = call(
            functools.partial(mix_kernel, layer),
            [SMEM, whole(HEADS), rows] + weights,
            [((ROWS, D), BF), ((ROWS, D), F32), ((ROWS, D), BF)],
            (table, heads, x, *later["out"]),
            weight_scratch(D),
        )
        found = gather_eight(h2)
        kept_ff, parts = [], [None] * 4
        for group in GROUPS:
            blocks = sum([found[step] for step in group], [])
            count = len(blocks)
            size = 2 * len(group)
            if kept_ff:
                blocks = after(blocks, kept_ff[-1][1])
            lin, hidden, *part = call(
                functools.partial(feed_kernel, count, layer),
                [SMEM] + row_specs(blocks) + [HBM] * 8 + [half_down, half_down],
                [((size * ROWS, 2 * UNITS), F32), ((size * ROWS, UNITS), BF)]
                + [((ROWS, D), BF)] * size,
                (table, *blocks, *later["feed"], kept, later["down"]),
                feed_scratch,
            )
            kept_ff.append((blocks, lin, hidden))
            for number, step in enumerate(group):
                parts[step] = part[2 * number : 2 * number + 2]
        both = jnp.concatenate([h1, mixed], axis=0)
        return parts, beside, (x, both, packed, lse, x2, kept_ff)

    def backward(layer, dy, found, kept_state, early, late):
        x, _, packed, lse, x2, kept_ff = kept_state
        parts, branches, lin_grads = [None] * 4, [], []
        for group, (_, lin, _) in zip(GROUPS, kept_ff):
            blocks = sum([found[step] for step in group], [])
            count = len(blocks)
            size = 2 * len(group)
            if lin_grads:
                blocks = after(blocks, lin_grads[-1])
            lin_grad, *part = call(
                functools.partial(feed_back_kernel, count, layer),
                [SMEM]
                + row_specs(blocks)
                + [HBM] * 8
                + [half_down, half_down]
                + [whole((size * ROWS, 2 * UNITS))],
                [((size * ROWS, 2 * UNITS), BF)] + [((ROWS, D), BF)] * size,
                (table, *blocks, *later["feed"], kept, later["down"], lin),
                feed_scratch,
            )
            branches += blocks
            lin_grads.append(lin_grad)
            for number, step in enumerate(group):
                parts[step] = part[2 * number : 2 * number + 2]
        dh2 = scatter_eight(parts)
        dx2, heads_grad, grad_gain_two = call(
            functools.partial(mix_back_kernel, layer),
            [SMEM, rows, rows, rows] + weights,
            [((ROWS, D), F32), (HEADS, BF), ((1, D), F32)],
            (table, dy, dh2, x2, *later["out"]),
            weight_scratch(D),
        )
        normed = sum([item[0] for item in kept_ff], [])
        sizes = [len(group) * 2 * ROWS for group in GROUPS]
        lin_grads = after(lin_grads, dx2)
        grad_ff = call(
            feed_grads_kernel,
            row_specs(normed + branches)
            + [whole((size, 2 * UNITS)) for size in sizes]
            + [whole((size, UNITS)) for size in sizes],
            [((NB, 4 * PIECE, FF_WIDTH), BF)],
            (*normed, *branches, *lin_grads, *[item[2] for item in kept_ff]),
        )[0]
        first = early(dx2)
        heads_grad, first, grad_ff = lax.optimization_barrier(
            (exchange(heads_grad), first, grad_ff)
        )
        packed_grad = call(
            attend_back_kernel,
            [SMEM, whole(PACK), whole(HEADS), whole((8, LEN))],
            [(PACK, BF)],
            (place, packed, heads_grad, lse),
            [row_scratch] * 4
            + [pltpu.VMEM((HD, LEN), BF)]
            + [pltpu.VMEM((LEN, HD), F32)] * 3,
        )[0]
        packed_grad, second = lax.optimization_barrier((exchange(packed_grad), late(first)))
        dx, *lin_parts = call(
            functools.partial(project_back_kernel, layer),
            [SMEM, whole(PACK), rows, rows, angle, angle, whole((1, D))] + weights,
            [((ROWS, D), F32)] + [((ROWS + 16, ATT_WIDTH), BF)] * 8,
            (table, packed_grad, dx2, x, cosine, sine, grad_gain_two, *wqkv),
            [pltpu.VMEM((8, ROWS + 16, ATT_WIDTH), BF)] + weight_scratch(WIDE),
        )
        return dx, lin_parts, grad_ff, second

    def attend_grads(blocks, lin_all):
        return call(
            attend_grads_kernel,
            [SMEM] + row_specs(blocks) + [whole((ROWS + 16, ATT_WIDTH))] * 8,
            [((NB, 4 * PIECE, ATT_WIDTH), BF)],
            (gain_owner, *blocks, *lin_all),
        )[0]

    def sum_feed(pieces):
        flat = pieces.reshape(NB * 4 * PIECE, FF_WIDTH)
        return lax.psum_scatter(flat, "blk", scatter_dimension=0, tiled=True)

    def by_section(of_first, of_second):
        own = jnp.where(section == 0, of_first, of_second)
        other = swap_section(jnp.where(section == 0, of_second, of_first))
        return jnp.where(section == 0, jnp.stack([own, other]), jnp.stack([other, own]))

    gain_owner = ((4 * section + shard) // 2).astype(jnp.int32).reshape(1)
    def first_weights(packed):
        later["near"] = gather_near(after(second, packed))
        return later["near"]

    def last_weights(first):
        near = later.pop("near")
        ready = after(pieces, near)
        for number in (3, 4, 5, 7):
            ready[number] = after(pieces[number], first)
        halves = after(sent, first)
        return {
            "out": sum(arranged(near, gather_far(near)), []),
            "feed": exchange_eight(ready),
            "down": swap_section(halves),
        }

    parts, _, kept0 = forward(0, x0, first_weights, last_weights)
    y0 = (kept0[4] + scatter_eight(parts)).astype(BF)
    parts1, (found_cot, near0), kept1 = forward(
        1,
        y0,
        lambda packed: gather_near(after(cot, packed)),
        lambda near: (arranged(near, gather_far(near)), gather_near(after(kept0[1], near))),
    )
    dx1, lin1, grad_ff1, (both0, near1) = backward(
        1,
        cot,
        found_cot,
        kept1,
        lambda dx2: (arranged(near0, gather_far(after(near0, dx2))), dx2),
        lambda first: (
            first[0],
            gather_near(after(kept1[1], first[1])),
        ),
    )
    dy0 = dx1.astype(BF)
    ff1 = sum_feed(grad_ff1)
    dx0, lin0, grad_ff0, (both1, lin1) = backward(
        0,
        dy0,
        gather_eight(dy0),
        kept0,
        lambda dx2: (arranged(near1, gather_far(after(near1, dx2))), dx2),
        lambda first: (
            first[0],
            exchange_eight(after(lin1, first[1])),
        ),
    )
    att1 = sum_over_blocks(attend_grads(sum(both1, []), after(lin1, dx0)))
    lin0 = exchange_eight(lin0)
    att0 = attend_grads(sum(both0, []), lin0)
    ff0, ff1, att0 = after((sum_feed(grad_ff0), ff1, att0), att1)
    y1 = (kept1[4] + scatter_eight(after(parts1, att0))).astype(BF)
    layer_outputs = by_section(y0, y1)
    upper = 2 * UNITS
    spread = jnp.stack([ff0[:, :upper], ff1[:, :upper]]).reshape(8, PIECE, upper)
    spread = lax.all_to_all(spread, EIGHT, 0, 0, tiled=True).reshape(8 * PIECE, upper)
    lower = by_section(ff0[:, upper:], ff1[:, upper:])
    lower = jnp.concatenate([lower[0], lower[1]], axis=1)
    found = lax.all_gather(jnp.concatenate([spread, lower], axis=0), "blk", axis=0)
    input_grads = by_section(dx0, dx1)
    att0 = sum_over_blocks(att0)
    grad_gate, grad_up, grad_down = call(
        finish_feed_kernel,
        [whole(found.shape)],
        [((SHARE, FF), F32), ((SHARE, FF), F32), ((D, FF // 4), F32)],
        (found,),
    )
    spread = jnp.stack([att0, att1]).reshape(8, PIECE, ATT_WIDTH)
    spread = lax.all_to_all(spread, EIGHT, 0, 0, tiled=True).reshape(1, 8 * PIECE, ATT_WIDTH)
    found = exchange(jnp.broadcast_to(spread, (NB, 8 * PIECE, ATT_WIDTH)))
    grad_query, grad_key, grad_value, grad_out, gain_grads = call(
        finish_attend_kernel,
        [whole(found.shape)],
        [
            ((SHARE, H * HD), F32),
            ((KV * HD, SHARE), F32),
            ((KV * HD, SHARE), F32),
            ((SHARE, D), F32),
            ((8, SHARE), F32),
        ],
        (found,),
    )
    return (
        layer_outputs[None, :, None],
        input_grads[None, :, None],
        gain_grads[0][None],
        grad_query[None],
        grad_key.T[None],
        grad_value.T[None],
        grad_out[None],
        gain_grads[1][None],
        grad_gate[None],
        grad_up[None],
        grad_down.T[None],
    )


def solution(mesh):
    return jax.shard_map(
        body,
        mesh=mesh,
        in_specs=(
            P(None, "wshard", "blk", None),
            P(None, "wshard", "blk", None),
            P(),
            P("section", "wshard"),
            P("section", "wshard", None),
            P("section", "wshard", None),
            P("section", "wshard", None),
            P("section", "wshard", None),
            P("section", "wshard"),
            P("section", "wshard", None),
            P("section", "wshard", None),
            P("section", "wshard", None),
        ),
        out_specs=(
            P("section", None, "wshard", "blk", None),
            P("section", None, "wshard", "blk", None),
            P("section", "wshard"),
            P("section", "wshard", None),
            P("section", "wshard", None),
            P("section", "wshard", None),
            P("section", "wshard", None),
            P("section", "wshard"),
            P("section", "wshard", None),
            P("section", "wshard", None),
            P("section", "wshard", None),
        ),
        check_vma=False,
    )
```
